32 devices in a mesh: scene: 4 (over y, x), blk: 8 (over z, core).
Axes of the slice: x: 2, y: 2, z: 4, core: 2. Of those that a mesh axis runs over, the one named last changes fastest.
Arguments:
- tokens_in: bfloat16 [8192, 1024], P(('scene', 'blk')), may hold values from -6 to 6
- view_heights: int32 [4, 4], P('scene'), may hold values from 8 to 24, as said below
- view_widths: int32 [4, 4], P('scene'), may hold values from 16 to 48
- view_scenes: int32 [4, 4], P('scene'), may hold values from 0 to 0, as said below
- out_grad: bfloat16 [8192, 1024], P(('scene', 'blk')), may hold values from -6 to 6
- w_qkv: bfloat16 [1024, 3072], P(('scene', 'blk')), may hold values from -0.1875 to 0.1875
- w_out: bfloat16 [1024, 1024], P(('scene', 'blk')), may hold values from -4 to 4
- w_up: bfloat16 [1024, 4096], P(('scene', 'blk')), may hold values from -0.1875 to 0.1875
- w_down: bfloat16 [4096, 1024], P(('scene', 'blk')), may hold values from -0.09375 to 0.09375
- norm1_gain: bfloat16 [1024], P(('scene', 'blk')), may hold values from 0.5 to 1.5
- norm1_bias: bfloat16 [1024], P(('scene', 'blk')), may hold values from -3 to 3
- norm2_gain: bfloat16 [1024], P(('scene', 'blk')), may hold values from 0.5 to 1.5
- norm2_bias: bfloat16 [1024], P(('scene', 'blk')), may hold values from -3 to 3
Outputs:
- layer_out: bfloat16 [8192, 1024], P(('scene', 'blk'))
- input_grad: float32 [8192, 1024], P(('scene', 'blk'))
- qkv_grad: float32 [1024, 3072], P(('scene', 'blk'))
- out_weight_grad: float32 [1024, 1024], P(('scene', 'blk'))
- up_grad: float32 [1024, 4096], P(('scene', 'blk'))
- down_grad: float32 [4096, 1024], P(('scene', 'blk'))
- gain1_grad: float32 [1024], P(('scene', 'blk'))
- bias1_grad: float32 [1024], P(('scene', 'blk'))
- gain2_grad: float32 [1024], P(('scene', 'blk'))
- bias2_grad: float32 [1024], P(('scene', 'blk'))
The draws below stay inside these ranges and needn't reach their ends.
Inputs may be any that keep to these rules, and one draw needn't show every extreme that they name: `view_heights`: within each group the views can be taken in fours whose areas add up to 2048; so a group's areas add up to 2048. `view_scenes`: each scene number of a group names exactly four of its views; the first and the last view of a group belong to one scene.
All inputs are finite; a program needn't handle non-finite values.
Results may differ from the reference program's by a relative error of at most 0.014.
Values may be sent and summed in bfloat16 or wider, within the bound.
No kernel may reach another device: no remote copies, remote signals or barrier semaphores. Data moves between devices by JAX's collectives and lax.ppermute only.
A program may use at most 256 MiB of HBM per device.

```python
import jax
import jax.numpy as jnp
from jax import lax

D = 1024
HEADS = 16
HEAD_DIM = 64
FF = 4096
GRID_H = 16
GRID_W = 32
GROUP_TOK = 2048
SCENES_G = 1
VIEWS_G = 4
GROUPS = 4
TOKENS = 8192
N_SCENE = 4


def view_grids(key):
    first_key, second_key, width_key, order_key = jax.random.split(key, 4)
    shape = (GROUPS, SCENES_G)
    lowest_h = GRID_H - GRID_H // 2
    lowest_w = GRID_W - GRID_W // 2
    first_h = jax.random.randint(first_key, shape, lowest_h, 2 * GRID_H - lowest_h + 1)
    second_h = jax.random.randint(second_key, shape, lowest_h, 2 * GRID_H - lowest_h + 1)
    first_w = jax.random.randint(width_key, shape, lowest_w, 2 * GRID_W - lowest_w + 1)
    first_h = first_h.at[:, 0].set(lowest_h)
    first_w = first_w.at[:, 0].set(lowest_w)
    heights = jnp.stack([first_h, 2 * GRID_H - first_h, second_h, 2 * GRID_H - second_h], axis=2)
    widths = jnp.stack([first_w, first_w, 2 * GRID_W - first_w, 2 * GRID_W - first_w], axis=2)
    heights = heights.reshape(GROUPS, VIEWS_G)
    widths = widths.reshape(GROUPS, VIEWS_G)
    orders = jax.vmap(lambda member: jax.random.permutation(member, VIEWS_G))(jax.random.split(order_key, GROUPS))
    heights = jnp.take_along_axis(heights, orders, axis=1)
    widths = jnp.take_along_axis(widths, orders, axis=1)
    return (heights.astype(jnp.int32), widths.astype(jnp.int32))


def draw_view_heights(key, part):
    return view_grids(key)[0]


def draw_view_widths(key, part):
    return view_grids(key)[1]


def draw_view_scenes(key, part):
    key = jax.random.fold_in(key, 7)

    def one_group(group_key):
        mix_key, name_key = jax.random.split(group_key)
        others = jnp.arange(2, VIEWS_G, dtype=jnp.int32) // 4
        middle = jax.random.permutation(mix_key, others)
        ends_label = jnp.zeros((1,), jnp.int32)
        labels = jnp.concatenate([ends_label, middle, ends_label])
        renamed = jax.random.permutation(name_key, SCENES_G).astype(jnp.int32)
        return renamed[labels]
    return jax.vmap(one_group)(jax.random.split(key, GROUPS)).astype(jnp.int32)


def spiked(values, own_key, source, target, parts, factor):
    owner, partner = [(jnp.arange(values.shape[dim]) // (values.shape[dim] // parts)).reshape([-1 if axis == dim else 1 for axis in range(values.ndim)]) for dim in (source, target)]
    chosen = jax.random.permutation(own_key, parts)[partner]
    strong = (owner == chosen) | (owner == (partner + parts // 2) % parts)
    return jnp.where(strong, factor * values, values)


def level_of(stream_key, shape, cuts, smallest, high):
    level = 1.0
    for position, blocks in cuts:
        steps = jax.random.uniform(jax.random.fold_in(jax.random.fold_in(stream_key, 6), position), (blocks,), jnp.float32, smallest / len(cuts), high / len(cuts))
        level = level * jnp.repeat(jnp.exp(steps), shape[position] // blocks).reshape((-1,) + (1,) * (len(shape) - 1 - position))
    return level


def bell_draw(rng, shape, deviation, most, pieces=(), held_as=jnp.bfloat16):
    entries = jax.random.normal(rng, shape, jnp.float32) * deviation
    if len(pieces) > 0:
        entries = level_of(rng, shape, pieces, -0.22, 0.18) * entries
    return jnp.clip(entries, min=-most, max=most).astype(held_as)


def gaussian_with(rng, dims, width, limit, cuts, heavy, held_as=jnp.bfloat16):
    values = width * jax.random.normal(rng, dims, jnp.float32)
    if cuts:
        values = values * level_of(rng, dims, cuts, -0.22, 0.18)
    return jnp.clip(spiked(values, jax.random.fold_in(rng, 3), *heavy), -limit, limit).astype(held_as)


def setup_inputs(seed: int = 0) -> dict:
    key_of = jax.random.split(jax.random.key(seed), 14)
    return {
        "tokens_in": bell_draw(key_of[0], (TOKENS, D), 1.0, 6.0, ((0, 32),)),
        "view_heights": draw_view_heights(jax.random.fold_in(key_of[13], 71), 0),
        "view_widths": draw_view_widths(jax.random.fold_in(key_of[13], 71), 0),
        "view_scenes": draw_view_scenes(jax.random.fold_in(key_of[13], 71), 0),
        "out_grad": gaussian_with(key_of[4], (TOKENS, D), 1.0, 6.0, ((0, 32),), (0, 1, 32, 2.75)),
        "w_qkv": bell_draw(key_of[5], (D, 3 * D), D ** -0.5, 0.1875, ((0, 32),)),
        "w_out": bell_draw(key_of[6], (D, D), 2 ** -0.5, 4.0, ((0, 32),)),
        "w_up": bell_draw(key_of[7], (D, FF), D ** -0.5, 0.1875, ((0, 32),)),
        "w_down": bell_draw(key_of[8], (FF, D), FF ** -0.5, 0.09375, ((0, 32),)),
        "norm1_gain": jnp.clip(1.0 + 0.1 * jax.random.normal(key_of[9], (D,), jnp.float32), 0.5, 1.5).astype(jnp.bfloat16),
        "norm1_bias": bell_draw(key_of[10], (D,), 0.5, 3.0, ((0, 32),)),
        "norm2_gain": jnp.clip(1.0 + 0.1 * jax.random.normal(key_of[11], (D,), jnp.float32), 0.5, 1.5).astype(jnp.bfloat16),
        "norm2_bias": bell_draw(key_of[12], (D,), 0.5, 3.0, ((0, 32),)),
    }


@jax.custom_vjp
def low(v):
    return lax.optimization_barrier(v.astype(jnp.bfloat16)).astype(jnp.float32)

@jax.custom_vjp
def low_back(v):
    return v

def low_keep(v):
    return (low(v), None)

def low_pass(kept, grad):
    return (grad,)

def back_keep(v):
    return (v, None)

def back_low(kept, grad):
    return (low(grad),)
low.defvjp(low_keep, low_pass)
low_back.defvjp(back_keep, back_low)
EPSILON = 1e-05
MASKED = -1e+30
PRECISE = lax.Precision.HIGHEST

def product(left, right):
    return jnp.dot(left, right, precision=PRECISE, preferred_element_type=jnp.float32)

def layer_norm(values, gain_row, bias_row):
    centred = values - lax.optimization_barrier(jnp.mean(values, axis=1, keepdims=True))
    scaled = centred * lax.rsqrt(lax.optimization_barrier(jnp.mean(centred * centred, axis=1, keepdims=True)) + EPSILON)
    return scaled * gain_row + bias_row

def scene_rows(view_ends, labels, first_row, count_rows):
    places = first_row + jnp.arange(count_rows, dtype=jnp.int32)
    view_index = lax.optimization_barrier(jnp.sum((places[:, None] >= view_ends[None, :]).astype(jnp.int32), axis=1))
    matches = view_index[:, None] == jnp.arange(labels.shape[0], dtype=jnp.int32)[None, :]
    return lax.optimization_barrier(jnp.sum(jnp.where(matches, labels[None, :], 0), axis=1)).astype(jnp.int32)

def group_scenes(heights, widths, labels):
    return scene_rows(jnp.cumsum(heights * widths).astype(jnp.int32), labels, 0, GROUP_TOK)

def attend_rows(query_block, block_scene, group_keys, group_values, group_scene):
    raw = jnp.einsum('qhe,khe->hqk', query_block, group_keys, precision=PRECISE) * HEAD_DIM ** (-0.5)
    raw = low_back(raw)
    allowed = (block_scene[:, None] == group_scene[None, :])[None]
    raw = jnp.where(allowed, raw, MASKED)
    highest = lax.optimization_barrier(jnp.max(raw, axis=2, keepdims=True))
    expo = jnp.exp(raw - highest)
    weights = low(expo / lax.optimization_barrier(jnp.sum(expo, axis=2, keepdims=True)))
    return jnp.einsum('hqk,khe->qhe', weights, group_values, precision=PRECISE)

def attention(query_rows, key_rows, value_rows, scene_ids):
    block_rows = min(512, GROUP_TOK)

    def per_group(members):
        group_queries, group_keys, group_values, group_scene = members

        def per_block(block):
            return attend_rows(block[0], block[1], group_keys, group_values, group_scene)
        blocks = (group_queries.reshape(GROUP_TOK // block_rows, block_rows, HEADS, HEAD_DIM), group_scene.reshape(GROUP_TOK // block_rows, block_rows))
        return lax.map(jax.checkpoint(per_block), blocks).reshape(GROUP_TOK, HEADS, HEAD_DIM)
    shaped = (query_rows.reshape(N_SCENE, GROUP_TOK, HEADS, HEAD_DIM), key_rows.reshape(N_SCENE, GROUP_TOK, HEADS, HEAD_DIM), value_rows.reshape(N_SCENE, GROUP_TOK, HEADS, HEAD_DIM), scene_ids)
    return lax.map(per_group, shaped).reshape(TOKENS, D)

def reference(tokens_in, view_heights, view_widths, view_scenes, out_grad, w_qkv, w_out, w_up, w_down, norm1_gain, norm1_bias, norm2_gain, norm2_bias):
    scene_ids = jax.vmap(group_scenes)(view_heights, view_widths, view_scenes)

    def layer(inputs, full_qkv, full_out, full_up, full_down, gain_one, bias_one, gain_two, bias_two):
        normed = low(layer_norm(inputs, gain_one, bias_one))
        projected = product(normed, full_qkv)
        query_rows = low_back(low(projected[:, :D]))
        key_rows = low_back(low(projected[:, D:2 * D]))
        value_rows = low_back(low(projected[:, 2 * D:]))
        attended = low_back(low(attention(query_rows, key_rows, value_rows, scene_ids)))
        hidden = inputs + low_back(product(attended, full_out))
        normed_two = low(layer_norm(hidden, gain_two, bias_two))
        upward = low_back(product(normed_two, full_up))
        active = low(jax.nn.gelu(upward))
        return hidden + low_back(product(active, full_down))
    floats = tuple((member.astype(jnp.float32) for member in (tokens_in, w_qkv, w_out, w_up, w_down, norm1_gain, norm1_bias, norm2_gain, norm2_bias)))
    result, pull = jax.vjp(layer, *floats)
    grads = pull(out_grad.astype(jnp.float32))
    return (result.astype(jnp.bfloat16), grads[0], grads[1], grads[2], grads[3], grads[4], grads[5], grads[6], grads[7], grads[8])
```

```python
import functools
import math

import jax
import jax.numpy as jnp
from jax import lax
from jax.experimental import pallas as pl
from jax.experimental.pallas import tpu as pltpu
from jax.sharding import Mesh
from jax.sharding import PartitionSpec as P

D = 1024
HEADS = 16
HEAD_DIM = 64


EPSILON = 1e-05
MASKED = -1e30


def layer_norm(values, gain_row, bias_row):
    centred = values - jnp.mean(values, axis=1, keepdims=True)
    scaled = centred * lax.rsqrt(jnp.mean(centred * centred, axis=1, keepdims=True) + EPSILON)
    return scaled * gain_row + bias_row


def scene_rows(view_ends, labels, first_row, count_rows):
    places = first_row + jnp.arange(count_rows, dtype=jnp.int32)
    view_index = jnp.sum((places[:, None] >= view_ends[None, :]).astype(jnp.int32), axis=1)
    matches = view_index[:, None] == jnp.arange(labels.shape[0], dtype=jnp.int32)[None, :]
    return jnp.sum(jnp.where(matches, labels[None, :], 0), axis=1)


def in_blocks(update, carry, members):
    total_rows = members[0].shape[0]
    width_rows = math.gcd(total_rows, 1024)
    block_count = total_rows // width_rows
    stacked = tuple(
        (member.reshape((block_count, width_rows) + member.shape[1:]) for member in members)
    )

    def advance(state_now, indexed):
        block_index, block_parts = indexed
        return (update(state_now, block_parts, block_index * width_rows), None)

    carry, _ = lax.scan(advance, carry, (jnp.arange(block_count, dtype=jnp.int32), stacked))
    return carry


def heads_of(rows):
    return rows.reshape(rows.shape[0], HEADS, HEAD_DIM)


def pair_terms(
    query_heads, delta_heads, log_rows, probe_rows, allowed, key_heads, value_heads, score_scale
):
    raw = (
        jnp.einsum("qhe,khe->hqk", query_heads, key_heads, preferred_element_type=jnp.float32)
        * score_scale
    )
    weights_now = jnp.where(allowed, jnp.exp(raw - log_rows[:, :, None]), 0.0)
    backward = jnp.einsum(
        "qhe,khe->hqk", delta_heads, value_heads, preferred_element_type=jnp.float32
    )
    score_delta = (weights_now * (backward - probe_rows[:, :, None])).astype(jnp.bfloat16)
    return (weights_now.astype(jnp.bfloat16), score_delta)


def outer(left, right):
    return lax.dot_general(
        left, right, (((0,), (0,)), ((), ())), preferred_element_type=jnp.float32
    )


def against(left, right):
    return lax.dot_general(
        left, right, (((1,), (1,)), ((), ())), preferred_element_type=jnp.float32
    )


def on_any_slice(
    tokens_in,
    view_heights,
    view_widths,
    view_scenes,
    out_grad,
    w_qkv,
    w_out,
    w_up,
    w_down,
    norm1_gain,
    norm1_bias,
    norm2_gain,
    norm2_bias,
):
    gathered = (
        lax.all_gather(w_qkv, ("scene", "blk"), axis=0, tiled=True),
        lax.all_gather(w_out, ("scene", "blk"), axis=0, tiled=True),
        lax.all_gather(w_up, ("scene", "blk"), axis=0, tiled=True),
        lax.all_gather(w_down, ("scene", "blk"), axis=0, tiled=True),
        lax.all_gather(norm1_gain, ("scene", "blk"), axis=0, tiled=True),
        lax.all_gather(norm1_bias, ("scene", "blk"), axis=0, tiled=True),
        lax.all_gather(norm2_gain, ("scene", "blk"), axis=0, tiled=True),
        lax.all_gather(norm2_bias, ("scene", "blk"), axis=0, tiled=True),
    )
    full_qkv, full_out, full_up, full_down = (gathered[0], gathered[1], gathered[2], gathered[3])
    gain_one = gathered[4].astype(jnp.float32)
    bias_one = gathered[5].astype(jnp.float32)
    gain_two = gathered[6].astype(jnp.float32)
    bias_two = gathered[7].astype(jnp.float32)
    local_rows = tokens_in.shape[0]
    view_ends = jnp.cumsum(view_heights[0] * view_widths[0])
    labels = view_scenes[0]
    own_first = lax.axis_index("blk") * local_rows
    own_scene = scene_rows(view_ends, labels, own_first, local_rows)
    score_scale = HEAD_DIM ** (-0.5)
    inputs = tokens_in.astype(jnp.float32)
    normed, norm_one_pull = jax.vjp(layer_norm, inputs, gain_one, bias_one)
    normed_low = normed.astype(jnp.bfloat16)
    projected = jnp.dot(normed_low, full_qkv, preferred_element_type=jnp.float32).astype(
        jnp.bfloat16
    )
    query_rows = projected[:, :D]
    key_rows = projected[:, D : 2 * D]
    value_rows = projected[:, 2 * D :]
    query_heads = heads_of(query_rows)

    def forward_update(state_now, members, first_row):
        run_max, run_sum, run_total = state_now
        piece_keys, piece_values = members
        piece_rows = piece_keys.shape[0]
        key_scene = scene_rows(view_ends, labels, first_row, piece_rows)
        allowed = (own_scene[:, None] == key_scene[None, :])[None]
        raw = (
            jnp.einsum(
                "qhe,khe->hqk",
                query_heads,
                heads_of(piece_keys),
                preferred_element_type=jnp.float32,
            )
            * score_scale
        )
        new_max = jnp.maximum(run_max, jnp.max(jnp.where(allowed, raw, MASKED), axis=2))
        expo = jnp.where(allowed, jnp.exp(raw - new_max[:, :, None]), 0.0)
        factor = jnp.exp(run_max - new_max)
        run_sum = run_sum * factor + jnp.sum(expo, axis=2)
        mixed = jnp.einsum(
            "hqk,khe->qhe",
            expo.astype(jnp.bfloat16),
            heads_of(piece_values),
            preferred_element_type=jnp.float32,
        )
        run_total = run_total * jnp.transpose(factor)[:, :, None] + mixed
        return (new_max, run_sum, run_total)

    start_state = (
        jnp.full((HEADS, local_rows), MASKED, jnp.float32),
        jnp.zeros((HEADS, local_rows), jnp.float32),
        jnp.zeros((local_rows, HEADS, HEAD_DIM), jnp.float32),
    )
    run_max, run_sum, run_total = in_blocks(
        forward_update,
        start_state,
        (
            lax.all_gather(key_rows, "blk", axis=0, tiled=True),
            lax.all_gather(value_rows, "blk", axis=0, tiled=True),
        ),
    )
    log_total = run_max + jnp.log(run_sum)
    attended_heads = run_total / jnp.transpose(run_sum)[:, :, None]
    attended_low = attended_heads.reshape(local_rows, D).astype(jnp.bfloat16)
    hidden = inputs + jnp.dot(attended_low, full_out, preferred_element_type=jnp.float32)
    normed_two, norm_two_pull = jax.vjp(layer_norm, hidden, gain_two, bias_two)
    normed_two_low = normed_two.astype(jnp.bfloat16)
    upward = jnp.dot(normed_two_low, full_up, preferred_element_type=jnp.float32)
    active, gelu_pull = jax.vjp(jax.nn.gelu, upward)
    active_low = active.astype(jnp.bfloat16)
    result = (hidden + jnp.dot(active_low, full_down, preferred_element_type=jnp.float32)).astype(
        jnp.bfloat16
    )
    down_term = outer(active_low, out_grad)
    up_delta = gelu_pull(against(out_grad, full_down))[0].astype(jnp.bfloat16)
    up_term = outer(normed_two_low, up_delta)
    hidden_back, gain_two_term, bias_two_term = norm_two_pull(against(up_delta, full_up))
    hidden_delta = out_grad.astype(jnp.float32) + hidden_back
    hidden_low = hidden_delta.astype(jnp.bfloat16)
    out_term = outer(attended_low, hidden_low)
    att_delta = against(hidden_low, full_out).astype(jnp.bfloat16)
    delta_heads = heads_of(att_delta)
    row_probe = jnp.transpose(jnp.sum(delta_heads.astype(jnp.float32) * attended_heads, axis=2))
    query_start = jnp.zeros((local_rows, HEADS, HEAD_DIM), jnp.float32)
    every_key, every_value = (
        lax.all_gather(key_rows, "blk", axis=0, tiled=True),
        lax.all_gather(value_rows, "blk", axis=0, tiled=True),
    )
    group_rows = every_key.shape[0]
    width_rows = math.gcd(group_rows, 1024)
    block_count = group_rows // width_rows

    def joint_step(total, indexed):
        block_index, block_keys, block_values = indexed
        block_first = block_index * width_rows
        key_heads = heads_of(block_keys)
        value_heads = heads_of(block_values)
        key_scene = scene_rows(view_ends, labels, block_first, width_rows)
        allowed = (own_scene[:, None] == key_scene[None, :])[None]
        weights_low, score_delta = pair_terms(
            query_heads,
            delta_heads,
            log_total,
            row_probe,
            allowed,
            key_heads,
            value_heads,
            score_scale,
        )
        total = (
            total
            + jnp.einsum("hqk,khe->qhe", score_delta, key_heads, preferred_element_type=jnp.float32)
            * score_scale
        )
        value_part = jnp.einsum(
            "hqk,qhe->khe", weights_low, delta_heads, preferred_element_type=jnp.float32
        )
        key_part = (
            jnp.einsum("hqk,qhe->khe", score_delta, query_heads, preferred_element_type=jnp.float32)
            * score_scale
        )
        rows_out = jnp.concatenate(
            [key_part.reshape(width_rows, D), value_part.reshape(width_rows, D)], axis=1
        )
        return (total, rows_out)

    query_total, pair_rows = lax.scan(
        joint_step,
        query_start,
        (
            jnp.arange(block_count, dtype=jnp.int32),
            every_key.reshape(block_count, width_rows, D),
            every_value.reshape(block_count, width_rows, D),
        ),
    )
    pair_rows = pair_rows.reshape(group_rows, 2 * D)
    both_sums = lax.psum_scatter(
        pair_rows.astype(jnp.bfloat16), "blk", scatter_dimension=0, tiled=True
    ).astype(jnp.float32)
    key_total = both_sums[:, :D]
    value_total = both_sums[:, D:]
    qkv_delta = jnp.concatenate(
        [query_total.reshape(local_rows, D), key_total, value_total], axis=1
    ).astype(jnp.bfloat16)
    qkv_term = outer(normed_low, qkv_delta)
    input_back, gain_one_term, bias_one_term = norm_one_pull(against(qkv_delta, full_qkv))
    input_grad = hidden_delta + input_back
    summed = (
        lax.psum_scatter(qkv_term, ("scene", "blk"), scatter_dimension=0, tiled=True),
        lax.psum_scatter(out_term, ("scene", "blk"), scatter_dimension=0, tiled=True),
        lax.psum_scatter(up_term, ("scene", "blk"), scatter_dimension=0, tiled=True),
        lax.psum_scatter(down_term, ("scene", "blk"), scatter_dimension=0, tiled=True),
        lax.psum_scatter(gain_one_term, ("scene", "blk"), scatter_dimension=0, tiled=True),
        lax.psum_scatter(bias_one_term, ("scene", "blk"), scatter_dimension=0, tiled=True),
        lax.psum_scatter(gain_two_term, ("scene", "blk"), scatter_dimension=0, tiled=True),
        lax.psum_scatter(bias_two_term, ("scene", "blk"), scatter_dimension=0, tiled=True),
    )
    return (
        result,
        input_grad,
        summed[0],
        summed[1],
        summed[2],
        summed[3],
        summed[4],
        summed[5],
        summed[6],
        summed[7],
    )


ALL = ("y", "x", "z", "c")
LANES = 128
ROOT = math.sqrt(2.0 / math.pi)
CUBIC = 0.044715


def swap(values, axis, size, distance):
    return lax.ppermute(values, axis, [(i, i ^ distance) for i in range(size)])


def pair(values):
    return swap(values, "c", 2, 1)


def whole(shape):
    return pl.BlockSpec(shape, lambda *_: (0,) * len(shape))


def params(megabytes=60):
    return pltpu.CompilerParams(vmem_limit_bytes=megabytes * 1024 * 1024)


def three_parts(column, lane, first):
    high = column.astype(jnp.bfloat16).astype(jnp.float32)
    rest = column - high
    middle = rest.astype(jnp.bfloat16).astype(jnp.float32)
    last = rest - middle
    zero = jnp.zeros_like(last)
    return jnp.where(
        lane == first,
        high,
        jnp.where(lane == first + 1, middle, jnp.where(lane == first + 2, last, zero)),
    )


def attend_kernel(q_ref, k_ref, v_ref, low_ref, att_ref, aug_ref):
    lane = lax.broadcasted_iota(jnp.int32, (1, LANES), 1)
    queries = q_ref[...].astype(jnp.float32) * HEAD_DIM ** (-0.5)
    keys = k_ref[...]
    values = v_ref[...].astype(jnp.float32)
    heads = []
    for head in range(2):
        mine = (lane < HEAD_DIM) if head == 0 else (lane >= HEAD_DIM)
        own_query = jnp.where(mine, queries, 0.0).astype(jnp.bfloat16)
        scores = against(own_query, keys)
        highest = jnp.max(scores, axis=1, keepdims=True)
        expo = jnp.exp(scores - highest).astype(jnp.bfloat16)
        ones = jnp.where(mine, values, 1.0).astype(jnp.bfloat16)
        mixed = jnp.dot(expo, ones, preferred_element_type=jnp.float32)
        heads.append(mixed / pltpu.roll(mixed, HEAD_DIM, 1))
        log_total = highest + jnp.log(mixed)
        parts = three_parts(-log_total, lane, HEAD_DIM if head == 0 else 0)
        aug_ref[head] = jnp.where(mine, queries, parts).astype(jnp.bfloat16)
    attended = jnp.where(lane < HEAD_DIM, heads[0], heads[1])
    att_ref[...] = attended
    low_ref[...] = attended.astype(jnp.bfloat16)


def attend(qkv):
    rows = qkv.shape[0]
    block = 512
    return pl.pallas_call(
        attend_kernel,
        grid=(rows // block,),
        in_specs=[
            pl.BlockSpec((block, LANES), lambda i: (i, 0)),
            pl.BlockSpec((rows, LANES), lambda i: (0, 1)),
            pl.BlockSpec((rows, LANES), lambda i: (0, 2)),
        ],
        out_specs=[
            pl.BlockSpec((block, LANES), lambda i: (i, 0)),
            pl.BlockSpec((block, LANES), lambda i: (i, 0)),
            pl.BlockSpec((2, block, LANES), lambda i: (0, i, 0)),
        ],
        out_shape=[
            jax.ShapeDtypeStruct((rows, LANES), jnp.bfloat16),
            jax.ShapeDtypeStruct((rows, LANES), jnp.float32),
            jax.ShapeDtypeStruct((2, rows, LANES), jnp.bfloat16),
        ],
        compiler_params=params(),
        cost_estimate=pl.CostEstimate(
            flops=16 * rows * rows * HEAD_DIM, bytes_accessed=16 * rows * LANES, transcendentals=2 * rows * rows
        ),
    )(qkv, qkv, qkv)


def attend_back_kernel(
    k_ref, v_ref, aug_ref, do_ref, att_ref, dq_ref, dk_ref, dv_ref, ka_ref, va_ref, kt_ref, dq_acc, dk_acc, dv_acc
):
    head, step = pl.program_id(0), pl.program_id(1)
    rows = k_ref.shape[0]
    block = do_ref.shape[0]
    width = 512
    lane = lax.broadcasted_iota(jnp.int32, (1, LANES), 1)
    spare = jnp.where(head == 0, HEAD_DIM, 0)
    mine = (lane < spare) | (lane >= spare + HEAD_DIM)

    @pl.when((head == 0) & (step == 0))
    def _():
        kt_ref[...] = k_ref[...].astype(jnp.float32).T.astype(jnp.bfloat16)

    @pl.when(step == 0)
    def _():
        ones = jnp.where(lane < spare + 3, 1.0, 0.0)
        ka_ref[...] = jnp.where(mine, k_ref[...].astype(jnp.float32), ones).astype(jnp.bfloat16)
        va_ref[...] = jnp.where(mine, v_ref[...].astype(jnp.float32), ones).astype(jnp.bfloat16)
        dk_acc[head] = jnp.zeros((rows, LANES), jnp.float32)
        dv_acc[head] = jnp.zeros((rows, LANES), jnp.float32)

    delta = do_ref[...].astype(jnp.float32)
    probe = jnp.sum(jnp.where(mine, delta * att_ref[...], 0.0), axis=1, keepdims=True)
    own_delta = jnp.where(mine, delta, three_parts(-probe, lane, spare)).astype(jnp.bfloat16)
    own_query = aug_ref[0]
    total = jnp.zeros((LANES, block), jnp.float32)
    for first in range(0, rows, width):
        part = slice(first, first + width)
        probs = jnp.exp(against(ka_ref[part, :], own_query))
        score_delta = (probs * against(va_ref[part, :], own_delta)).astype(jnp.bfloat16)
        dv_acc[head, part, :] += jnp.dot(
            probs.astype(jnp.bfloat16), own_delta, preferred_element_type=jnp.float32
        )
        dk_acc[head, part, :] += jnp.dot(score_delta, own_query, preferred_element_type=jnp.float32)
        total += jnp.dot(kt_ref[:, part], score_delta, preferred_element_type=jnp.float32)
    query_delta = (total * HEAD_DIM ** (-0.5)).T
    place = pl.ds(pl.multiple_of(step * block, block), block)

    @pl.when(head == 0)
    def _():
        dq_acc[place, :] = query_delta

    @pl.when(head == 1)
    def _():
        dq_ref[place, :] = jnp.where(lane < HEAD_DIM, dq_acc[place, :], query_delta).astype(jnp.bfloat16)

    @pl.when((head == 1) & (step == pl.num_programs(1) - 1))
    def _():
        dk_ref[...] = jnp.where(lane < HEAD_DIM, dk_acc[0], dk_acc[1]).astype(jnp.bfloat16)
        dv_ref[...] = jnp.where(lane < HEAD_DIM, dv_acc[0], dv_acc[1]).astype(jnp.bfloat16)


def attend_back(qkv, augmented, delta, attended):
    rows = qkv.shape[0]
    block = 256
    shape = jax.ShapeDtypeStruct((rows, LANES), jnp.bfloat16)
    return pl.pallas_call(
        attend_back_kernel,
        grid=(2, rows // block),
        in_specs=[
            pl.BlockSpec((rows, LANES), lambda h, i: (0, 1)),
            pl.BlockSpec((rows, LANES), lambda h, i: (0, 2)),
            pl.BlockSpec((1, block, LANES), lambda h, i: (h, i, 0)),
            pl.BlockSpec((block, LANES), lambda h, i: (i, 0)),
            pl.BlockSpec((block, LANES), lambda h, i: (i, 0)),
        ],
        out_specs=[whole((rows, LANES))] * 3,
        out_shape=[shape] * 3,
        scratch_shapes=[
            pltpu.VMEM((rows, LANES), jnp.bfloat16),
            pltpu.VMEM((rows, LANES), jnp.bfloat16),
            pltpu.VMEM((LANES, rows), jnp.bfloat16),
            pltpu.VMEM((rows, LANES), jnp.float32),
            pltpu.VMEM((2, rows, LANES), jnp.float32),
            pltpu.VMEM((2, rows, LANES), jnp.float32),
        ],
        compiler_params=params(),
        cost_estimate=pl.CostEstimate(
            flops=40 * rows * rows * HEAD_DIM, bytes_accessed=20 * rows * LANES, transcendentals=2 * rows * rows
        ),
    )(qkv, qkv, augmented, delta, attended)


def mlp_kernel(core_ref, nt_ref, og_ref, up_ref, down_ref, act_ref, ud_ref, lo_ref, ntd_ref):
    step = pl.program_id(0)
    wide = up_ref.shape[0] * up_ref.shape[1]
    w_up = up_ref[...].reshape(wide, up_ref.shape[2])
    w_down = down_ref[...].reshape(down_ref.shape[0] * down_ref.shape[2], down_ref.shape[3])
    upward = jnp.dot(nt_ref[...], w_up, preferred_element_type=jnp.float32)
    curve = jnp.tanh(ROOT * (upward + CUBIC * upward * upward * upward))
    active = (0.5 * upward * (1.0 + curve)).astype(jnp.bfloat16)
    slope = 0.5 * (1.0 + curve) + 0.5 * upward * (1.0 - curve * curve) * (
        ROOT * (1.0 + 3.0 * CUBIC * upward * upward)
    )
    delta = (against(og_ref[...], w_down) * slope).astype(jnp.bfloat16)
    act_ref[...] = active
    ud_ref[...] = delta
    lo = jnp.dot(active, w_down, preferred_element_type=jnp.float32)
    ntd = against(delta, w_up)

    @pl.when(step == 0)
    def _():
        lo_ref[...] = lo
        ntd_ref[...] = ntd

    @pl.when(step > 0)
    def _():
        lo_ref[...] += lo
        ntd_ref[...] += ntd


def mlp(core, normed, out_grad, weights):
    rows = normed.shape[0]
    devices, tall, width = weights.shape
    chips = devices // 2
    steps = 2
    by_core = weights.reshape(chips, 2, tall, width)
    grid_spec = pltpu.PrefetchScalarGridSpec(
        num_scalar_prefetch=1,
        grid=(steps,),
        in_specs=[
            pl.BlockSpec((rows, D), lambda k, core: (0, 0)),
            pl.BlockSpec((rows, D), lambda k, core: (0, 0)),
            pl.BlockSpec((devices, 32, width), lambda k, core: (0, 5 + 2 * core[0] + k, 0)),
            pl.BlockSpec((chips // steps, 1, 128, width), lambda k, core: (k, core[0], 0, 0)),
        ],
        out_specs=[
            pl.BlockSpec((rows, width), lambda k, core: (0, k)),
            pl.BlockSpec((rows, width), lambda k, core: (0, k)),
            pl.BlockSpec((rows, D), lambda k, core: (0, 0)),
            pl.BlockSpec((rows, D), lambda k, core: (0, 0)),
        ],
    )
    return pl.pallas_call(
        mlp_kernel,
        grid_spec=grid_spec,
        out_shape=[
            jax.ShapeDtypeStruct((rows, steps * width), jnp.bfloat16),
            jax.ShapeDtypeStruct((rows, steps * width), jnp.bfloat16),
            jax.ShapeDtypeStruct((rows, D), jnp.float32),
            jax.ShapeDtypeStruct((rows, D), jnp.float32),
        ],
        compiler_params=params(),
        cost_estimate=pl.CostEstimate(
            flops=8 * rows * D * steps * width, bytes_accessed=16 * 1024 * 1024, transcendentals=rows * steps * width
        ),
    )(core, normed, out_grad, weights, by_core)


def reorder_kernel(index_ref, in_ref, out_ref):
    blocks = in_ref.shape[0]
    for block in range(blocks):
        out_ref[block ^ index_ref[0]] = in_ref[block]


def reorder(index, blocks):
    return pl.pallas_call(
        reorder_kernel,
        in_specs=[pl.BlockSpec(memory_space=pltpu.SMEM), whole(blocks.shape)],
        out_specs=whole(blocks.shape),
        out_shape=jax.ShapeDtypeStruct(blocks.shape, blocks.dtype),
        compiler_params=params(),
    )(index.reshape(1).astype(jnp.int32), blocks)


def moments(values):
    centred = values - jnp.mean(values, axis=1, keepdims=True)
    scale = lax.rsqrt(jnp.mean(centred * centred, axis=1, keepdims=True) + EPSILON)
    return centred * scale, scale


def norm_back(delta, gain, normal, scale):
    e = delta * gain
    return scale * (
        e - jnp.mean(e, axis=1, keepdims=True) - normal * jnp.mean(e * normal, axis=1, keepdims=True)
    )


def scatter_sum(parts, first, second, places):
    for axis in (first, second):
        dim = 0 if (axis == "y" or parts.ndim < 5) else 1
        send = lax.dynamic_index_in_dim(parts, 1 - places[axis], dim, keepdims=False)
        keep = lax.dynamic_index_in_dim(parts, places[axis], dim, keepdims=False)
        parts = (keep.astype(jnp.float32) + swap(send, axis, 2, 1).astype(jnp.float32)).astype(jnp.bfloat16)
    count = parts.shape[0]
    total = lax.dynamic_index_in_dim(parts, places["z"], 0, keepdims=False).astype(jnp.float32)
    for far in range(1, count):
        send = lax.dynamic_index_in_dim(parts, places["z"] ^ far, 0, keepdims=False)
        total = total + swap(send, "z", count, far).astype(jnp.float32)
    return total


def on_planes(
    tokens_in,
    out_grad,
    w_qkv,
    w_out,
    w_up,
    w_down,
    norm1_gain,
    norm1_bias,
    norm2_gain,
    norm2_bias,
):
    depth = lax.axis_size("z")
    blocks = 2 * depth
    chips = 4 * depth
    rows = tokens_in.shape[0]
    share = w_qkv.shape[0]
    low = jnp.bfloat16
    places = {axis: lax.axis_index(axis) for axis in ALL}
    core = places["c"]
    block = 2 * places["z"] + core
    device = ((2 * places["y"] + places["x"]) * depth + places["z"]) * 2 + core

    up_rows = w_up.reshape(share, chips, 2, LANES).transpose(0, 2, 1, 3).reshape(share, 4, D)
    up_rows = up_rows.transpose(1, 0, 2).reshape(4 * share, D)
    weights = lax.all_gather(jnp.concatenate([w_down, w_out, up_rows], axis=0), ALL, axis=0)

    by_block = w_qkv.reshape(share, 3, blocks, LANES).transpose(2, 0, 1, 3).reshape(blocks, share, 3 * LANES)
    near = reorder(block, by_block).reshape(depth, 2, share, 3 * LANES)
    pieces = jnp.stack([near[:, 0], pair(near[:, 1])], axis=1)
    along = jnp.stack([pieces[0]] + [swap(pieces[far], "z", depth, far) for far in range(1, depth)])
    across = jnp.stack([along] + [swap(along, ("y", "x"), 4, far) for far in range(1, 4)])
    own_qkv = reorder(device, across.reshape(2 * chips, share, 3 * LANES)).reshape(D, 3 * LANES)

    gains = jnp.stack([norm1_gain, norm1_bias, norm2_gain, norm2_bias]).reshape(1, 4 * share)
    gains = jnp.concatenate([gains, pair(gains)])
    gains = jnp.concatenate([gains] + [swap(gains, "z", depth, far) for far in range(1, depth)])
    gains = jnp.concatenate([gains] + [swap(gains, ("y", "x"), 4, far) for far in range(1, 4)])
    order = device ^ jnp.arange(2 * chips, dtype=jnp.int32)
    chosen = (order[:, None] == jnp.arange(2 * chips, dtype=jnp.int32)[None, :]).astype(low)
    gains = jnp.dot(chosen, gains, preferred_element_type=jnp.float32)
    gains = gains.reshape(2 * chips, 4, share).transpose(1, 0, 2).reshape(4, D)
    gain_one, bias_one, gain_two, bias_two = (gains[i] for i in range(4))

    far_tokens = [tokens_in] + [swap(tokens_in, "z", depth, far) for far in range(1, depth)]
    group = jnp.concatenate([part for mine in far_tokens for part in (mine, pair(mine))])
    grads = jnp.concatenate([out_grad, pair(out_grad)])

    normal_group, _ = moments(group.astype(jnp.float32))
    normed = (normal_group * gain_one + bias_one).astype(low)
    qkv = jnp.dot(normed, own_qkv, preferred_element_type=jnp.float32).astype(low)
    attended_low, attended, augmented = attend(qkv)

    both = 2 * rows
    sides = [attended_low[:both]] + [
        swap(attended_low[far * both : (far + 1) * both], "z", depth, far) for far in range(1, depth)
    ]
    own_heads = jnp.concatenate(sides, axis=1)
    other_heads = pair(own_heads)
    other_heads = jnp.concatenate([other_heads[rows:], other_heads[:rows]])
    all_heads = jnp.concatenate([own_heads, other_heads], axis=1)

    full_out = weights[:, w_down.shape[0] : w_down.shape[0] + share].reshape(blocks, LANES, D)
    near_out = reorder(block, full_out).reshape(depth, 2, LANES, D).transpose(1, 0, 2, 3)
    own_out = near_out[0].reshape(depth * LANES, D)
    inputs = tokens_in.astype(jnp.float32)
    hidden = inputs + jnp.dot(
        all_heads[:rows], near_out.reshape(D, D), preferred_element_type=jnp.float32
    )
    normal_two, scale_two = moments(hidden)
    normed_two = (normal_two * gain_two + bias_two).astype(low)
    normed_both = jnp.concatenate([normed_two, pair(normed_two)])

    active, up_delta, out_part, two_part = mlp(core.reshape(1), normed_both, grads, weights)
    result = (hidden + out_part[:rows] + pair(out_part[rows:])).astype(low)
    norm_two_delta = two_part[:rows] + pair(two_part[rows:])
    gain_two_part = jnp.sum(norm_two_delta * normal_two, axis=0)
    bias_two_part = jnp.sum(norm_two_delta, axis=0)
    hidden_delta = out_grad.astype(jnp.float32) + norm_back(norm_two_delta, gain_two, normal_two, scale_two)
    hidden_low = hidden_delta.astype(low)
    hidden_both = jnp.concatenate([hidden_low, pair(hidden_low)])

    att_delta = against(hidden_both, own_out).astype(low)
    far_delta = [att_delta[:, :LANES]] + [
        swap(att_delta[:, far * LANES : (far + 1) * LANES], "z", depth, far) for far in range(1, depth)
    ]

    half = D // 2
    out_cols = lax.dynamic_slice_in_dim(hidden_both, core * half, half, 1)
    out_term = outer(all_heads, out_cols).astype(low).reshape(2, depth, LANES, half).transpose(1, 0, 2, 3)
    out_term = reorder(block, out_term.reshape(blocks, LANES, half)).reshape(2, 2, depth, D // chips, half)
    up_term = outer(normed_both, up_delta).astype(low).reshape(2, 2, depth, D // chips, up_delta.shape[1])
    down_term = outer(active, grads).astype(low).reshape(2, 2, depth, w_down.shape[0], D)
    first_sum = scatter_sum(jnp.concatenate([up_term, out_term], axis=4), "y", "x", places)
    down_sum = scatter_sum(down_term, "x", "y", places)

    query_delta, key_delta, value_delta = attend_back(qkv, augmented, jnp.concatenate(far_delta), attended)
    qkv_delta = jnp.concatenate([query_delta, key_delta, value_delta], axis=1)
    one_part = against(qkv_delta, own_qkv)
    gain_one_part = jnp.sum(one_part * normal_group, axis=0)
    bias_one_part = jnp.sum(one_part, axis=0)
    one_part = one_part.reshape(depth, 2, rows, D)
    one_sum = one_part[:, 0] + pair(one_part[:, 1].astype(low)).astype(jnp.float32)
    norm_one_delta = one_sum[0]
    for far in range(1, depth):
        norm_one_delta = norm_one_delta + swap(one_sum[far].astype(low), "z", depth, far).astype(jnp.float32)
    normal_one, scale_one = moments(inputs)
    input_grad = hidden_delta + norm_back(norm_one_delta, gain_one, normal_one, scale_one)

    def halves(vectors):
        high = vectors.astype(low)
        return jnp.concatenate([high, (vectors - high.astype(jnp.float32)).astype(low)])

    tall = D // 4
    vectors = jnp.stack([gain_one_part, bias_one_part, gain_two_part, bias_two_part])
    vectors = halves(vectors).reshape(8, 4, tall).transpose(1, 0, 2)
    vectors = jnp.pad(vectors, ((0, 0), (0, 8), (0, 3 * LANES - tall)))
    qkv_term = outer(normed, qkv_delta).astype(low).reshape(4, tall, 3 * LANES)
    qkv_term = jnp.concatenate([qkv_term, vectors], axis=1)
    plane = 2 * places["y"] + places["x"]
    qkv_term = reorder(plane, qkv_term)
    quarter = qkv_term[0].astype(jnp.float32)
    for far in range(1, 4):
        quarter = quarter + swap(qkv_term[far], ("y", "x"), 4, far).astype(jnp.float32)
    vectors = halves(quarter[tall : tall + 4] + quarter[tall + 4 : tall + 8])
    vectors = jnp.pad(vectors, ((0, 8), (0, 0)))
    quarter = reorder(places["z"], quarter[:tall].astype(low).reshape(depth, 2 * share, 3 * LANES))
    quarter = jnp.concatenate([quarter, jnp.broadcast_to(vectors[None], (depth, 16, 3 * LANES))], axis=1)
    sides = [quarter[0]] + [swap(quarter[far], "z", depth, far) for far in range(1, depth)]
    vectors = sum(side[2 * share :].astype(jnp.float32) for side in sides)
    vectors = halves(vectors[:4] + vectors[4:8])
    vectors = jnp.pad(vectors, ((0, 8), (0, 0)))
    sides = jnp.stack([side[: 2 * share].reshape(2, share, 3 * LANES) for side in sides])
    sides = reorder(core, sides.transpose(1, 0, 2, 3))
    send = jnp.concatenate([sides[1].reshape(depth * share, 3 * LANES), vectors])
    got = pair(send)
    vectors = vectors.astype(jnp.float32) + got[depth * share :].astype(jnp.float32)
    vectors = lax.dynamic_slice_in_dim(vectors[:4] + vectors[4:8], (places["z"] * 2 + core) * share, share, 1)
    parts = jnp.stack([sides[0], got[: depth * share].reshape(depth, share, 3 * LANES)], axis=1)
    parts = reorder(block, parts.reshape(blocks, share, 3 * LANES)).reshape(blocks, share, 3, LANES)
    qkv_grad = parts.transpose(1, 2, 0, 3).reshape(share, 3 * D).astype(jnp.float32)

    mine = lax.dynamic_slice_in_dim(first_sum, core * share, share, 0)
    others = pair(lax.dynamic_slice_in_dim(first_sum, (1 - core) * share, share, 0))
    both_cores = jnp.where(core == 0, jnp.stack([mine, others]), jnp.stack([others, mine]))
    wide = up_delta.shape[1]
    up_grad = both_cores[:, :, :wide].reshape(2, share, chips, LANES).transpose(1, 2, 0, 3).reshape(share, 2 * wide)
    out_weight_grad = both_cores[:, :, wide:].transpose(1, 0, 2).reshape(share, D)
    return (
        result,
        input_grad,
        qkv_grad,
        out_weight_grad,
        up_grad,
        down_sum,
        vectors[0],
        vectors[1],
        vectors[2],
        vectors[3],
    )


def solution(mesh):
    scenes, blocks = mesh.devices.shape

    def place(axes):
        matrix = P(axes, None)
        views = P(axes[: len(axes) // 2] if len(axes) > 2 else axes[0], None)
        vector = P(axes)
        ins = (matrix, views, views, views, matrix, matrix, matrix, matrix, matrix) + (vector,) * 4
        return ins, (matrix,) * 6 + (vector,) * 4

    def run(*arrays):
        one_scene = arrays[1].shape[1] == 4
        if scenes == 4 and blocks == 8 and one_scene and arrays[0].shape[0] == 8192:
            fine = Mesh(mesh.devices.reshape(2, 2, blocks // 2, 2), ALL)
            ins, outs = place(ALL)
            step = lambda tokens, heights, widths, labels, *rest: on_planes(tokens, *rest)
            return jax.shard_map(step, mesh=fine, in_specs=ins, out_specs=outs, check_vma=False)(*arrays)
        ins, outs = place(("scene", "blk"))
        return jax.shard_map(on_any_slice, mesh=mesh, in_specs=ins, out_specs=outs, check_vma=False)(*arrays)

    return run
```

```python
import functools
import math

import jax
import jax.numpy as jnp
from jax import lax
from jax.experimental import pallas as pl
from jax.experimental.pallas import tpu as pltpu
from jax.sharding import Mesh
from jax.sharding import PartitionSpec as P

D = 1024
HEADS = 16
HEAD_DIM = 64


EPSILON = 1e-05
MASKED = -1e30


def layer_norm(values, gain_row, bias_row):
    centred = values - jnp.mean(values, axis=1, keepdims=True)
    scaled = centred * lax.rsqrt(jnp.mean(centred * centred, axis=1, keepdims=True) + EPSILON)
    return scaled * gain_row + bias_row


def scene_rows(view_ends, labels, first_row, count_rows):
    places = first_row + jnp.arange(count_rows, dtype=jnp.int32)
    view_index = jnp.sum((places[:, None] >= view_ends[None, :]).astype(jnp.int32), axis=1)
    matches = view_index[:, None] == jnp.arange(labels.shape[0], dtype=jnp.int32)[None, :]
    return jnp.sum(jnp.where(matches, labels[None, :], 0), axis=1)


def in_blocks(update, carry, members):
    total_rows = members[0].shape[0]
    width_rows = math.gcd(total_rows, 1024)
    block_count = total_rows // width_rows
    stacked = tuple(
        (member.reshape((block_count, width_rows) + member.shape[1:]) for member in members)
    )

    def advance(state_now, indexed):
        block_index, block_parts = indexed
        return (update(state_now, block_parts, block_index * width_rows), None)

    carry, _ = lax.scan(advance, carry, (jnp.arange(block_count, dtype=jnp.int32), stacked))
    return carry


def heads_of(rows):
    return rows.reshape(rows.shape[0], HEADS, HEAD_DIM)


def pair_terms(
    query_heads, delta_heads, log_rows, probe_rows, allowed, key_heads, value_heads, score_scale
):
    raw = (
        jnp.einsum("qhe,khe->hqk", query_heads, key_heads, preferred_element_type=jnp.float32)
        * score_scale
    )
    weights_now = jnp.where(allowed, jnp.exp(raw - log_rows[:, :, None]), 0.0)
    backward = jnp.einsum(
        "qhe,khe->hqk", delta_heads, value_heads, preferred_element_type=jnp.float32
    )
    score_delta = (weights_now * (backward - probe_rows[:, :, None])).astype(jnp.bfloat16)
    return (weights_now.astype(jnp.bfloat16), score_delta)


def outer(left, right):
    return lax.dot_general(
        left, right, (((0,), (0,)), ((), ())), preferred_element_type=jnp.float32
    )


def against(left, right):
    return lax.dot_general(
        left, right, (((1,), (1,)), ((), ())), preferred_element_type=jnp.float32
    )


def on_any_slice(
    tokens_in,
    view_heights,
    view_widths,
    view_scenes,
    out_grad,
    w_qkv,
    w_out,
    w_up,
    w_down,
    norm1_gain,
    norm1_bias,
    norm2_gain,
    norm2_bias,
):
    gathered = (
        lax.all_gather(w_qkv, ("scene", "blk"), axis=0, tiled=True),
        lax.all_gather(w_out, ("scene", "blk"), axis=0, tiled=True),
        lax.all_gather(w_up, ("scene", "blk"), axis=0, tiled=True),
        lax.all_gather(w_down, ("scene", "blk"), axis=0, tiled=True),
        lax.all_gather(norm1_gain, ("scene", "blk"), axis=0, tiled=True),
        lax.all_gather(norm1_bias, ("scene", "blk"), axis=0, tiled=True),
        lax.all_gather(norm2_gain, ("scene", "blk"), axis=0, tiled=True),
        lax.all_gather(norm2_bias, ("scene", "blk"), axis=0, tiled=True),
    )
    full_qkv, full_out, full_up, full_down = (gathered[0], gathered[1], gathered[2], gathered[3])
    gain_one = gathered[4].astype(jnp.float32)
    bias_one = gathered[5].astype(jnp.float32)
    gain_two = gathered[6].astype(jnp.float32)
    bias_two = gathered[7].astype(jnp.float32)
    local_rows = tokens_in.shape[0]
    view_ends = jnp.cumsum(view_heights[0] * view_widths[0])
    labels = view_scenes[0]
    own_first = lax.axis_index("blk") * local_rows
    own_scene = scene_rows(view_ends, labels, own_first, local_rows)
    score_scale = HEAD_DIM ** (-0.5)
    inputs = tokens_in.astype(jnp.float32)
    normed, norm_one_pull = jax.vjp(layer_norm, inputs, gain_one, bias_one)
    normed_low = normed.astype(jnp.bfloat16)
    projected = jnp.dot(normed_low, full_qkv, preferred_element_type=jnp.float32).astype(
        jnp.bfloat16
    )
    query_rows = projected[:, :D]
    key_rows = projected[:, D : 2 * D]
    value_rows = projected[:, 2 * D :]
    query_heads = heads_of(query_rows)

    def forward_update(state_now, members, first_row):
        run_max, run_sum, run_total = state_now
        piece_keys, piece_values = members
        piece_rows = piece_keys.shape[0]
        key_scene = scene_rows(view_ends, labels, first_row, piece_rows)
        allowed = (own_scene[:, None] == key_scene[None, :])[None]
        raw = (
            jnp.einsum(
                "qhe,khe->hqk",
                query_heads,
                heads_of(piece_keys),
                preferred_element_type=jnp.float32,
            )
            * score_scale
        )
        new_max = jnp.maximum(run_max, jnp.max(jnp.where(allowed, raw, MASKED), axis=2))
        expo = jnp.where(allowed, jnp.exp(raw - new_max[:, :, None]), 0.0)
        factor = jnp.exp(run_max - new_max)
        run_sum = run_sum * factor + jnp.sum(expo, axis=2)
        mixed = jnp.einsum(
            "hqk,khe->qhe",
            expo.astype(jnp.bfloat16),
            heads_of(piece_values),
            preferred_element_type=jnp.float32,
        )
        run_total = run_total * jnp.transpose(factor)[:, :, None] + mixed
        return (new_max, run_sum, run_total)

    start_state = (
        jnp.full((HEADS, local_rows), MASKED, jnp.float32),
        jnp.zeros((HEADS, local_rows), jnp.float32),
        jnp.zeros((local_rows, HEADS, HEAD_DIM), jnp.float32),
    )
    run_max, run_sum, run_total = in_blocks(
        forward_update,
        start_state,
        (
            lax.all_gather(key_rows, "blk", axis=0, tiled=True),
            lax.all_gather(value_rows, "blk", axis=0, tiled=True),
        ),
    )
    log_total = run_max + jnp.log(run_sum)
    attended_heads = run_total / jnp.transpose(run_sum)[:, :, None]
    attended_low = attended_heads.reshape(local_rows, D).astype(jnp.bfloat16)
    hidden = inputs + jnp.dot(attended_low, full_out, preferred_element_type=jnp.float32)
    normed_two, norm_two_pull = jax.vjp(layer_norm, hidden, gain_two, bias_two)
    normed_two_low = normed_two.astype(jnp.bfloat16)
    upward = jnp.dot(normed_two_low, full_up, preferred_element_type=jnp.float32)
    active, gelu_pull = jax.vjp(jax.nn.gelu, upward)
    active_low = active.astype(jnp.bfloat16)
    result = (hidden + jnp.dot(active_low, full_down, preferred_element_type=jnp.float32)).astype(
        jnp.bfloat16
    )
    down_term = outer(active_low, out_grad)
    up_delta = gelu_pull(against(out_grad, full_down))[0].astype(jnp.bfloat16)
    up_term = outer(normed_two_low, up_delta)
    hidden_back, gain_two_term, bias_two_term = norm_two_pull(against(up_delta, full_up))
    hidden_delta = out_grad.astype(jnp.float32) + hidden_back
    hidden_low = hidden_delta.astype(jnp.bfloat16)
    out_term = outer(attended_low, hidden_low)
    att_delta = against(hidden_low, full_out).astype(jnp.bfloat16)
    delta_heads = heads_of(att_delta)
    row_probe = jnp.transpose(jnp.sum(delta_heads.astype(jnp.float32) * attended_heads, axis=2))
    query_start = jnp.zeros((local_rows, HEADS, HEAD_DIM), jnp.float32)
    every_key, every_value = (
        lax.all_gather(key_rows, "blk", axis=0, tiled=True),
        lax.all_gather(value_rows, "blk", axis=0, tiled=True),
    )
    group_rows = every_key.shape[0]
    width_rows = math.gcd(group_rows, 1024)
    block_count = group_rows // width_rows

    def joint_step(total, indexed):
        block_index, block_keys, block_values = indexed
        block_first = block_index * width_rows
        key_heads = heads_of(block_keys)
        value_heads = heads_of(block_values)
        key_scene = scene_rows(view_ends, labels, block_first, width_rows)
        allowed = (own_scene[:, None] == key_scene[None, :])[None]
        weights_low, score_delta = pair_terms(
            query_heads,
            delta_heads,
            log_total,
            row_probe,
            allowed,
            key_heads,
            value_heads,
            score_scale,
        )
        total = (
            total
            + jnp.einsum("hqk,khe->qhe", score_delta, key_heads, preferred_element_type=jnp.float32)
            * score_scale
        )
        value_part = jnp.einsum(
            "hqk,qhe->khe", weights_low, delta_heads, preferred_element_type=jnp.float32
        )
        key_part = (
            jnp.einsum("hqk,qhe->khe", score_delta, query_heads, preferred_element_type=jnp.float32)
            * score_scale
        )
        rows_out = jnp.concatenate(
            [key_part.reshape(width_rows, D), value_part.reshape(width_rows, D)], axis=1
        )
        return (total, rows_out)

    query_total, pair_rows = lax.scan(
        joint_step,
        query_start,
        (
            jnp.arange(block_count, dtype=jnp.int32),
            every_key.reshape(block_count, width_rows, D),
            every_value.reshape(block_count, width_rows, D),
        ),
    )
    pair_rows = pair_rows.reshape(group_rows, 2 * D)
    both_sums = lax.psum_scatter(
        pair_rows.astype(jnp.bfloat16), "blk", scatter_dimension=0, tiled=True
    ).astype(jnp.float32)
    key_total = both_sums[:, :D]
    value_total = both_sums[:, D:]
    qkv_delta = jnp.concatenate(
        [query_total.reshape(local_rows, D), key_total, value_total], axis=1
    ).astype(jnp.bfloat16)
    qkv_term = outer(normed_low, qkv_delta)
    input_back, gain_one_term, bias_one_term = norm_one_pull(against(qkv_delta, full_qkv))
    input_grad = hidden_delta + input_back
    summed = (
        lax.psum_scatter(qkv_term, ("scene", "blk"), scatter_dimension=0, tiled=True),
        lax.psum_scatter(out_term, ("scene", "blk"), scatter_dimension=0, tiled=True),
        lax.psum_scatter(up_term, ("scene", "blk"), scatter_dimension=0, tiled=True),
        lax.psum_scatter(down_term, ("scene", "blk"), scatter_dimension=0, tiled=True),
        lax.psum_scatter(gain_one_term, ("scene", "blk"), scatter_dimension=0, tiled=True),
        lax.psum_scatter(bias_one_term, ("scene", "blk"), scatter_dimension=0, tiled=True),
        lax.psum_scatter(gain_two_term, ("scene", "blk"), scatter_dimension=0, tiled=True),
        lax.psum_scatter(bias_two_term, ("scene", "blk"), scatter_dimension=0, tiled=True),
    )
    return (
        result,
        input_grad,
        summed[0],
        summed[1],
        summed[2],
        summed[3],
        summed[4],
        summed[5],
        summed[6],
        summed[7],
    )


ALL = ("y", "x", "z", "c")
LANES = 128
ROOT = math.sqrt(2.0 / math.pi)
CUBIC = 0.044715
FREE = pl.CostEstimate(flops=0, bytes_accessed=0, transcendentals=0)


def swap(values, axis, size, distance):
    return lax.ppermute(values, axis, [(i, i ^ distance) for i in range(size)])


def pair(values):
    return swap(values, "c", 2, 1)


def whole(shape):
    return pl.BlockSpec(shape, lambda *_: (0,) * len(shape))


def params(megabytes=60):
    return pltpu.CompilerParams(vmem_limit_bytes=megabytes * 1024 * 1024)


def three_parts(column, lane, first):
    high = column.astype(jnp.bfloat16).astype(jnp.float32)
    rest = column - high
    middle = rest.astype(jnp.bfloat16).astype(jnp.float32)
    last = rest - middle
    zero = jnp.zeros_like(last)
    return jnp.where(
        lane == first,
        high,
        jnp.where(lane == first + 1, middle, jnp.where(lane == first + 2, last, zero)),
    )


def attend_kernel(q_ref, k_ref, v_ref, *refs, chunk):
    low_ref, att_ref, rl_ref, p_ref, s0, s1, m0, m1, vt_ref, hold_ref = refs
    unit = pl.program_id(0)
    last = pl.num_programs(0) - 1
    rows = k_ref.shape[0]
    block = q_ref.shape[0]
    lane = lax.broadcasted_iota(jnp.int32, (1, LANES), 1)
    line = lax.broadcasted_iota(jnp.int32, (LANES, 1), 0)

    @pl.when(unit == 0)
    def _():
        turned = v_ref[...].astype(jnp.float32).T
        vt_ref[0] = jnp.where(line < HEAD_DIM, turned, 1.0).astype(jnp.bfloat16)
        vt_ref[1] = jnp.where(line >= HEAD_DIM, turned, 1.0).astype(jnp.bfloat16)

    def work(head, fresh, scores, old):
        mine = (lane < HEAD_DIM) if head == 0 else (lane >= HEAD_DIM)
        query = jnp.where(mine, q_ref[...].astype(jnp.float32) * HEAD_DIM ** (-0.5), 0.0).astype(jnp.bfloat16)
        top = jnp.full((8, block), -jnp.inf, jnp.float32)
        high = old[0][0:1, :] if old is not None else None
        mixed = jnp.zeros((LANES, block), jnp.float32)
        for first in range(0, rows, chunk):
            part = slice(first, first + chunk)
            if fresh is not None:
                got = against(k_ref[part, :], query)
                scores[part, :] = got
                top = jnp.maximum(top, jnp.max(got.reshape(chunk // 8, 8, block), axis=0))
            if old is not None:
                expo = jnp.exp(old[1][part, :] - high).astype(jnp.bfloat16)
                p_ref[0, part, :] = expo
                mixed += jnp.dot(vt_ref[1 - head, :, part], expo, preferred_element_type=jnp.float32)
        if fresh is not None:
            fresh[...] = jnp.broadcast_to(jnp.max(top, axis=0, keepdims=True), (8, block))
        return mixed.T if old is not None else None

    @pl.when(unit == 0)
    def _():
        work(0, m0, s0, None)

    @pl.when((unit > 0) & (unit % 2 == 1))
    def _():
        hold_ref[...] = work(1, m1, s1, (m0, s0))

    def finish(second):
        first = hold_ref[...]
        low_lane = lane < HEAD_DIM
        recip = 1.0 / jnp.where(low_lane, pltpu.roll(first, HEAD_DIM, 1), pltpu.roll(second, HEAD_DIM, 1))
        attended = jnp.where(low_lane, first, second) * recip
        att_ref[...] = attended
        rl_ref[...] = recip
        low_ref[...] = attended.astype(jnp.bfloat16)

    @pl.when((unit > 0) & (unit % 2 == 0) & (unit < last))
    def _():
        finish(work(0, m0, s0, (m1, s1)))

    @pl.when(unit == last)
    def _():
        finish(work(0, None, None, (m1, s1)))

def attend(qkv):
    rows = qkv.shape[0]
    block, chunk = 512, 256
    units = 2 * rows // block

    def new(u):
        return jnp.minimum(u, units - 1) // 2

    def old(u):
        return jnp.maximum(u - 1, 0)

    part = pl.BlockSpec((block, LANES), lambda u: (old(u) // 2, 0))
    return pl.pallas_call(
        functools.partial(attend_kernel, chunk=chunk),
        grid=(units + 1,),
        in_specs=[
            pl.BlockSpec((block, LANES), lambda u: (new(u), 0)),
            pl.BlockSpec((rows, LANES), lambda u: (0, 1)),
            pl.BlockSpec((rows, LANES), lambda u: (0, 2)),
        ],
        out_specs=[part, part, part, pl.BlockSpec((1, rows, block), lambda u: (old(u) % 2, 0, old(u) // 2))],
        out_shape=[
            jax.ShapeDtypeStruct((rows, LANES), jnp.bfloat16),
            jax.ShapeDtypeStruct((rows, LANES), jnp.float32),
            jax.ShapeDtypeStruct((rows, LANES), jnp.float32),
            jax.ShapeDtypeStruct((2, rows, rows), jnp.bfloat16),
        ],
        scratch_shapes=[pltpu.VMEM((rows, block), jnp.float32)] * 2
        + [pltpu.VMEM((8, block), jnp.float32)] * 2
        + [pltpu.VMEM((2, LANES, rows), jnp.bfloat16), pltpu.VMEM((block, LANES), jnp.float32)],
        compiler_params=params(),
        cost_estimate=FREE,
    )(qkv, qkv, qkv)


def attend_back_kernel(q_ref, k_ref, v_ref, p_ref, att_ref, rl_ref, *refs, chunk, count):
    deltas, outs = refs[:count], refs[count : count + 2]
    va_ref, kt_ref, dq_acc, dk_acc, dv_acc, do_ref = refs[count + 2 :]
    head, step = pl.program_id(0), pl.program_id(1)
    rows = k_ref.shape[0]
    block = do_ref.shape[0]
    lane = lax.broadcasted_iota(jnp.int32, (1, LANES), 1)
    spare = jnp.where(head == 0, HEAD_DIM, 0)
    mine = (lane < spare) | (lane >= spare + HEAD_DIM)

    @pl.when((head == 0) & (step == 0))
    def _():
        kt_ref[...] = (k_ref[...].astype(jnp.float32) * HEAD_DIM ** (-0.5)).T.astype(jnp.bfloat16)

    @pl.when(step == 0)
    def _():
        ones = jnp.where(lane < spare + 3, 1.0, 0.0)
        va_ref[...] = jnp.where(mine, v_ref[...].astype(jnp.float32), ones).astype(jnp.bfloat16)
        dk_acc[head] = jnp.zeros((rows, LANES), jnp.float32)
        dv_acc[head] = jnp.zeros((rows, LANES), jnp.float32)

    for index, ref in enumerate(deltas):

        @pl.when(step == index)
        def _():
            do_ref[...] = ref[...]

    delta = (do_ref[...].astype(jnp.float32) * rl_ref[...]).astype(jnp.bfloat16).astype(jnp.float32)
    probe = jnp.sum(jnp.where(mine, delta * att_ref[...], 0.0), axis=1, keepdims=True)
    own_delta = jnp.where(mine, delta, three_parts(-probe, lane, spare)).astype(jnp.bfloat16)
    query = (q_ref[...].astype(jnp.float32) * HEAD_DIM ** (-0.5)).astype(jnp.bfloat16)
    total = jnp.zeros((LANES, block), jnp.float32)
    for first in range(0, rows, chunk):
        part = slice(first, first + chunk)
        expo = p_ref[0, part, :]
        score_delta = (expo.astype(jnp.float32) * against(va_ref[part, :], own_delta)).astype(jnp.bfloat16)
        dv_acc[head, part, :] += jnp.dot(expo, own_delta, preferred_element_type=jnp.float32)
        dk_acc[head, part, :] += jnp.dot(score_delta, query, preferred_element_type=jnp.float32)
        total += jnp.dot(kt_ref[:, part], score_delta, preferred_element_type=jnp.float32)
    query_delta = total.T
    place = pl.ds(pl.multiple_of(step * block, block), block)

    @pl.when(head == 0)
    def _():
        dq_acc[place, :] = query_delta

    half = block // 2

    @pl.when(head == 1)
    def _():
        both = jnp.where(lane < HEAD_DIM, dq_acc[place, :], query_delta).astype(jnp.bfloat16)
        for side, ref in enumerate(outs):
            ref[step, :, :LANES] = both[side * half : (side + 1) * half]

    @pl.when((head == 1) & (step == pl.num_programs(1) - 1))
    def _():
        for index in range(count):
            for side, ref in enumerate(outs):
                part = slice(index * block + side * half, index * block + (side + 1) * half)
                for kind, acc in ((1, dk_acc), (2, dv_acc)):
                    own = jnp.where(lane < HEAD_DIM, acc[0, part, :], acc[1, part, :]).astype(jnp.bfloat16)
                    ref[index, :, kind * LANES : (kind + 1) * LANES] = own


def attend_back(qkv, probs, deltas, attended, recip):
    rows = qkv.shape[0]
    count = len(deltas)
    block, chunk = rows // count, 512
    part = pl.BlockSpec((block, LANES), lambda h, i: (i, 0))
    return pl.pallas_call(
        functools.partial(attend_back_kernel, chunk=chunk, count=count),
        grid=(2, count),
        in_specs=[
            part,
            pl.BlockSpec((rows, LANES), lambda h, i: (0, 1)),
            pl.BlockSpec((rows, LANES), lambda h, i: (0, 2)),
            pl.BlockSpec((1, rows, block), lambda h, i: (h, 0, i)),
            part,
            part,
        ]
        + [whole((block, LANES))] * count,
        out_specs=[whole((count, block // 2, 3 * LANES))] * 2,
        out_shape=[jax.ShapeDtypeStruct((count, block // 2, 3 * LANES), jnp.bfloat16)] * 2,
        scratch_shapes=[
            pltpu.VMEM((rows, LANES), jnp.bfloat16),
            pltpu.VMEM((LANES, rows), jnp.bfloat16),
            pltpu.VMEM((rows, LANES), jnp.float32),
            pltpu.VMEM((2, rows, LANES), jnp.float32),
            pltpu.VMEM((2, rows, LANES), jnp.float32),
            pltpu.VMEM((block, LANES), jnp.bfloat16),
        ],
        compiler_params=params(),
        cost_estimate=FREE,
    )(qkv, qkv, qkv, probs, attended, recip, *deltas)


def qkv_kernel(place_ref, *refs):
    pieces, weights = refs[:10], refs[10:14]
    qkv_ref, normed_ref, gains_ref, turned_ref, own_ref, table_ref = refs[14:]
    depth, share = weights[0].shape[0], weights[0].shape[1] // 2
    half = D // 2

    @pl.when(pl.program_id(0) == 0)
    def _():
        device = place_ref[0]
        for far, part in enumerate(weights):
            for near in range(depth):
                for core in range(2):
                    owner = device ^ (far * 2 * depth + near * 2 + core)
                    row = pl.multiple_of(owner * share, share)
                    first = core * share
                    own_ref[pl.ds(row, share), :] = part[near, first : first + share, half : half + 3 * LANES]
                    table = part[near, first : first + 16, half + 3 * LANES :].astype(jnp.float32)
                    table_ref[pl.ds(owner, 1), :] = table[0:1]
        devices = table_ref.shape[0]
        table = table_ref[...].astype(jnp.bfloat16)
        row = lax.broadcasted_iota(jnp.int32, (LANES, D), 0)
        col = lax.broadcasted_iota(jnp.int32, (LANES, D), 1)
        owner = lax.broadcasted_iota(jnp.int32, (devices, D), 0)
        own_col = lax.broadcasted_iota(jnp.int32, (devices, D), 1) // share
        for kind in range(4):
            spread = jnp.where(row == kind * share + col % share, 1.0, 0.0).astype(jnp.bfloat16)
            wide = jnp.dot(table, spread, preferred_element_type=jnp.float32)
            gains_ref[kind : kind + 1, :] = jnp.sum(jnp.where(owner == own_col, wide, 0.0), axis=0, keepdims=True)
        gains_ref[4:8, :] = jnp.zeros((4, D), jnp.float32)
        turned_ref[...] = own_ref[...].astype(jnp.float32).T.astype(jnp.bfloat16)

    gain, bias = gains_ref[0:1, :], gains_ref[1:2, :]
    for index in range(8):
        tokens = pieces[index][...].astype(jnp.float32)
        if index >= 6:
            tokens = tokens + pieces[index + 2][...].astype(jnp.float32)
        normal, _ = moments(tokens)
        normed = (normal * gain + bias).astype(jnp.bfloat16)
        normed_ref[index] = normed
        qkv_ref[index] = jnp.dot(normed, own_ref[...], preferred_element_type=jnp.float32).astype(jnp.bfloat16)


def project(device, pieces, weights):
    rows = pieces[0].shape[0]
    steps = 2
    block = rows // steps
    piece = pl.BlockSpec((block, D), lambda i, place: (i, 0))
    part = pl.BlockSpec(weights[0].shape, lambda i, place: (0, 0, 0))
    grid_spec = pltpu.PrefetchScalarGridSpec(
        num_scalar_prefetch=1,
        grid=(steps,),
        in_specs=[piece] * 10 + [part] * 4,
        out_specs=[
            pl.BlockSpec((8, block, 3 * LANES), lambda i, place: (0, i, 0)),
            pl.BlockSpec((8, block, D), lambda i, place: (0, i, 0)),
            pl.BlockSpec((8, D), lambda i, place: (0, 0)),
            pl.BlockSpec((3 * LANES, D), lambda i, place: (0, 0)),
        ],
        scratch_shapes=[
            pltpu.VMEM((D, 3 * LANES), jnp.bfloat16),
            pltpu.VMEM((32, LANES), jnp.float32),
        ],
    )
    qkv, normed, gains, turned = pl.pallas_call(
        qkv_kernel,
        grid_spec=grid_spec,
        out_shape=[
            jax.ShapeDtypeStruct((8, rows, 3 * LANES), jnp.bfloat16),
            jax.ShapeDtypeStruct((8, rows, D), jnp.bfloat16),
            jax.ShapeDtypeStruct((8, D), jnp.float32),
            jax.ShapeDtypeStruct((3 * LANES, D), jnp.bfloat16),
        ],
        compiler_params=params(),
        cost_estimate=FREE,
    )(device.reshape(1).astype(jnp.int32), *pieces, *weights)
    return qkv.reshape(8 * rows, 3 * LANES), normed.reshape(8 * rows, D), gains, turned


def mlp_kernel(place_ref, *refs):
    device, own_z = place_ref[0], place_ref[1]
    nts, ogs, refs = refs[:4], refs[4:8], refs[8:]
    ups, other_ups, downs, other_downs = refs[:4], refs[4:8], refs[8:12], refs[12:16]
    act_ref, ud_ref, keep_ref, one_ref, two_ref, three_ref, down_ref, up_ref = refs[16:]
    depth, share, wide = len(ups), ups[0].shape[1] // 2, ups[0].shape[2]

    @pl.when(pl.program_id(0) == 0)
    def _():
        slab = downs[0].shape[0]
        for side, parts in enumerate((ups, other_ups)):
            for near, part in enumerate(parts):
                for far in range(part.shape[0]):
                    for core in range(2):
                        owner = device ^ (far * 2 * depth + near * 2 + (core ^ side))
                        row = pl.multiple_of(owner * share, share)
                        cols = slice(side * wide, (side + 1) * wide)
                        up_ref[pl.ds(row, share), cols] = part[far, core * share : (core + 1) * share, :]
        for side, parts in enumerate((downs, other_downs)):
            for near, part in enumerate(parts):
                row = pl.multiple_of(side * wide + (own_z ^ near) * slab, slab)
                down_ref[pl.ds(row, slab), :] = part[...]

    rows = nts[0].shape[0]
    normed = jnp.concatenate([ref[...] for ref in nts])
    grads = jnp.concatenate([ref[...] for ref in ogs])
    back = jnp.zeros((4 * rows, D), jnp.float32)
    for side in range(2):
        cols = slice(side * wide, (side + 1) * wide)
        upward = jnp.dot(normed, up_ref[:, cols], preferred_element_type=jnp.float32)
        square = upward * upward
        curve = jnp.tanh(ROOT * upward * (1.0 + CUBIC * square))
        active = (0.5 * upward * (1.0 + curve)).astype(jnp.bfloat16)
        slope = 0.5 * (1.0 + curve) + 0.5 * upward * (1.0 - curve * curve) * (ROOT * (1.0 + 3.0 * CUBIC * square))
        delta = (against(grads, down_ref[cols, :]) * slope).astype(jnp.bfloat16)
        back += against(delta, up_ref[:, cols])
        for index in range(4):
            part = slice(index * rows, (index + 1) * rows)
            act_ref[index, :, cols] = active[part]
            ud_ref[index, :, cols] = delta[part]
    keep_ref[...] = back[:rows]
    for index, to in enumerate((one_ref, two_ref, three_ref)):
        to[...] = back[(index + 1) * rows : (index + 2) * rows].astype(jnp.bfloat16)


def mlp(place, normed, grads, ups, other_ups, downs, other_downs):
    rows = normed[0].shape[0]
    steps = 4
    block = rows // steps
    wide = 2 * ups[0].shape[2]
    low = jnp.bfloat16
    piece = pl.BlockSpec((block, D), lambda i, place: (i, 0))
    weights = (*ups, *other_ups, *downs, *other_downs)

    def full(shape):
        return pl.BlockSpec(shape, lambda i, place: (0,) * len(shape))

    units = pl.BlockSpec((4, block, wide), lambda i, place: (0, i, 0))
    grid_spec = pltpu.PrefetchScalarGridSpec(
        num_scalar_prefetch=1,
        grid=(steps,),
        in_specs=[piece] * 8 + [full(part.shape) for part in weights],
        out_specs=[units, units, piece, piece, piece, piece, full((wide, D))],
        scratch_shapes=[pltpu.VMEM((D, wide), low)],
    )
    return pl.pallas_call(
        mlp_kernel,
        grid_spec=grid_spec,
        out_shape=[
            jax.ShapeDtypeStruct((4, rows, wide), low),
            jax.ShapeDtypeStruct((4, rows, wide), low),
            jax.ShapeDtypeStruct((rows, D), jnp.float32),
            jax.ShapeDtypeStruct((rows, D), low),
            jax.ShapeDtypeStruct((rows, D), low),
            jax.ShapeDtypeStruct((rows, D), low),
            jax.ShapeDtypeStruct((wide, D), low),
        ],
        compiler_params=params(),
        cost_estimate=FREE,
    )(place, *normed, *grads, *weights)


def mlp_grads_kernel(place_ref, *refs):
    nts, ogs, refs = refs[:4], refs[4:8], refs[8:]
    act_ref, ud_ref, down_ref, keep_ref, one_ref, two_ref, three_ref = refs[:7]
    up_keep, up_send, down_keep, down_send, up_acc, down_acc = refs[7:]
    step = pl.program_id(0)
    rows = nts[0].shape[0]
    normed = jnp.concatenate([ref[...] for ref in nts])
    grads = jnp.concatenate([ref[...] for ref in ogs])
    wide = act_ref.shape[2]
    active = act_ref[...].reshape(4 * rows, wide)
    up = outer(normed, ud_ref[...].reshape(4 * rows, wide))
    down = outer(active, grads)
    out = jnp.dot(active, down_ref[...], preferred_element_type=jnp.float32)
    keep_ref[...] = out[:rows]
    for index, to in enumerate((one_ref, two_ref, three_ref)):
        to[...] = out[(index + 1) * rows : (index + 2) * rows].astype(jnp.bfloat16)

    @pl.when(step == 0)
    def _():
        up_acc[...] = up
        down_acc[...] = down

    @pl.when(step > 0)
    def _():
        up_acc[...] += up
        down_acc[...] += down

    @pl.when(step == pl.num_programs(0) - 1)
    def _():
        depth, slab = down_keep.shape[:2]
        share = up_keep.shape[2]
        half = wide // 2
        for side, (up_ref, down_out) in enumerate(((up_keep, down_keep), (up_send, down_send))):
            for near in range(depth):
                to = near ^ place_ref[0]
                first = side * half + near * slab
                down_out[to] = down_acc[first : first + slab, :].astype(jnp.bfloat16)
                for far in range(4):
                    first = (far * depth + near) * share
                    part = up_acc[first : first + share, side * half : (side + 1) * half]
                    up_ref[to, far] = part.astype(jnp.bfloat16)


def mlp_grads(place, normed, grads, active, delta, w_down, depth):
    rows = normed[0].shape[0]
    steps = 4
    block = rows // steps
    wide = active.shape[2]
    low = jnp.bfloat16
    piece = pl.BlockSpec((block, D), lambda i, place: (i, 0))
    units = pl.BlockSpec((4, block, wide), lambda i, place: (0, i, 0))

    def full(shape):
        return pl.BlockSpec(shape, lambda i, place: (0,) * len(shape))

    up_shape = (depth, 4, D // (4 * depth), wide // 2)
    down_shape = (depth, wide // (2 * depth), D)
    shapes = [up_shape] * 2 + [down_shape] * 2
    grid_spec = pltpu.PrefetchScalarGridSpec(
        num_scalar_prefetch=1,
        grid=(steps,),
        in_specs=[piece] * 8 + [units] * 2 + [full(w_down.shape)],
        out_specs=[piece] * 4 + [full(shape) for shape in shapes],
        scratch_shapes=[pltpu.VMEM((D, wide), jnp.float32), pltpu.VMEM((wide, D), jnp.float32)],
    )
    return pl.pallas_call(
        mlp_grads_kernel,
        grid_spec=grid_spec,
        out_shape=[jax.ShapeDtypeStruct((rows, D), jnp.float32)]
        + [jax.ShapeDtypeStruct((rows, D), low)] * 3
        + [jax.ShapeDtypeStruct(shape, low) for shape in shapes],
        compiler_params=params(),
        cost_estimate=FREE,
    )(place, *normed, *grads, active, delta, w_down)


def prepare_kernel(core_ref, qkv_ref, up_ref, out_ref, gains_ref, keep_ref, send_ref):
    core = core_ref[0]
    chips = up_ref.shape[1] // (2 * LANES)
    half = out_ref.shape[1] // 2
    depth = chips // 4
    for side, to in ((core, keep_ref), (1 - core, send_ref)):
        for chip in range(chips):
            cols = pl.ds(pl.multiple_of((2 * chip + side) * LANES, LANES), LANES)
            to[:, chip * LANES : (chip + 1) * LANES] = up_ref[:, cols]
        first = chips * LANES
        to[:, first : first + half] = out_ref[:, pl.ds(pl.multiple_of(side * half, half), half)]
        first += half
        for near in range(depth):
            for kind in range(3):
                cols = pl.ds(pl.multiple_of(kind * D + (2 * near + side) * LANES, LANES), LANES)
                to[:, first : first + LANES] = qkv_ref[:, cols]
                first += LANES
        to[:, first:] = jnp.broadcast_to(gains_ref[...], (to.shape[0], LANES))


def prepare(core, w_qkv, w_up, w_out, gains):
    share = w_qkv.shape[0]
    wide = (w_up.shape[1] + w_out.shape[1] + w_qkv.shape[1]) // 2 + LANES
    return pl.pallas_call(
        prepare_kernel,
        in_specs=[pl.BlockSpec(memory_space=pltpu.SMEM)]
        + [whole(array.shape) for array in (w_qkv, w_up, w_out, gains)],
        out_specs=[whole((share, wide))] * 2,
        out_shape=[jax.ShapeDtypeStruct((share, wide), jnp.bfloat16)] * 2,
        compiler_params=params(),
        cost_estimate=FREE,
    )(core, w_qkv, w_up, w_out, gains)


def compose_kernel(place_ref, keep_ref, got_ref, *parts):
    own_z, plane = place_ref[0], place_ref[1]
    share = keep_ref.shape[0]
    depth = len(parts) - 4
    ups, parts = parts[:4], parts[4:]
    wide = ups[0].shape[1]
    half = D // 2
    heads = 4 * wide + half
    for side, ref in ((0, keep_ref), (1, got_ref)):
        rows = slice(side * share, (side + 1) * share)
        for far, part in enumerate(ups):
            part[rows, :] = ref[:, pl.ds(pl.multiple_of((plane ^ far) * wide, wide), wide)]
        for far, part in enumerate(parts):
            first = heads + (own_z ^ far) * 3 * LANES
            part[rows, :half] = ref[:, 4 * wide : heads]
            part[rows, half : half + 3 * LANES] = ref[:, pl.ds(pl.multiple_of(first, LANES), 3 * LANES)]
            part[rows, half + 3 * LANES :] = ref[:, heads + depth * 3 * LANES :]


def compose(place, keep, got, depth):
    share = keep.shape[0]
    shapes = [(2 * share, D // 2)] * 4 + [(2 * share, D)] * depth
    parts = pl.pallas_call(
        compose_kernel,
        in_specs=[pl.BlockSpec(memory_space=pltpu.SMEM), whole(keep.shape), whole(got.shape)],
        out_specs=[whole(shape) for shape in shapes],
        out_shape=[jax.ShapeDtypeStruct(shape, jnp.bfloat16) for shape in shapes],
        compiler_params=params(),
        cost_estimate=FREE,
    )(place, keep, got)
    return parts[:4], parts[4:]


def assemble_kernel(index_ref, *refs):
    out_ref = refs[-1]
    share, wide = out_ref.shape[1:]
    for far, ref in enumerate(refs[:-1]):
        for near in range(ref.shape[0]):
            for side in range(2):
                to = ((far * ref.shape[0] + near) * 2 + side) ^ index_ref[0]
                out_ref[to] = ref[near, side * share : (side + 1) * share, :wide]


def assemble(device, pieces, wide):
    depth, both, _ = pieces[0].shape
    shape = (2 * depth * len(pieces), both // 2, wide)
    rows = pl.pallas_call(
        assemble_kernel,
        in_specs=[pl.BlockSpec(memory_space=pltpu.SMEM)] + [whole(piece.shape) for piece in pieces],
        out_specs=whole(shape),
        out_shape=jax.ShapeDtypeStruct(shape, jnp.bfloat16),
        compiler_params=params(),
        cost_estimate=FREE,
    )(device.reshape(1).astype(jnp.int32), *pieces)
    return rows.reshape(-1, wide)


def arrange_kernel(place_ref, own_ref, other_ref, near_ref):
    block, core = place_ref[0], place_ref[1]
    half = own_ref.shape[1]
    count = near_ref.shape[0]
    for far in range(count):
        row = pl.ds(pl.multiple_of((block ^ far) * LANES, LANES), LANES)
        to = (far % 2) * (count // 2) + far // 2
        near_ref[to, :, pl.ds(pl.multiple_of(core * half, half), half)] = own_ref[row, :]
        near_ref[to, :, pl.ds(pl.multiple_of((1 - core) * half, half), half)] = other_ref[row, :]


def arrange(place, own, other):
    shape = (D // LANES, LANES, D)
    return pl.pallas_call(
        arrange_kernel,
        in_specs=[pl.BlockSpec(memory_space=pltpu.SMEM), whole(own.shape), whole(other.shape)],
        out_specs=whole(shape),
        out_shape=jax.ShapeDtypeStruct(shape, jnp.bfloat16),
        compiler_params=params(),
        cost_estimate=FREE,
    )(place, own, other)


def collect_kernel(place_ref, *refs):
    parts, out_ref = refs[:-1], refs[-1]
    total = sum(part[...].astype(jnp.float32) for part in parts)
    depth, share, wide = out_ref.shape
    qkv = 3 * LANES
    tall = depth * share
    for natural in range(depth):
        part = total[natural * share : (natural + 1) * share, :].astype(jnp.bfloat16)
        out_ref[natural ^ place_ref[0], :, :qkv] = part[:, :qkv]
        out_ref[natural ^ place_ref[0], :, qkv + LANES :] = part[:, qkv:]
    exact = total[tall : tall + 4, :tall] + total[tall + 4 : tall + 8, :tall]
    high = exact.astype(jnp.bfloat16).astype(jnp.float32)
    parts = jnp.concatenate([high, exact - high], axis=0)
    parts = jnp.concatenate([parts[:, :LANES], parts[:, LANES:]], axis=0).astype(jnp.bfloat16)
    for far in range(depth):
        out_ref[far, :16, qkv : qkv + LANES] = parts
        out_ref[far, 16:, qkv : qkv + LANES] = jnp.zeros((share - 16, LANES), jnp.bfloat16)


def collect(place, parts, depth):
    rows, wide = parts[0].shape
    shape = (depth, (rows - 16) // depth, wide + LANES)
    return pl.pallas_call(
        collect_kernel,
        in_specs=[pl.BlockSpec(memory_space=pltpu.SMEM)] + [whole(part.shape) for part in parts],
        out_specs=whole(shape),
        out_shape=jax.ShapeDtypeStruct(shape, jnp.bfloat16),
        compiler_params=params(),
        cost_estimate=FREE,
    )(place, *parts)


def divide_kernel(place_ref, *refs):
    parts, (own_ref, sent_ref, own_out, sent_out) = refs[:-4], refs[-4:]
    core = place_ref[0]
    qkv = 3 * LANES
    share = own_ref.shape[1]
    depth = len(parts)
    own_rows = pl.ds(pl.multiple_of(core * share, share), share)
    other_rows = pl.ds(pl.multiple_of((1 - core) * share, share), share)
    for far, part in enumerate(parts):
        own_ref[far] = part[own_rows, : 3 * LANES]
        sent_ref[far] = part[other_rows, : 3 * LANES]
    for rows, ref in ((own_rows, own_out), (other_rows, sent_out)):
        ref[...] = sum(part[rows, qkv + LANES :].astype(jnp.float32) for part in parts)
    vectors = sum(part[0:16, qkv : qkv + LANES].astype(jnp.float32) for part in parts)
    high = vectors.astype(jnp.bfloat16).astype(jnp.float32)
    zero = jnp.zeros((16, LANES), jnp.float32)
    both = jnp.concatenate([high, vectors - high, zero], axis=1).astype(jnp.bfloat16)
    for ref in (own_ref, sent_ref):
        ref[depth, :16, :] = both
        ref[depth, 16:, :] = jnp.zeros((share - 16, 3 * LANES), jnp.bfloat16)


def divide(core, parts):
    share = parts[0].shape[0] // 2
    shapes = [jax.ShapeDtypeStruct((len(parts) + 1, share, 3 * LANES), jnp.bfloat16)] * 2
    shapes += [jax.ShapeDtypeStruct((share, parts[0].shape[1] - 4 * LANES), jnp.float32)] * 2
    return pl.pallas_call(
        divide_kernel,
        in_specs=[pl.BlockSpec(memory_space=pltpu.SMEM)] + [whole(part.shape) for part in parts],
        out_specs=[whole(shape.shape) for shape in shapes],
        out_shape=shapes,
        compiler_params=params(),
        cost_estimate=FREE,
    )(core, *parts)


def finish_kernel(place_ref, qkv_ref, got_qkv_ref, own_out, got_out, grad_ref, vector_ref, out_ref):
    block, core = place_ref[0], place_ref[1]
    half = out_ref.shape[1] // 2
    out_ref[:, pl.ds(pl.multiple_of(core * half, half), half)] = own_out[...]
    out_ref[:, pl.ds(pl.multiple_of((1 - core) * half, half), half)] = got_out[...]
    depth = qkv_ref.shape[0] - 1
    for near, qkv in enumerate((qkv_ref, got_qkv_ref)):
        for far in range(depth):
            first = (block ^ (2 * far + near)) * LANES
            for kind in range(3):
                to = pl.ds(pl.multiple_of(kind * D + first, LANES), LANES)
                grad_ref[:, to] = qkv[far, :, kind * LANES : (kind + 1) * LANES].astype(jnp.float32)
    both = qkv_ref[depth, :16, :].astype(jnp.float32) + got_qkv_ref[depth, :16, :].astype(jnp.float32)
    exact = both[:, :LANES] + both[:, LANES : 2 * LANES]
    vector_ref[:, :LANES] = exact[0:4] + exact[4:8]
    vector_ref[:, LANES:] = exact[8:12] + exact[12:16]


def finish(place, qkv, got_qkv, own_out, got_out):
    share = qkv.shape[1]
    shapes = [(share, 3 * D), (4, 2 * LANES), (share, D)]
    arrays = (qkv, got_qkv, own_out, got_out)
    return pl.pallas_call(
        finish_kernel,
        in_specs=[pl.BlockSpec(memory_space=pltpu.SMEM)] + [whole(array.shape) for array in arrays],
        out_specs=[whole(shape) for shape in shapes],
        out_shape=[jax.ShapeDtypeStruct(shape, jnp.float32) for shape in shapes],
        compiler_params=params(),
        cost_estimate=FREE,
    )(place, *arrays)


def finish_up_kernel(place_ref, *refs):
    owns, gots, up_ref = refs[:4], refs[4:8], refs[8]
    plane, core = place_ref[0], place_ref[1]
    depth = owns[0].shape[1] // LANES
    for near, parts in enumerate((owns, gots)):
        side = core ^ near
        for far, part in enumerate(parts):
            for chip in range(depth):
                to = pl.ds(pl.multiple_of((((plane ^ far) * depth + chip) * 2 + side) * LANES, LANES), LANES)
                up_ref[:, to] = part[:, chip * LANES : (chip + 1) * LANES].astype(jnp.float32)


def finish_up(place, owns, gots):
    shape = (owns[0].shape[0], 4 * D)
    return pl.pallas_call(
        finish_up_kernel,
        in_specs=[pl.BlockSpec(memory_space=pltpu.SMEM)] + [whole(part.shape) for part in (*owns, *gots)],
        out_specs=whole(shape),
        out_shape=jax.ShapeDtypeStruct(shape, jnp.float32),
        compiler_params=params(),
        cost_estimate=FREE,
    )(place, *owns, *gots)


def turned(values):
    return values.astype(jnp.float32).T.astype(jnp.bfloat16)


def out_grads_kernel(place_ref, heads_ref, cols_ref, *refs):
    outs, heads_t = refs[:4], refs[4]
    plane, own_block = place_ref[0], place_ref[1]
    depth = D // (2 * LANES)
    for far in range(2 * depth):
        core, near = far // depth, far % depth
        row = pl.multiple_of((own_block ^ (2 * near + core)) * LANES, LANES)
        heads_t[pl.ds(row, LANES), :] = turned(heads_ref[:, far * LANES : (far + 1) * LANES])
    tall = D // 4
    for far, out in enumerate(outs):
        row = pl.multiple_of((plane ^ far) * tall, tall)
        left = heads_t[pl.ds(row, tall), :]
        out[:tall, :] = jnp.dot(left, cols_ref[...], preferred_element_type=jnp.float32).astype(jnp.bfloat16)
        out[tall:, :] = jnp.zeros((out.shape[0] - tall, out.shape[1]), jnp.bfloat16)


def out_grads(place, heads, hidden_both):
    rows = heads.shape[0]
    low = jnp.bfloat16

    def full(shape):
        return pl.BlockSpec(shape, lambda i, place: (0,) * len(shape))

    shape = (D // 4 + 16, D // 2)
    grid_spec = pltpu.PrefetchScalarGridSpec(
        num_scalar_prefetch=1,
        grid=(1,),
        in_specs=[full((rows, D)), pl.BlockSpec((rows, D // 2), lambda i, place: (0, place[2]))],
        out_specs=[full(shape)] * 4,
        scratch_shapes=[pltpu.VMEM((D, rows), low)],
    )
    return pl.pallas_call(
        out_grads_kernel,
        grid_spec=grid_spec,
        out_shape=[jax.ShapeDtypeStruct(shape, low)] * 4,
        compiler_params=params(),
        cost_estimate=FREE,
    )(place, heads, hidden_both)


def back_project_kernel(own_ref, other_ref, own_weights, other_weights, keep_ref, *outs):
    for far in range(own_ref.shape[0]):
        total = jnp.dot(own_ref[far], own_weights[...], preferred_element_type=jnp.float32)
        total += jnp.dot(other_ref[far], other_weights[...], preferred_element_type=jnp.float32)
        if far == 0:
            keep_ref[...] = total
        else:
            outs[far - 1][...] = total.astype(jnp.bfloat16)


def back_project(own, other, own_weights, other_weights):
    count, rows, _ = own.shape
    arrays = (own, other, own_weights, other_weights)
    return pl.pallas_call(
        back_project_kernel,
        in_specs=[whole(array.shape) for array in arrays],
        out_specs=[whole((rows, D))] * count,
        out_shape=[jax.ShapeDtypeStruct((rows, D), jnp.float32)]
        + [jax.ShapeDtypeStruct((rows, D), jnp.bfloat16)] * (count - 1),
        compiler_params=params(),
        cost_estimate=FREE,
    )(*arrays)


def qkv_grad_kernel(place_ref, nm_ref, turned_ref, gains_ref, two_ref, *refs):
    deltas, outs, (total, sums) = refs[:-6], refs[-6:-2], refs[-2:]
    count, rows, _ = deltas[0].shape
    ones = jnp.ones((rows, LANES), jnp.bfloat16)
    for index in range(2 * count):
        delta = deltas[index % 2][index // 2]
        part = outer(delta, nm_ref[index * rows : (index + 1) * rows, :])
        column = outer(delta, ones)
        if index == 0:
            total[...] = part
            sums[...] = column
        else:
            total[...] += part
            sums[...] += column
    gain, bias = gains_ref[0:1, :], gains_ref[1:2, :]
    weights = turned_ref[...].astype(jnp.float32)
    column = sums[:, 0:1]
    bias_part = jnp.sum(weights * column, axis=0, keepdims=True)
    gain_part = (jnp.sum(weights * total[...], axis=0, keepdims=True) - bias * bias_part) / gain
    exact = jnp.concatenate([gain_part, bias_part, two_ref[0:2, :]], axis=0)
    high = exact.astype(jnp.bfloat16).astype(jnp.float32)
    parts = jnp.concatenate([high, exact - high, jnp.zeros((8, D), jnp.float32)], axis=0)
    total_parts = parts.astype(jnp.bfloat16)
    tall = D // 4
    for natural in range(4):
        for far in range(4):

            @pl.when((place_ref[0] ^ far) == natural)
            def _():
                cols = slice(natural * tall, (natural + 1) * tall)
                outs[far][:tall, :] = total[:, cols].T.astype(jnp.bfloat16)
                outs[far][tall:, :tall] = total_parts[:, cols]
                outs[far][tall:, tall:] = jnp.zeros((16, 3 * LANES - tall), jnp.bfloat16)


def qkv_gradient(place, deltas, normed, turned_weights, gains, two):
    shape = (D // 4 + 16, 3 * LANES)
    arrays = (normed, turned_weights, gains, two, *deltas)
    return pl.pallas_call(
        qkv_grad_kernel,
        in_specs=[pl.BlockSpec(memory_space=pltpu.SMEM)] + [whole(array.shape) for array in arrays],
        out_specs=[whole(shape)] * 4,
        out_shape=[jax.ShapeDtypeStruct(shape, jnp.bfloat16)] * 4,
        scratch_shapes=[pltpu.VMEM((3 * LANES, D), jnp.float32), pltpu.VMEM((3 * LANES, LANES), jnp.float32)],
        compiler_params=params(),
        cost_estimate=FREE,
    )(place, *arrays)


def moments(values):
    centred = values - jnp.mean(values, axis=1, keepdims=True)
    scale = lax.rsqrt(jnp.mean(centred * centred, axis=1, keepdims=True) + EPSILON)
    return centred * scale, scale


def norm_back(delta, gain, normal, scale):
    e = delta * gain
    return scale * (
        e - jnp.mean(e, axis=1, keepdims=True) - normal * jnp.mean(e * normal, axis=1, keepdims=True)
    )


def added(keep, got):
    return (keep.astype(jnp.float32) + got.astype(jnp.float32)).astype(jnp.bfloat16)


def on_planes(
    tokens_in,
    out_grad,
    w_qkv,
    w_out,
    w_up,
    w_down,
    norm1_gain,
    norm1_bias,
    norm2_gain,
    norm2_bias,
):
    depth = lax.axis_size("z")
    blocks = 2 * depth
    chips = 4 * depth
    rows = tokens_in.shape[0]
    share = w_qkv.shape[0]
    low = jnp.bfloat16
    places = {axis: lax.axis_index(axis) for axis in ALL}
    core = places["c"]
    block = 2 * places["z"] + core
    device = ((2 * places["y"] + places["x"]) * depth + places["z"]) * 2 + core

    hold = lax.optimization_barrier
    plane = 2 * places["y"] + places["x"]
    chip = plane * depth + places["z"]

    def index_of(*values):
        return jnp.stack(values).astype(jnp.int32)

    def along_z(part, far):
        return swap(part, "z", depth, far)

    def middle_z(part):
        return lax.ppermute(part, "z", [(1, 2), (2, 1)])

    def over_plane(part, far):
        return swap(part, ("y", "x"), 4, far)

    gains = jnp.concatenate([norm1_gain, norm1_bias, norm2_gain, norm2_bias]).reshape(1, LANES)
    keep, send = prepare(core.reshape(1), w_qkv, w_up, w_out, gains)
    ups, parts = compose(index_of(places["z"], plane), keep, pair(send), depth)

    along = [parts[0]] + [along_z(parts[far], far) for far in range(1, depth)]
    ups = [ups[0]] + [over_plane(ups[far], far) for far in range(1, 4)]
    along, ups, sent_tokens = hold((along, ups, tokens_in))

    along, ups = jnp.stack(along), jnp.stack(ups)
    tokens_two, tokens_one = along_z(sent_tokens, 2), along_z(sent_tokens, 1)
    across = [along] + [over_plane(along, far) for far in range(1, 4)]
    tokens_two, sent_tokens = hold((tokens_two, sent_tokens))
    middle, ends = middle_z(sent_tokens), lax.ppermute(tokens_two, "z", [(1, 0), (2, 3)])
    across, sent_grad = hold((across, out_grad))
    grads = [out_grad] + [over_plane(sent_grad, far) for far in (1, 2)]
    half_out = assemble(device, across, D // 2)
    other_out = pair(half_out)
    group = [part for mine in (tokens_in, tokens_one, tokens_two, middle, ends) for part in (mine, pair(mine))]
    group, across, grads, half_out, other_out, sent_ups, sent_grad = hold(
        (group, across, grads, half_out, other_out, ups, sent_grad)
    )

    qkv, normed, gains, turned_qkv = project(device, group, across)
    gain_one, bias_one, gain_two, bias_two = (gains[i : i + 1] for i in range(4))
    ups = [ups] + [along_z(sent_ups, far) for far in range(1, depth)]
    grads.append(over_plane(sent_grad, 3))
    attended_low, attended, recip, probs = attend(qkv)
    attended_low, ups, grads = hold((attended_low, ups, grads))

    both = 2 * rows
    sides = [attended_low[:both]] + [
        along_z(attended_low[far * both : (far + 1) * both], far) for far in range(1, depth)
    ]
    near_out = arrange(index_of(block, core), half_out, other_out)
    own_out = near_out[:depth].reshape(depth * LANES, D)
    sides, near_out, ups, sent_down = hold((sides, near_out, ups, w_down))
    own_heads = jnp.concatenate(sides, axis=1)
    other_heads = pair(own_heads)
    other_heads = jnp.concatenate([other_heads[rows:], other_heads[:rows]])
    all_heads = jnp.concatenate([own_heads, other_heads], axis=1)
    inputs = tokens_in.astype(jnp.float32)
    hidden = inputs + jnp.dot(
        all_heads[:rows], near_out.reshape(D, D), preferred_element_type=jnp.float32
    )
    normal_two, scale_two = moments(hidden)
    normed_two = (normal_two * gain_two + bias_two).astype(low)
    normed_two, sent_down = hold((normed_two, sent_down))

    plane_normed = [normed_two] + [over_plane(normed_two, far) for far in range(1, 4)]
    downs = [w_down] + [along_z(sent_down, far) for far in range(1, depth)]
    other_ups, other_downs = [pair(part) for part in ups], [pair(part) for part in downs]
    plane_normed, downs, other_ups, other_downs = hold((plane_normed, downs, other_ups, other_downs))
    active, up_delta, two_delta, *part, own_down = mlp(
        index_of(device, places["z"]), plane_normed, grads, ups, other_ups, downs, other_downs
    )

    two_sides = [over_plane(part[far - 1], far) for far in range(1, 4)]
    out_own, *out_parts, up_term, up_send, down_term, down_send = mlp_grads(
        index_of(places["z"]), plane_normed, grads, active, up_delta, own_down, depth
    )
    other_turned = pair(turned_qkv)
    two_sides, out_parts, up_term, up_send, down_term, down_send, other_turned = hold(
        (two_sides, out_parts, up_term, up_send, down_term, down_send, other_turned)
    )
    for side in two_sides:
        two_delta = two_delta + side.astype(jnp.float32)
    two_sums = jnp.stack([jnp.sum(two_delta * normal_two, axis=0), jnp.sum(two_delta, axis=0)])
    hidden_delta = out_grad.astype(jnp.float32) + norm_back(two_delta, gain_two, normal_two, scale_two)
    hidden_low = hidden_delta.astype(low)
    hidden_both = jnp.concatenate([hidden_low, pair(hidden_low)])
    att_delta = against(hidden_both, own_out).astype(low)
    att_delta, up_send, down_send = hold((att_delta, up_send, down_send))
    far_delta = [att_delta[:, :LANES]] + [
        along_z(att_delta[:, far * LANES : (far + 1) * LANES], far) for far in range(1, depth)
    ]
    up_got, down_got = pair(up_send), pair(down_send)
    out_terms = out_grads(index_of(plane, block, core), all_heads, hidden_both)
    up_term = [added(up_term[far], up_got[far]) for far in range(depth)]
    down_term = [added(down_term[far], down_got[far]) for far in range(depth)]
    far_delta, out_terms, up_term, down_term = hold((far_delta, out_terms, up_term, down_term))

    deltas = attend_back(qkv, probs, far_delta, attended, recip)
    up_sides = [up_term[0]] + [along_z(up_term[far], far) for far in range(1, depth)]
    deltas, up_sides, down_term = hold((deltas, up_sides, down_term))

    got = pair(deltas[1])
    down_sides = [down_term[0]] + [along_z(down_term[far], far) for far in range(1, depth)]
    out_sides = [over_plane(out_parts[far - 1], far) for far in (1, 2)]
    one_delta, *part = back_project(deltas[0], got, turned_qkv, other_turned)
    qkv_terms = qkv_gradient(index_of(plane), deltas, normed, turned_qkv, gains, two_sums)
    terms = [jnp.concatenate(pieces, axis=1) for pieces in zip(qkv_terms, out_terms)]
    part, terms, up_sides, down_sides, out_sides, out_last = hold(
        (part, terms, up_sides, down_sides, out_sides, out_parts[2])
    )

    ends, middle = lax.ppermute(part[2], "z", [(0, 1), (3, 2)]), middle_z(part[2])
    out_sides.append(over_plane(out_last, 3))
    down_sum = sum(side.astype(jnp.float32) for side in down_sides)
    ends, middle, out_sides, down_sum, terms, up_sides = hold((ends, middle, out_sides, down_sum, terms, up_sides))

    one_sides = [along_z(added(part[1], ends), 2), along_z(part[0], 1), middle]
    terms = [terms[0]] + [over_plane(terms[far], far) for far in range(1, 4)]
    qkv_part = collect(index_of(places["z"]), terms, depth)
    up_sum = sum(side.astype(jnp.float32) for side in up_sides).astype(low)
    out_sum = hidden + out_own
    for side in out_sides:
        out_sum = out_sum + side.astype(jnp.float32)
    result = out_sum.astype(low)
    one_sides, qkv_part, result, up_sum = hold((one_sides, qkv_part, result, up_sum))

    qkv_sides = [qkv_part[0]] + [along_z(qkv_part[far], far) for far in range(1, depth)]
    up_parts = [lax.dynamic_index_in_dim(up_sum, plane, 0, keepdims=False)] + [
        over_plane(lax.dynamic_index_in_dim(up_sum, plane ^ far, 0, keepdims=False), far) for far in range(1, 4)
    ]
    own_parts = [lax.dynamic_slice_in_dim(part, core * share, share, 0) for part in up_parts]
    other_parts = [lax.dynamic_slice_in_dim(part, (1 - core) * share, share, 0) for part in up_parts]
    got_parts = pair(jnp.concatenate(other_parts, axis=1))
    wide = D // 2
    got_parts = [got_parts[:, at * wide : (at + 1) * wide] for at in range(4)]
    up_grad = finish_up(index_of(plane, core), own_parts, got_parts)
    one_delta = sum((side.astype(jnp.float32) for side in one_sides), one_delta)
    normal_one, scale_one = moments(inputs)
    input_grad = hidden_delta + norm_back(one_delta, gain_one, normal_one, scale_one)
    own_qkv, sent_qkv, own_out, sent_out = divide(index_of(core), qkv_sides)
    qkv_grad, vectors, out_weight_grad = finish(
        index_of(block, core), own_qkv, pair(sent_qkv), own_out, pair(sent_out)
    )
    vectors = lax.dynamic_slice_in_dim(vectors, (places["z"] * 2 + core) * share, share, 1)
    return (
        result,
        input_grad,
        qkv_grad,
        out_weight_grad,
        up_grad,
        down_sum,
        vectors[0],
        vectors[1],
        vectors[2],
        vectors[3],
    )


def solution(mesh):
    scenes, blocks = mesh.devices.shape

    def place(axes):
        matrix = P(axes, None)
        views = P(axes[: len(axes) // 2] if len(axes) > 2 else axes[0], None)
        vector = P(axes)
        ins = (matrix, views, views, views, matrix, matrix, matrix, matrix, matrix) + (vector,) * 4
        return ins, (matrix,) * 6 + (vector,) * 4

    def run(*arrays):
        one_scene = arrays[1].shape[1] == 4
        if scenes == 4 and blocks == 8 and one_scene and arrays[0].shape[0] == 8192:
            fine = Mesh(mesh.devices.reshape(2, 2, blocks // 2, 2), ALL)
            ins, outs = place(ALL)
            step = lambda tokens, heights, widths, labels, *rest: on_planes(tokens, *rest)
            return jax.shard_map(step, mesh=fine, in_specs=ins, out_specs=outs, check_vma=False)(*arrays)
        ins, outs = place(("scene", "blk"))
        return jax.shard_map(on_any_slice, mesh=mesh, in_specs=ins, out_specs=outs, check_vma=False)(*arrays)

    return run
```

```python
import functools
import math

import jax
import jax.numpy as jnp
from jax import lax
from jax.experimental import pallas as pl
from jax.experimental.pallas import tpu as pltpu
from jax.sharding import Mesh
from jax.sharding import PartitionSpec as P

D = 1024
HEADS = 16
HEAD_DIM = 64


EPSILON = 1e-05
MASKED = -1e30


def layer_norm(values, gain_row, bias_row):
    centred = values - jnp.mean(values, axis=1, keepdims=True)
    scaled = centred * lax.rsqrt(jnp.mean(centred * centred, axis=1, keepdims=True) + EPSILON)
    return scaled * gain_row + bias_row


def scene_rows(view_ends, labels, first_row, count_rows):
    places = first_row + jnp.arange(count_rows, dtype=jnp.int32)
    view_index = jnp.sum((places[:, None] >= view_ends[None, :]).astype(jnp.int32), axis=1)
    matches = view_index[:, None] == jnp.arange(labels.shape[0], dtype=jnp.int32)[None, :]
    return jnp.sum(jnp.where(matches, labels[None, :], 0), axis=1)


def in_blocks(update, carry, members):
    total_rows = members[0].shape[0]
    width_rows = math.gcd(total_rows, 1024)
    block_count = total_rows // width_rows
    stacked = tuple(
        (member.reshape((block_count, width_rows) + member.shape[1:]) for member in members)
    )

    def advance(state_now, indexed):
        block_index, block_parts = indexed
        return (update(state_now, block_parts, block_index * width_rows), None)

    carry, _ = lax.scan(advance, carry, (jnp.arange(block_count, dtype=jnp.int32), stacked))
    return carry


def heads_of(rows):
    return rows.reshape(rows.shape[0], HEADS, HEAD_DIM)


def pair_terms(
    query_heads, delta_heads, log_rows, probe_rows, allowed, key_heads, value_heads, score_scale
):
    raw = (
        jnp.einsum("qhe,khe->hqk", query_heads, key_heads, preferred_element_type=jnp.float32)
        * score_scale
    )
    weights_now = jnp.where(allowed, jnp.exp(raw - log_rows[:, :, None]), 0.0)
    backward = jnp.einsum(
        "qhe,khe->hqk", delta_heads, value_heads, preferred_element_type=jnp.float32
    )
    score_delta = (weights_now * (backward - probe_rows[:, :, None])).astype(jnp.bfloat16)
    return (weights_now.astype(jnp.bfloat16), score_delta)


def outer(left, right):
    return lax.dot_general(
        left, right, (((0,), (0,)), ((), ())), preferred_element_type=jnp.float32
    )


def against(left, right):
    return lax.dot_general(
        left, right, (((1,), (1,)), ((), ())), preferred_element_type=jnp.float32
    )


def on_any_slice(
    tokens_in,
    view_heights,
    view_widths,
    view_scenes,
    out_grad,
    w_qkv,
    w_out,
    w_up,
    w_down,
    norm1_gain,
    norm1_bias,
    norm2_gain,
    norm2_bias,
):
    gathered = (
        lax.all_gather(w_qkv, ("scene", "blk"), axis=0, tiled=True),
        lax.all_gather(w_out, ("scene", "blk"), axis=0, tiled=True),
        lax.all_gather(w_up, ("scene", "blk"), axis=0, tiled=True),
        lax.all_gather(w_down, ("scene", "blk"), axis=0, tiled=True),
        lax.all_gather(norm1_gain, ("scene", "blk"), axis=0, tiled=True),
        lax.all_gather(norm1_bias, ("scene", "blk"), axis=0, tiled=True),
        lax.all_gather(norm2_gain, ("scene", "blk"), axis=0, tiled=True),
        lax.all_gather(norm2_bias, ("scene", "blk"), axis=0, tiled=True),
    )
    full_qkv, full_out, full_up, full_down = (gathered[0], gathered[1], gathered[2], gathered[3])
    gain_one = gathered[4].astype(jnp.float32)
    bias_one = gathered[5].astype(jnp.float32)
    gain_two = gathered[6].astype(jnp.float32)
    bias_two = gathered[7].astype(jnp.float32)
    local_rows = tokens_in.shape[0]
    view_ends = jnp.cumsum(view_heights[0] * view_widths[0])
    labels = view_scenes[0]
    own_first = lax.axis_index("blk") * local_rows
    own_scene = scene_rows(view_ends, labels, own_first, local_rows)
    score_scale = HEAD_DIM ** (-0.5)
    inputs = tokens_in.astype(jnp.float32)
    normed, norm_one_pull = jax.vjp(layer_norm, inputs, gain_one, bias_one)
    normed_low = normed.astype(jnp.bfloat16)
    projected = jnp.dot(normed_low, full_qkv, preferred_element_type=jnp.float32).astype(
        jnp.bfloat16
    )
    query_rows = projected[:, :D]
    key_rows = projected[:, D : 2 * D]
    value_rows = projected[:, 2 * D :]
    query_heads = heads_of(query_rows)

    def forward_update(state_now, members, first_row):
        run_max, run_sum, run_total = state_now
        piece_keys, piece_values = members
        piece_rows = piece_keys.shape[0]
        key_scene = scene_rows(view_ends, labels, first_row, piece_rows)
        allowed = (own_scene[:, None] == key_scene[None, :])[None]
        raw = (
            jnp.einsum(
                "qhe,khe->hqk",
                query_heads,
                heads_of(piece_keys),
                preferred_element_type=jnp.float32,
            )
            * score_scale
        )
        new_max = jnp.maximum(run_max, jnp.max(jnp.where(allowed, raw, MASKED), axis=2))
        expo = jnp.where(allowed, jnp.exp(raw - new_max[:, :, None]), 0.0)
        factor = jnp.exp(run_max - new_max)
        run_sum = run_sum * factor + jnp.sum(expo, axis=2)
        mixed = jnp.einsum(
            "hqk,khe->qhe",
            expo.astype(jnp.bfloat16),
            heads_of(piece_values),
            preferred_element_type=jnp.float32,
        )
        run_total = run_total * jnp.transpose(factor)[:, :, None] + mixed
        return (new_max, run_sum, run_total)

    start_state = (
        jnp.full((HEADS, local_rows), MASKED, jnp.float32),
        jnp.zeros((HEADS, local_rows), jnp.float32),
        jnp.zeros((local_rows, HEADS, HEAD_DIM), jnp.float32),
    )
    run_max, run_sum, run_total = in_blocks(
        forward_update,
        start_state,
        (
            lax.all_gather(key_rows, "blk", axis=0, tiled=True),
            lax.all_gather(value_rows, "blk", axis=0, tiled=True),
        ),
    )
    log_total = run_max + jnp.log(run_sum)
    attended_heads = run_total / jnp.transpose(run_sum)[:, :, None]
    attended_low = attended_heads.reshape(local_rows, D).astype(jnp.bfloat16)
    hidden = inputs + jnp.dot(attended_low, full_out, preferred_element_type=jnp.float32)
    normed_two, norm_two_pull = jax.vjp(layer_norm, hidden, gain_two, bias_two)
    normed_two_low = normed_two.astype(jnp.bfloat16)
    upward = jnp.dot(normed_two_low, full_up, preferred_element_type=jnp.float32)
    active, gelu_pull = jax.vjp(jax.nn.gelu, upward)
    active_low = active.astype(jnp.bfloat16)
    result = (hidden + jnp.dot(active_low, full_down, preferred_element_type=jnp.float32)).astype(
        jnp.bfloat16
    )
    down_term = outer(active_low, out_grad)
    up_delta = gelu_pull(against(out_grad, full_down))[0].astype(jnp.bfloat16)
    up_term = outer(normed_two_low, up_delta)
    hidden_back, gain_two_term, bias_two_term = norm_two_pull(against(up_delta, full_up))
    hidden_delta = out_grad.astype(jnp.float32) + hidden_back
    hidden_low = hidden_delta.astype(jnp.bfloat16)
    out_term = outer(attended_low, hidden_low)
    att_delta = against(hidden_low, full_out).astype(jnp.bfloat16)
    delta_heads = heads_of(att_delta)
    row_probe = jnp.transpose(jnp.sum(delta_heads.astype(jnp.float32) * attended_heads, axis=2))
    query_start = jnp.zeros((local_rows, HEADS, HEAD_DIM), jnp.float32)
    every_key, every_value = (
        lax.all_gather(key_rows, "blk", axis=0, tiled=True),
        lax.all_gather(value_rows, "blk", axis=0, tiled=True),
    )
    group_rows = every_key.shape[0]
    width_rows = math.gcd(group_rows, 1024)
    block_count = group_rows // width_rows

    def joint_step(total, indexed):
        block_index, block_keys, block_values = indexed
        block_first = block_index * width_rows
        key_heads = heads_of(block_keys)
        value_heads = heads_of(block_values)
        key_scene = scene_rows(view_ends, labels, block_first, width_rows)
        allowed = (own_scene[:, None] == key_scene[None, :])[None]
        weights_low, score_delta = pair_terms(
            query_heads,
            delta_heads,
            log_total,
            row_probe,
            allowed,
            key_heads,
            value_heads,
            score_scale,
        )
        total = (
            total
            + jnp.einsum("hqk,khe->qhe", score_delta, key_heads, preferred_element_type=jnp.float32)
            * score_scale
        )
        value_part = jnp.einsum(
            "hqk,qhe->khe", weights_low, delta_heads, preferred_element_type=jnp.float32
        )
        key_part = (
            jnp.einsum("hqk,qhe->khe", score_delta, query_heads, preferred_element_type=jnp.float32)
            * score_scale
        )
        rows_out = jnp.concatenate(
            [key_part.reshape(width_rows, D), value_part.reshape(width_rows, D)], axis=1
        )
        return (total, rows_out)

    query_total, pair_rows = lax.scan(
        joint_step,
        query_start,
        (
            jnp.arange(block_count, dtype=jnp.int32),
            every_key.reshape(block_count, width_rows, D),
            every_value.reshape(block_count, width_rows, D),
        ),
    )
    pair_rows = pair_rows.reshape(group_rows, 2 * D)
    both_sums = lax.psum_scatter(
        pair_rows.astype(jnp.bfloat16), "blk", scatter_dimension=0, tiled=True
    ).astype(jnp.float32)
    key_total = both_sums[:, :D]
    value_total = both_sums[:, D:]
    qkv_delta = jnp.concatenate(
        [query_total.reshape(local_rows, D), key_total, value_total], axis=1
    ).astype(jnp.bfloat16)
    qkv_term = outer(normed_low, qkv_delta)
    input_back, gain_one_term, bias_one_term = norm_one_pull(against(qkv_delta, full_qkv))
    input_grad = hidden_delta + input_back
    summed = (
        lax.psum_scatter(qkv_term, ("scene", "blk"), scatter_dimension=0, tiled=True),
        lax.psum_scatter(out_term, ("scene", "blk"), scatter_dimension=0, tiled=True),
        lax.psum_scatter(up_term, ("scene", "blk"), scatter_dimension=0, tiled=True),
        lax.psum_scatter(down_term, ("scene", "blk"), scatter_dimension=0, tiled=True),
        lax.psum_scatter(gain_one_term, ("scene", "blk"), scatter_dimension=0, tiled=True),
        lax.psum_scatter(bias_one_term, ("scene", "blk"), scatter_dimension=0, tiled=True),
        lax.psum_scatter(gain_two_term, ("scene", "blk"), scatter_dimension=0, tiled=True),
        lax.psum_scatter(bias_two_term, ("scene", "blk"), scatter_dimension=0, tiled=True),
    )
    return (
        result,
        input_grad,
        summed[0],
        summed[1],
        summed[2],
        summed[3],
        summed[4],
        summed[5],
        summed[6],
        summed[7],
    )


ALL = ("y", "x", "z", "c")
LANES = 128
BESIDE = {
    "up1": "tokens", "ogd": "tokens", "turned": "delta", "oups0": "units", "oups2": "units", "oups3": "units",
    "dz2": "sums", "dz3": "back", "dz1": "back", "lo1": "middle", "lo2": "middle", "lo3": "last", "upa": "last",
}
ROOT = math.sqrt(2.0 / math.pi)
CUBIC = 0.044715
FREE = pl.CostEstimate(flops=0, bytes_accessed=0, transcendentals=0)


def swap(values, axis, size, distance):
    return lax.ppermute(values, axis, [(i, i ^ distance) for i in range(size)])


def pair(values):
    return swap(values, "c", 2, 1)


def whole(shape):
    return pl.BlockSpec(shape, lambda *_: (0,) * len(shape))


def params(megabytes=60):
    return pltpu.CompilerParams(vmem_limit_bytes=megabytes * 1024 * 1024)


def three_parts(column, lane, first):
    high = column.astype(jnp.bfloat16).astype(jnp.float32)
    rest = column - high
    middle = rest.astype(jnp.bfloat16).astype(jnp.float32)
    last = rest - middle
    zero = jnp.zeros_like(last)
    return jnp.where(
        lane == first,
        high,
        jnp.where(lane == first + 1, middle, jnp.where(lane == first + 2, last, zero)),
    )


def attend_kernel(q_ref, k_ref, v_ref, *refs, chunk):
    low_ref, att_ref, rl_ref, p_ref, s0, s1, m0, m1, vt_ref, hold_ref = refs
    unit = pl.program_id(0)
    last = pl.num_programs(0) - 1
    rows = k_ref.shape[0]
    block = q_ref.shape[0]
    lane = lax.broadcasted_iota(jnp.int32, (1, LANES), 1)
    line = lax.broadcasted_iota(jnp.int32, (LANES, 1), 0)

    @pl.when(unit == 0)
    def _():
        turned = v_ref[...].astype(jnp.float32).T
        vt_ref[0] = jnp.where(line < HEAD_DIM, turned, 1.0).astype(jnp.bfloat16)
        vt_ref[1] = jnp.where(line >= HEAD_DIM, turned, 1.0).astype(jnp.bfloat16)

    def work(head, fresh, scores, old):
        mine = (lane < HEAD_DIM) if head == 0 else (lane >= HEAD_DIM)
        query = jnp.where(mine, q_ref[...].astype(jnp.float32) * HEAD_DIM ** (-0.5), 0.0).astype(jnp.bfloat16)
        top = jnp.full((8, block), -jnp.inf, jnp.float32)
        high = old[0][0:1, :] if old is not None else None
        mixed = jnp.zeros((LANES, block), jnp.float32)
        for first in range(0, rows, chunk):
            part = slice(first, first + chunk)
            if fresh is not None:
                got = against(k_ref[part, :], query)
                scores[part, :] = got
                top = jnp.maximum(top, jnp.max(got.reshape(chunk // 8, 8, block), axis=0))
            if old is not None:
                expo = jnp.exp(old[1][part, :] - high).astype(jnp.bfloat16)
                p_ref[0, part, :] = expo
                mixed += jnp.dot(vt_ref[1 - head, :, part], expo, preferred_element_type=jnp.float32)
        if fresh is not None:
            fresh[...] = jnp.broadcast_to(jnp.max(top, axis=0, keepdims=True), (8, block))
        return mixed.T if old is not None else None

    @pl.when(unit == 0)
    def _():
        work(0, m0, s0, None)

    @pl.when((unit > 0) & (unit % 2 == 1))
    def _():
        hold_ref[...] = work(1, m1, s1, (m0, s0))

    def finish(second):
        first = hold_ref[...]
        low_lane = lane < HEAD_DIM
        recip = 1.0 / jnp.where(low_lane, pltpu.roll(first, HEAD_DIM, 1), pltpu.roll(second, HEAD_DIM, 1))
        attended = jnp.where(low_lane, first, second) * recip
        att_ref[...] = attended
        rl_ref[...] = recip
        low_ref[...] = attended.astype(jnp.bfloat16)

    @pl.when((unit > 0) & (unit % 2 == 0) & (unit < last))
    def _():
        finish(work(0, m0, s0, (m1, s1)))

    @pl.when(unit == last)
    def _():
        finish(work(0, None, None, (m1, s1)))

def attend(qkv):
    rows = qkv.shape[0]
    block, chunk = 512, 256
    units = 2 * rows // block

    def new(u):
        return jnp.minimum(u, units - 1) // 2

    def old(u):
        return jnp.maximum(u - 1, 0)

    part = pl.BlockSpec((block, LANES), lambda u: (old(u) // 2, 0))
    return pl.pallas_call(
        functools.partial(attend_kernel, chunk=chunk),
        grid=(units + 1,),
        in_specs=[
            pl.BlockSpec((block, LANES), lambda u: (new(u), 0)),
            pl.BlockSpec((rows, LANES), lambda u: (0, 1)),
            pl.BlockSpec((rows, LANES), lambda u: (0, 2)),
        ],
        out_specs=[part, part, part, pl.BlockSpec((1, rows, block), lambda u: (old(u) % 2, 0, old(u) // 2))],
        out_shape=[
            jax.ShapeDtypeStruct((rows, LANES), jnp.bfloat16),
            jax.ShapeDtypeStruct((rows, LANES), jnp.float32),
            jax.ShapeDtypeStruct((rows, LANES), jnp.float32),
            jax.ShapeDtypeStruct((2, rows, rows), jnp.bfloat16),
        ],
        scratch_shapes=[pltpu.VMEM((rows, block), jnp.float32)] * 2
        + [pltpu.VMEM((8, block), jnp.float32)] * 2
        + [pltpu.VMEM((2, LANES, rows), jnp.bfloat16), pltpu.VMEM((block, LANES), jnp.float32)],
        compiler_params=params(34),
        cost_estimate=FREE,
    )(qkv, qkv, qkv)


def attend_back_kernel(q_ref, k_ref, v_ref, p_ref, att_ref, rl_ref, *refs, chunk, count):
    deltas, outs = refs[:count], refs[count : count + 2]
    va_ref, kt_ref, dq_acc, dk_acc, dv_acc, do_ref = refs[count + 2 :]
    head, step = pl.program_id(0), pl.program_id(1)
    rows = k_ref.shape[0]
    block = do_ref.shape[0]
    lane = lax.broadcasted_iota(jnp.int32, (1, LANES), 1)
    spare = jnp.where(head == 0, HEAD_DIM, 0)
    mine = (lane < spare) | (lane >= spare + HEAD_DIM)

    @pl.when((head == 0) & (step == 0))
    def _():
        kt_ref[...] = (k_ref[...].astype(jnp.float32) * HEAD_DIM ** (-0.5)).T.astype(jnp.bfloat16)

    @pl.when(step == 0)
    def _():
        ones = jnp.where(lane < spare + 3, 1.0, 0.0)
        va_ref[...] = jnp.where(mine, v_ref[...].astype(jnp.float32), ones).astype(jnp.bfloat16)
        dk_acc[head] = jnp.zeros((rows, LANES), jnp.float32)
        dv_acc[head] = jnp.zeros((rows, LANES), jnp.float32)

    for index, ref in enumerate(deltas):

        @pl.when(step == index)
        def _():
            do_ref[...] = ref[...]

    delta = (do_ref[...].astype(jnp.float32) * rl_ref[...]).astype(jnp.bfloat16).astype(jnp.float32)
    probe = jnp.sum(jnp.where(mine, delta * att_ref[...], 0.0), axis=1, keepdims=True)
    own_delta = jnp.where(mine, delta, three_parts(-probe, lane, spare)).astype(jnp.bfloat16)
    query = (q_ref[...].astype(jnp.float32) * HEAD_DIM ** (-0.5)).astype(jnp.bfloat16)
    total = jnp.zeros((LANES, block), jnp.float32)
    for first in range(0, rows, chunk):
        part = slice(first, first + chunk)
        expo = p_ref[0, part, :]
        score_delta = (expo.astype(jnp.float32) * against(va_ref[part, :], own_delta)).astype(jnp.bfloat16)
        dv_acc[head, part, :] += jnp.dot(expo, own_delta, preferred_element_type=jnp.float32)
        dk_acc[head, part, :] += jnp.dot(score_delta, query, preferred_element_type=jnp.float32)
        total += jnp.dot(kt_ref[:, part], score_delta, preferred_element_type=jnp.float32)
    query_delta = total.T
    place = pl.ds(pl.multiple_of(step * block, block), block)

    @pl.when(head == 0)
    def _():
        dq_acc[place, :] = query_delta

    half = block // 2

    @pl.when(head == 1)
    def _():
        both = jnp.where(lane < HEAD_DIM, dq_acc[place, :], query_delta).astype(jnp.bfloat16)
        for side, ref in enumerate(outs):
            ref[step, :, :LANES] = both[side * half : (side + 1) * half]

    @pl.when((head == 1) & (step == pl.num_programs(1) - 1))
    def _():
        for index in range(count):
            for side, ref in enumerate(outs):
                part = slice(index * block + side * half, index * block + (side + 1) * half)
                for kind, acc in ((1, dk_acc), (2, dv_acc)):
                    own = jnp.where(lane < HEAD_DIM, acc[0, part, :], acc[1, part, :]).astype(jnp.bfloat16)
                    ref[index, :, kind * LANES : (kind + 1) * LANES] = own


def attend_back(qkv, probs, deltas, attended, recip):
    rows = qkv.shape[0]
    count = len(deltas)
    block, chunk = rows // count, 512
    part = pl.BlockSpec((block, LANES), lambda h, i: (i, 0))
    return pl.pallas_call(
        functools.partial(attend_back_kernel, chunk=chunk, count=count),
        grid=(2, count),
        in_specs=[
            part,
            pl.BlockSpec((rows, LANES), lambda h, i: (0, 1)),
            pl.BlockSpec((rows, LANES), lambda h, i: (0, 2)),
            pl.BlockSpec((1, rows, block), lambda h, i: (h, 0, i)),
            part,
            part,
        ]
        + [whole((block, LANES))] * count,
        out_specs=[whole((count, block // 2, 3 * LANES))] * 2,
        out_shape=[jax.ShapeDtypeStruct((count, block // 2, 3 * LANES), jnp.bfloat16)] * 2,
        scratch_shapes=[
            pltpu.VMEM((rows, LANES), jnp.bfloat16),
            pltpu.VMEM((LANES, rows), jnp.bfloat16),
            pltpu.VMEM((rows, LANES), jnp.float32),
            pltpu.VMEM((2, rows, LANES), jnp.float32),
            pltpu.VMEM((2, rows, LANES), jnp.float32),
            pltpu.VMEM((block, LANES), jnp.bfloat16),
        ],
        compiler_params=params(36),
        cost_estimate=FREE,
    )(qkv, qkv, qkv, probs, attended, recip, *deltas)


def qkv_kernel(place_ref, *refs):
    pieces, weights = refs[:10], refs[10:14]
    qkv_ref, normed_ref, gains_ref, turned_ref, own_ref, table_ref = refs[14:]
    depth, share = weights[0].shape[0], weights[0].shape[1] // 2

    @pl.when(pl.program_id(0) == 0)
    def _():
        device = place_ref[0]
        for far, part in enumerate(weights):
            for near in range(depth):
                for core in range(2):
                    owner = device ^ (far * 2 * depth + near * 2 + core)
                    row = pl.multiple_of(owner * share, share)
                    first = core * share
                    own_ref[pl.ds(row, share), :] = part[near, first : first + share, : 3 * LANES]
                    table = part[near, first : first + 16, 3 * LANES :].astype(jnp.float32)
                    table_ref[pl.ds(owner, 1), :] = table[0:1]
        devices = table_ref.shape[0]
        table = table_ref[...].astype(jnp.bfloat16)
        row = lax.broadcasted_iota(jnp.int32, (LANES, D), 0)
        col = lax.broadcasted_iota(jnp.int32, (LANES, D), 1)
        owner = lax.broadcasted_iota(jnp.int32, (devices, D), 0)
        own_col = lax.broadcasted_iota(jnp.int32, (devices, D), 1) // share
        for kind in range(4):
            spread = jnp.where(row == kind * share + col % share, 1.0, 0.0).astype(jnp.bfloat16)
            wide = jnp.dot(table, spread, preferred_element_type=jnp.float32)
            gains_ref[kind : kind + 1, :] = jnp.sum(jnp.where(owner == own_col, wide, 0.0), axis=0, keepdims=True)
        gains_ref[4:8, :] = jnp.zeros((4, D), jnp.float32)
        turned_ref[...] = own_ref[...].astype(jnp.float32).T.astype(jnp.bfloat16)

    gain, bias = gains_ref[0:1, :], gains_ref[1:2, :]
    for index in range(8):
        tokens = pieces[index][...].astype(jnp.float32)
        if index >= 6:
            tokens = tokens + pieces[index + 2][...].astype(jnp.float32)
        normal, _ = moments(tokens)
        normed = (normal * gain + bias).astype(jnp.bfloat16)
        normed_ref[index] = normed
        qkv_ref[index] = jnp.dot(normed, own_ref[...], preferred_element_type=jnp.float32).astype(jnp.bfloat16)


def project(device, pieces, weights):
    rows = pieces[0].shape[0]
    steps = 2
    block = rows // steps
    piece = pl.BlockSpec((block, D), lambda i, place: (i, 0))
    part = pl.BlockSpec(weights[0].shape, lambda i, place: (0, 0, 0))
    grid_spec = pltpu.PrefetchScalarGridSpec(
        num_scalar_prefetch=1,
        grid=(steps,),
        in_specs=[piece] * 10 + [part] * 4,
        out_specs=[
            pl.BlockSpec((8, block, 3 * LANES), lambda i, place: (0, i, 0)),
            pl.BlockSpec((8, block, D), lambda i, place: (0, i, 0)),
            pl.BlockSpec((8, D), lambda i, place: (0, 0)),
            pl.BlockSpec((3 * LANES, D), lambda i, place: (0, 0)),
        ],
        scratch_shapes=[
            pltpu.VMEM((D, 3 * LANES), jnp.bfloat16),
            pltpu.VMEM((32, LANES), jnp.float32),
        ],
    )
    qkv, normed, gains, turned = pl.pallas_call(
        qkv_kernel,
        grid_spec=grid_spec,
        out_shape=[
            jax.ShapeDtypeStruct((8, rows, 3 * LANES), jnp.bfloat16),
            jax.ShapeDtypeStruct((8, rows, D), jnp.bfloat16),
            jax.ShapeDtypeStruct((8, D), jnp.float32),
            jax.ShapeDtypeStruct((3 * LANES, D), jnp.bfloat16),
        ],
        compiler_params=params(60),
        cost_estimate=FREE,
    )(device.reshape(1).astype(jnp.int32), *pieces, *weights)
    return qkv.reshape(8 * rows, 3 * LANES), normed.reshape(8 * rows, D), gains, turned


def mlp_kernel(place_ref, *refs):
    device, own_z = place_ref[0], place_ref[1]
    nts, ogs, refs = refs[:4], refs[4:8], refs[8:]
    ups, other_ups, downs, other_downs = refs[:4], refs[4:8], refs[8:12], refs[12:16]
    act_ref, ud_ref, keep_ref, one_ref, two_ref, three_ref, down_ref, down_keep, down_send, up_ref, down_acc = refs[16:]
    depth, share, wide = len(ups), ups[0].shape[1] // 2, ups[0].shape[2]

    @pl.when(pl.program_id(0) == 0)
    def _():
        slab = downs[0].shape[0]
        for side, parts in enumerate((ups, other_ups)):
            for near, part in enumerate(parts):
                for far in range(part.shape[0]):
                    for core in range(2):
                        owner = far * 2 * depth + ((device % (2 * depth)) ^ (near * 2 + (core ^ side)))
                        row = pl.multiple_of(owner * share, share)
                        cols = slice(side * wide, (side + 1) * wide)
                        up_ref[pl.ds(row, share), cols] = part[far, core * share : (core + 1) * share, :]
        for side, parts in enumerate((downs, other_downs)):
            for near, part in enumerate(parts):
                row = pl.multiple_of(side * wide + (own_z ^ near) * slab, slab)
                down_ref[pl.ds(row, slab), :] = part[...]

    rows = nts[0].shape[0]
    normed = jnp.concatenate([ref[...] for ref in nts])
    grads = jnp.concatenate([ref[...] for ref in ogs])
    back = jnp.zeros((4 * rows, D), jnp.float32)
    for side in range(2):
        cols = slice(side * wide, (side + 1) * wide)
        upward = jnp.dot(normed, up_ref[:, cols], preferred_element_type=jnp.float32)
        square = upward * upward
        curve = jnp.tanh(ROOT * upward * (1.0 + CUBIC * square))
        active = (0.5 * upward * (1.0 + curve)).astype(jnp.bfloat16)
        slope = 0.5 * (1.0 + curve) + 0.5 * upward * (1.0 - curve * curve) * (ROOT * (1.0 + 3.0 * CUBIC * square))
        delta = (against(grads, down_ref[cols, :]) * slope).astype(jnp.bfloat16)
        back += against(delta, up_ref[:, cols])
        down_acc[cols, :] = outer(active, grads)
        for index in range(4):
            part = slice(index * rows, (index + 1) * rows)
            act_ref[index, :, cols] = active[part]
            ud_ref[index, :, cols] = delta[part]
    keep_ref[...] = back[:rows]
    for index, to in enumerate((one_ref, two_ref, three_ref)):
        to[...] = back[(index + 1) * rows : (index + 2) * rows].astype(jnp.bfloat16)

    slab = down_keep.shape[1]
    for side, to in enumerate((down_keep, down_send)):
        for near in range(depth):
            first = side * wide + near * slab
            to[near ^ own_z] = down_acc[first : first + slab, :].astype(jnp.bfloat16)


def mlp(place, normed, grads, ups, other_ups, downs, other_downs):
    rows = normed[0].shape[0]
    steps = 1
    block = rows // steps
    wide = 2 * ups[0].shape[2]
    low = jnp.bfloat16
    piece = pl.BlockSpec((block, D), lambda i, place: (i, 0))
    weights = (*ups, *other_ups, *downs, *other_downs)
    down_shape = (len(downs), *downs[0].shape)

    def full(shape):
        return pl.BlockSpec(shape, lambda i, place: (0,) * len(shape))

    units = pl.BlockSpec((4, block, wide), lambda i, place: (0, i, 0))
    grid_spec = pltpu.PrefetchScalarGridSpec(
        num_scalar_prefetch=1,
        grid=(steps,),
        in_specs=[piece] * 8 + [full(part.shape) for part in weights],
        out_specs=[units, units, piece, piece, piece, piece, full((wide, D))] + [full(down_shape)] * 2,
        scratch_shapes=[pltpu.VMEM((D, wide), low), pltpu.VMEM((wide, D), jnp.float32)],
    )
    return pl.pallas_call(
        mlp_kernel,
        grid_spec=grid_spec,
        out_shape=[
            jax.ShapeDtypeStruct((4, rows, wide), low),
            jax.ShapeDtypeStruct((4, rows, wide), low),
            jax.ShapeDtypeStruct((rows, D), jnp.float32),
            jax.ShapeDtypeStruct((rows, D), low),
            jax.ShapeDtypeStruct((rows, D), low),
            jax.ShapeDtypeStruct((rows, D), low),
            jax.ShapeDtypeStruct((wide, D), low),
        ]
        + [jax.ShapeDtypeStruct(down_shape, low)] * 2,
        compiler_params=params(40),
        cost_estimate=FREE,
    )(place, *normed, *grads, *weights)


def mlp_grads_kernel(place_ref, *refs):
    nts, refs = refs[:4], refs[4:]
    act_ref, ud_ref, down_ref, keep_ref, one_ref, two_ref, three_ref, up_keep, up_send, up_acc = refs
    step = pl.program_id(0)
    rows = nts[0].shape[0]
    normed = jnp.concatenate([ref[...] for ref in nts])
    wide = act_ref.shape[2]
    active = act_ref[...].reshape(4 * rows, wide)
    up = outer(normed, ud_ref[...].reshape(4 * rows, wide))
    out = jnp.dot(active, down_ref[...], preferred_element_type=jnp.float32)
    keep_ref[...] = out[:rows]
    for index, to in enumerate((one_ref, two_ref, three_ref)):
        to[...] = out[(index + 1) * rows : (index + 2) * rows].astype(jnp.bfloat16)

    @pl.when(step == 0)
    def _():
        up_acc[...] = up

    @pl.when(step > 0)
    def _():
        up_acc[...] += up

    @pl.when(step == pl.num_programs(0) - 1)
    def _():
        depth, _, share = up_keep.shape[:3]
        half = wide // 2
        for side, to in enumerate((up_keep, up_send)):
            for near in range(depth):
                for far in range(4):
                    first = (far * depth + near) * share
                    part = up_acc[first : first + share, side * half : (side + 1) * half]
                    to[near ^ place_ref[0], far] = part.astype(jnp.bfloat16)


def mlp_grads(place, normed, active, delta, w_down, depth):
    rows = normed[0].shape[0]
    steps = 4
    block = rows // steps
    wide = active.shape[2]
    low = jnp.bfloat16
    piece = pl.BlockSpec((block, D), lambda i, place: (i, 0))
    units = pl.BlockSpec((4, block, wide), lambda i, place: (0, i, 0))

    def full(shape):
        return pl.BlockSpec(shape, lambda i, place: (0,) * len(shape))

    shapes = [(depth, 4, D // (4 * depth), wide // 2)] * 2
    grid_spec = pltpu.PrefetchScalarGridSpec(
        num_scalar_prefetch=1,
        grid=(steps,),
        in_specs=[piece] * 4 + [units] * 2 + [full(w_down.shape)],
        out_specs=[piece] * 4 + [full(shape) for shape in shapes],
        scratch_shapes=[pltpu.VMEM((D, wide), jnp.float32)],
    )
    return pl.pallas_call(
        mlp_grads_kernel,
        grid_spec=grid_spec,
        out_shape=[jax.ShapeDtypeStruct((rows, D), jnp.float32)]
        + [jax.ShapeDtypeStruct((rows, D), low)] * 3
        + [jax.ShapeDtypeStruct(shape, low) for shape in shapes],
        compiler_params=params(36),
        cost_estimate=FREE,
    )(place, *normed, active, delta, w_down)


def prepare_kernel(core_ref, qkv_ref, up_ref, out_ref, gains_ref, keep_ref, send_ref):
    core = core_ref[0]
    chips = up_ref.shape[1] // (2 * LANES)
    half = out_ref.shape[1] // 2
    depth = chips // 4
    for side, to in ((core, keep_ref), (1 - core, send_ref)):
        for chip in range(chips):
            cols = pl.ds(pl.multiple_of((2 * chip + side) * LANES, LANES), LANES)
            to[:, chip * LANES : (chip + 1) * LANES] = up_ref[:, cols]
        first = chips * LANES
        to[:, first : first + half] = out_ref[:, pl.ds(pl.multiple_of(side * half, half), half)]
        first += half
        for near in range(depth):
            for kind in range(3):
                cols = pl.ds(pl.multiple_of(kind * D + (2 * near + side) * LANES, LANES), LANES)
                to[:, first : first + LANES] = qkv_ref[:, cols]
                first += LANES
        to[:, first:] = jnp.broadcast_to(gains_ref[...], (to.shape[0], LANES))


def prepare(core, w_qkv, w_up, w_out, gains):
    share = w_qkv.shape[0]
    wide = (w_up.shape[1] + w_out.shape[1] + w_qkv.shape[1]) // 2 + LANES
    return pl.pallas_call(
        prepare_kernel,
        in_specs=[pl.BlockSpec(memory_space=pltpu.SMEM)]
        + [whole(array.shape) for array in (w_qkv, w_up, w_out, gains)],
        out_specs=[whole((share, wide))] * 2,
        out_shape=[jax.ShapeDtypeStruct((share, wide), jnp.bfloat16)] * 2,
        compiler_params=params(8),
        cost_estimate=FREE,
    )(core, w_qkv, w_up, w_out, gains)


def compose_kernel(place_ref, keep_ref, got_ref, up_ref, *parts):
    own_z = place_ref[0]
    share = keep_ref.shape[0]
    depth = len(parts)
    wide = up_ref.shape[2]
    half = D // 2
    heads = 4 * wide + half
    for side, ref in ((0, keep_ref), (1, got_ref)):
        rows = slice(side * share, (side + 1) * share)
        for far in range(4):
            up_ref[far, rows, :] = ref[:, far * wide : (far + 1) * wide]
        for far, part in enumerate(parts):
            first = heads + (own_z ^ far) * 3 * LANES
            part[rows, :half] = ref[:, 4 * wide : heads]
            part[rows, half : half + 3 * LANES] = ref[:, pl.ds(pl.multiple_of(first, LANES), 3 * LANES)]
            part[rows, half + 3 * LANES :] = ref[:, heads + depth * 3 * LANES :]


def compose(place, keep, got, depth):
    share = keep.shape[0]
    shapes = [(4, 2 * share, D // 2)] + [(2 * share, D)] * depth
    ups, *parts = pl.pallas_call(
        compose_kernel,
        in_specs=[pl.BlockSpec(memory_space=pltpu.SMEM), whole(keep.shape), whole(got.shape)],
        out_specs=[whole(shape) for shape in shapes],
        out_shape=[jax.ShapeDtypeStruct(shape, jnp.bfloat16) for shape in shapes],
        compiler_params=params(8),
        cost_estimate=FREE,
    )(place, keep, got)
    return ups, parts


def arrange_kernel(place_ref, own_ref, other_ref, near_ref):
    device, block, core = place_ref[0], place_ref[1], place_ref[2]
    planes, depth, share, half = own_ref.shape
    share //= 2
    count = near_ref.shape[0]
    per_block = LANES // share
    for ref, swapped, col in ((own_ref, 0, core), (other_ref, 1, 1 - core)):
        cols = pl.ds(pl.multiple_of(col * half, half), half)
        for far in range(planes):
            for near in range(depth):
                for side in range(2):
                    owner = device ^ ((far * depth + near) * 2 + (side ^ swapped))
                    heads = (owner // per_block) ^ block
                    to = (heads % 2) * (count // 2) + heads // 2
                    row = pl.ds(pl.multiple_of((owner % per_block) * share, share), share)
                    near_ref[to, row, cols] = ref[far, near, side * share : (side + 1) * share, :]


def arrange(place, own, other):
    shape = (D // LANES, LANES, D)
    return pl.pallas_call(
        arrange_kernel,
        in_specs=[pl.BlockSpec(memory_space=pltpu.SMEM), whole(own.shape), whole(other.shape)],
        out_specs=whole(shape),
        out_shape=jax.ShapeDtypeStruct(shape, jnp.bfloat16),
        compiler_params=params(12),
        cost_estimate=FREE,
    )(place, own, other)


def collect_kernel(place_ref, *refs):
    parts, outs = refs[:4], refs[4:]
    total = sum(part[...].astype(jnp.float32) for part in parts)
    depth, (share, wide) = len(outs), outs[0].shape
    qkv = 3 * LANES
    tall = depth * share
    for natural in range(depth):
        part = total[natural * share : (natural + 1) * share, :].astype(jnp.bfloat16)
        for far, out_ref in enumerate(outs):

            @pl.when((place_ref[0] ^ far) == natural)
            def _():
                out_ref[:, :qkv] = part[:, :qkv]
                out_ref[:, qkv + LANES :] = part[:, qkv:]

    exact = total[tall : tall + 4, :tall] + total[tall + 4 : tall + 8, :tall]
    high = exact.astype(jnp.bfloat16).astype(jnp.float32)
    parts = jnp.concatenate([high, exact - high], axis=0)
    parts = jnp.concatenate([parts[:, :LANES], parts[:, LANES:]], axis=0).astype(jnp.bfloat16)
    for out_ref in outs:
        out_ref[:16, qkv : qkv + LANES] = parts
        out_ref[16:, qkv : qkv + LANES] = jnp.zeros((share - 16, LANES), jnp.bfloat16)


def collect(place, parts, depth):
    rows, wide = parts[0].shape
    shape = ((rows - 16) // depth, wide + LANES)
    return pl.pallas_call(
        collect_kernel,
        in_specs=[pl.BlockSpec(memory_space=pltpu.SMEM)] + [whole(part.shape) for part in parts],
        out_specs=[whole(shape)] * depth,
        out_shape=[jax.ShapeDtypeStruct(shape, jnp.bfloat16)] * depth,
        compiler_params=params(8),
        cost_estimate=FREE,
    )(place, *parts)


def divide_kernel(place_ref, *refs):
    parts, (own_ref, sent_ref, own_out, sent_out) = refs[:-4], refs[-4:]
    core = place_ref[0]
    qkv = 3 * LANES
    share = own_ref.shape[1]
    depth = len(parts)
    own_rows = pl.ds(pl.multiple_of(core * share, share), share)
    other_rows = pl.ds(pl.multiple_of((1 - core) * share, share), share)
    for far, part in enumerate(parts):
        own_ref[far] = part[own_rows, : 3 * LANES]
        sent_ref[far] = part[other_rows, : 3 * LANES]
    for rows, ref in ((own_rows, own_out), (other_rows, sent_out)):
        ref[...] = sum(part[rows, qkv + LANES :].astype(jnp.float32) for part in parts)
    vectors = sum(part[0:16, qkv : qkv + LANES].astype(jnp.float32) for part in parts)
    high = vectors.astype(jnp.bfloat16).astype(jnp.float32)
    zero = jnp.zeros((16, LANES), jnp.float32)
    both = jnp.concatenate([high, vectors - high, zero], axis=1).astype(jnp.bfloat16)
    for ref in (own_ref, sent_ref):
        ref[depth, :16, :] = both
        ref[depth, 16:, :] = jnp.zeros((share - 16, 3 * LANES), jnp.bfloat16)


def divide(core, parts):
    share = parts[0].shape[0] // 2
    shapes = [jax.ShapeDtypeStruct((len(parts) + 1, share, 3 * LANES), jnp.bfloat16)] * 2
    shapes += [jax.ShapeDtypeStruct((share, parts[0].shape[1] - 4 * LANES), jnp.float32)] * 2
    return pl.pallas_call(
        divide_kernel,
        in_specs=[pl.BlockSpec(memory_space=pltpu.SMEM)] + [whole(part.shape) for part in parts],
        out_specs=[whole(shape.shape) for shape in shapes],
        out_shape=shapes,
        compiler_params=params(8),
        cost_estimate=FREE,
    )(core, *parts)


def finish_kernel(place_ref, qkv_ref, got_qkv_ref, own_out, got_out, grad_ref, vector_ref, out_ref):
    block, core = place_ref[0], place_ref[1]
    half = out_ref.shape[1] // 2
    out_ref[:, pl.ds(pl.multiple_of(core * half, half), half)] = own_out[...]
    out_ref[:, pl.ds(pl.multiple_of((1 - core) * half, half), half)] = got_out[...]
    depth = qkv_ref.shape[0] - 1
    for near, qkv in enumerate((qkv_ref, got_qkv_ref)):
        for far in range(depth):
            first = (block ^ (2 * far + near)) * LANES
            for kind in range(3):
                to = pl.ds(pl.multiple_of(kind * D + first, LANES), LANES)
                grad_ref[:, to] = qkv[far, :, kind * LANES : (kind + 1) * LANES].astype(jnp.float32)
    both = qkv_ref[depth, :16, :].astype(jnp.float32) + got_qkv_ref[depth, :16, :].astype(jnp.float32)
    exact = both[:, :LANES] + both[:, LANES : 2 * LANES]
    vector_ref[:, :LANES] = exact[0:4] + exact[4:8]
    vector_ref[:, LANES:] = exact[8:12] + exact[12:16]


def finish(place, qkv, got_qkv, own_out, got_out):
    share = qkv.shape[1]
    shapes = [(share, 3 * D), (4, 2 * LANES), (share, D)]
    arrays = (qkv, got_qkv, own_out, got_out)
    return pl.pallas_call(
        finish_kernel,
        in_specs=[pl.BlockSpec(memory_space=pltpu.SMEM)] + [whole(array.shape) for array in arrays],
        out_specs=[whole(shape) for shape in shapes],
        out_shape=[jax.ShapeDtypeStruct(shape, jnp.float32) for shape in shapes],
        compiler_params=params(8),
        cost_estimate=FREE,
    )(place, *arrays)


def finish_up_kernel(core_ref, own_ref, got_ref, up_ref):
    depth = own_ref.shape[2] // LANES
    for near, ref in enumerate((own_ref, got_ref)):
        side = core_ref[0] ^ near
        for far in range(4):
            for chip in range(depth):
                to = pl.ds(pl.multiple_of(((far * depth + chip) * 2 + side) * LANES, LANES), LANES)
                up_ref[:, to] = ref[far, :, chip * LANES : (chip + 1) * LANES].astype(jnp.float32)


def finish_up(core, own, got):
    shape = (own.shape[1], 4 * D)
    return pl.pallas_call(
        finish_up_kernel,
        in_specs=[pl.BlockSpec(memory_space=pltpu.SMEM), whole(own.shape), whole(got.shape)],
        out_specs=whole(shape),
        out_shape=jax.ShapeDtypeStruct(shape, jnp.float32),
        compiler_params=params(8),
        cost_estimate=FREE,
    )(core, own, got)


def turned(values):
    return values.astype(jnp.float32).T.astype(jnp.bfloat16)


def out_project_kernel(gains_ref, tokens_ref, near_ref, *refs):
    heads, (hidden_ref, normed_ref) = refs[:-2], refs[-2:]
    rows = tokens_ref.shape[0]
    depth = len(heads) // 2
    parts = [ref[:rows, :] if far < depth else ref[rows:, :] for far, ref in enumerate(heads)]
    hidden = tokens_ref[...].astype(jnp.float32) + jnp.dot(
        jnp.concatenate(parts, axis=1), near_ref[...].reshape(D, D), preferred_element_type=jnp.float32
    )
    normal, _ = moments(hidden)
    hidden_ref[...] = hidden
    normed_ref[...] = (normal * gains_ref[2:3, :] + gains_ref[3:4, :]).astype(jnp.bfloat16)


def out_project(gains, tokens, near_out, heads):
    arrays = (gains, tokens, near_out, *heads)
    return pl.pallas_call(
        out_project_kernel,
        in_specs=[whole(array.shape) for array in arrays],
        out_specs=[whole(tokens.shape)] * 2,
        out_shape=[
            jax.ShapeDtypeStruct(tokens.shape, jnp.float32),
            jax.ShapeDtypeStruct(tokens.shape, jnp.bfloat16),
        ],
        compiler_params=params(12),
        cost_estimate=FREE,
    )(*arrays)


def norm_two_kernel(gains_ref, hidden_ref, grad_ref, own_ref, *refs):
    sides, (delta_ref, low_ref, sums_ref) = refs[:-3], refs[-3:]
    delta = own_ref[...]
    for side in sides:
        delta += side[...].astype(jnp.float32)
    normal, scale = moments(hidden_ref[...])
    sums = jnp.concatenate(
        [jnp.sum(delta * normal, axis=0, keepdims=True), jnp.sum(delta, axis=0, keepdims=True)], axis=0
    )

    @pl.when(pl.program_id(0) == 0)
    def _():
        sums_ref[...] = sums

    @pl.when(pl.program_id(0) > 0)
    def _():
        sums_ref[...] += sums

    hidden_delta = grad_ref[...].astype(jnp.float32) + norm_back(delta, gains_ref[2:3, :], normal, scale)
    delta_ref[...] = hidden_delta
    low_ref[...] = hidden_delta.astype(jnp.bfloat16)


def by_rows(shape, steps):
    return pl.BlockSpec((shape[0] // steps, shape[1]), lambda i: (i, 0))


def norm_two(gains, hidden, out_grad, own, sides):
    arrays = (hidden, out_grad, own, *sides)
    piece = by_rows(hidden.shape, 4)
    return pl.pallas_call(
        norm_two_kernel,
        grid=(4,),
        in_specs=[whole(gains.shape)] + [piece] * len(arrays),
        out_specs=[piece, piece, whole((2, D))],
        out_shape=[
            jax.ShapeDtypeStruct(hidden.shape, jnp.float32),
            jax.ShapeDtypeStruct(hidden.shape, jnp.bfloat16),
            jax.ShapeDtypeStruct((2, D), jnp.float32),
        ],
        compiler_params=params(10),
        cost_estimate=FREE,
    )(gains, *arrays)


def norm_one_kernel(gains_ref, tokens_ref, hidden_ref, own_ref, *refs):
    sides, out_ref = refs[:-1], refs[-1]
    delta = own_ref[...]
    for side in sides:
        delta += side[...].astype(jnp.float32)
    normal, scale = moments(tokens_ref[...].astype(jnp.float32))
    out_ref[...] = hidden_ref[...] + norm_back(delta, gains_ref[0:1, :], normal, scale)


def norm_one(gains, tokens, hidden_delta, own, sides):
    arrays = (tokens, hidden_delta, own, *sides)
    piece = by_rows(tokens.shape, 4)
    return pl.pallas_call(
        norm_one_kernel,
        grid=(4,),
        in_specs=[whole(gains.shape)] + [piece] * len(arrays),
        out_specs=piece,
        out_shape=jax.ShapeDtypeStruct(tokens.shape, jnp.float32),
        compiler_params=params(10),
        cost_estimate=FREE,
    )(gains, *arrays)


def out_grads_kernel(place_ref, cols_ref, *refs):
    heads, outs, heads_t = refs[:-5], refs[-5:-1], refs[-1]
    plane, own_block = place_ref[0], place_ref[1]
    depth = len(heads) // 2
    rows = cols_ref.shape[0] // 2
    for far, ref in enumerate(heads):
        core, near = far // depth, far % depth
        row = pl.multiple_of((own_block ^ (2 * near + core)) * LANES, LANES)
        part = ref[...] if core == 0 else jnp.concatenate([ref[rows:, :], ref[:rows, :]])
        heads_t[pl.ds(row, LANES), :] = turned(part)
    tall = D // 4
    for far, out in enumerate(outs):
        row = pl.multiple_of((plane ^ far) * tall, tall)
        left = heads_t[pl.ds(row, tall), :]
        out[:tall, :] = jnp.dot(left, cols_ref[...], preferred_element_type=jnp.float32).astype(jnp.bfloat16)
        out[tall:, :] = jnp.zeros((out.shape[0] - tall, out.shape[1]), jnp.bfloat16)


def out_grads(place, heads, hidden_both):
    rows = hidden_both.shape[0]
    low = jnp.bfloat16

    def full(shape):
        return pl.BlockSpec(shape, lambda i, place: (0,) * len(shape))

    shape = (D // 4 + 16, D // 2)
    grid_spec = pltpu.PrefetchScalarGridSpec(
        num_scalar_prefetch=1,
        grid=(1,),
        in_specs=[pl.BlockSpec((rows, D // 2), lambda i, place: (0, place[2]))]
        + [full(part.shape) for part in heads],
        out_specs=[full(shape)] * 4,
        scratch_shapes=[pltpu.VMEM((D, rows), low)],
    )
    return pl.pallas_call(
        out_grads_kernel,
        grid_spec=grid_spec,
        out_shape=[jax.ShapeDtypeStruct(shape, low)] * 4,
        compiler_params=params(12),
        cost_estimate=FREE,
    )(place, hidden_both, *heads)


def back_project_kernel(own_ref, other_ref, own_weights, other_weights, keep_ref, *outs):
    for far in range(own_ref.shape[0]):
        total = jnp.dot(own_ref[far], own_weights[...], preferred_element_type=jnp.float32)
        total += jnp.dot(other_ref[far], other_weights[...], preferred_element_type=jnp.float32)
        if far == 0:
            keep_ref[...] = total
        else:
            outs[far - 1][...] = total.astype(jnp.bfloat16)


def back_project(own, other, own_weights, other_weights):
    count, rows, _ = own.shape
    arrays = (own, other, own_weights, other_weights)
    return pl.pallas_call(
        back_project_kernel,
        in_specs=[whole(array.shape) for array in arrays],
        out_specs=[whole((rows, D))] * count,
        out_shape=[jax.ShapeDtypeStruct((rows, D), jnp.float32)]
        + [jax.ShapeDtypeStruct((rows, D), jnp.bfloat16)] * (count - 1),
        compiler_params=params(24),
        cost_estimate=FREE,
    )(*arrays)


def qkv_grad_kernel(place_ref, nm_ref, turned_ref, gains_ref, two_ref, *refs):
    deltas, terms, outs, (total, sums) = refs[:-10], refs[-10:-6], refs[-6:-2], refs[-2:]
    count, rows, _ = deltas[0].shape
    ones = jnp.ones((rows, LANES), jnp.bfloat16)
    for index in range(2 * count):
        delta = deltas[index % 2][index // 2]
        part = outer(delta, nm_ref[index * rows : (index + 1) * rows, :])
        column = outer(delta, ones)
        if index == 0:
            total[...] = part
            sums[...] = column
        else:
            total[...] += part
            sums[...] += column
    gain, bias = gains_ref[0:1, :], gains_ref[1:2, :]
    weights = turned_ref[...].astype(jnp.float32)
    column = sums[:, 0:1]
    bias_part = jnp.sum(weights * column, axis=0, keepdims=True)
    gain_part = (jnp.sum(weights * total[...], axis=0, keepdims=True) - bias * bias_part) / gain
    exact = jnp.concatenate([gain_part, bias_part, two_ref[0:2, :]], axis=0)
    high = exact.astype(jnp.bfloat16).astype(jnp.float32)
    parts = jnp.concatenate([high, exact - high, jnp.zeros((8, D), jnp.float32)], axis=0)
    total_parts = parts.astype(jnp.bfloat16)
    tall = D // 4
    for natural in range(4):
        for far in range(4):

            @pl.when((place_ref[0] ^ far) == natural)
            def _():
                cols = slice(natural * tall, (natural + 1) * tall)
                outs[far][:tall, : 3 * LANES] = total[:, cols].T.astype(jnp.bfloat16)
                outs[far][tall:, :tall] = total_parts[:, cols]
    for term, out in zip(terms, outs):
        wide = out.shape[1] - term.shape[1]
        out[:, wide:] = term[...]
        out[D // 4 :, D // 4 : wide] = jnp.zeros((16, wide - D // 4), jnp.bfloat16)


def qkv_gradient(place, deltas, normed, turned_weights, gains, two, terms):
    shape = (D // 4 + 16, 3 * LANES + terms[0].shape[1])
    arrays = (normed, turned_weights, gains, two, *deltas, *terms)
    return pl.pallas_call(
        qkv_grad_kernel,
        in_specs=[pl.BlockSpec(memory_space=pltpu.SMEM)] + [whole(array.shape) for array in arrays],
        out_specs=[whole(shape)] * 4,
        out_shape=[jax.ShapeDtypeStruct(shape, jnp.bfloat16)] * 4,
        scratch_shapes=[pltpu.VMEM((3 * LANES, D), jnp.float32), pltpu.VMEM((3 * LANES, LANES), jnp.float32)],
        compiler_params=params(28),
        cost_estimate=FREE,
    )(place, *arrays)


def moments(values):
    centred = values - jnp.mean(values, axis=1, keepdims=True)
    scale = lax.rsqrt(jnp.mean(centred * centred, axis=1, keepdims=True) + EPSILON)
    return centred * scale, scale


def norm_back(delta, gain, normal, scale):
    e = delta * gain
    return scale * (
        e - jnp.mean(e, axis=1, keepdims=True) - normal * jnp.mean(e * normal, axis=1, keepdims=True)
    )


def added(keep, got):
    return (keep.astype(jnp.float32) + got.astype(jnp.float32)).astype(jnp.bfloat16)


def on_planes(
    tokens_in,
    out_grad,
    w_qkv,
    w_out,
    w_up,
    w_down,
    norm1_gain,
    norm1_bias,
    norm2_gain,
    norm2_bias,
):
    depth = lax.axis_size("z")
    rows = tokens_in.shape[0]
    share = w_qkv.shape[0]
    low = jnp.bfloat16
    places = {axis: lax.axis_index(axis) for axis in ALL}
    core = places["c"]
    block = 2 * places["z"] + core
    device = ((2 * places["y"] + places["x"]) * depth + places["z"]) * 2 + core

    hold = lax.optimization_barrier
    plane = 2 * places["y"] + places["x"]

    def index_of(*values):
        return jnp.stack(values).astype(jnp.int32)

    def along_z(part, far):
        return swap(part, "z", depth, far)

    def middle_z(part):
        return lax.ppermute(part, "z", [(1, 2), (2, 1)])

    def over_plane(part, far):
        return swap(part, ("y", "x"), 4, far)

    waiting, have = {}, {}

    def stage(name, *main):
        extra = {}
        for item in list(waiting):
            if BESIDE[item] == name:
                operand, function = waiting.pop(item)
                extra[item] = function(operand)
        main, extra, left = hold((main, extra, {item: waiting[item][0] for item in waiting}))
        for item in waiting:
            waiting[item] = (left[item], waiting[item][1])
        have.update(extra)
        return main

    def on_line(far):
        return lambda part: along_z(part, far)

    def on_plane(far):
        return lambda part: over_plane(part, far)

    tokens_two = along_z(tokens_in, 2)
    gains = jnp.concatenate([norm1_gain, norm1_bias, norm2_gain, norm2_bias]).reshape(1, LANES)
    keep, send = prepare(core.reshape(1), w_qkv, w_up, w_out, gains)
    keep, sent_one, sent_grad = hold((keep, tokens_in, out_grad))
    got = pair(send)
    tokens_one = along_z(sent_one, 1)
    grads = [out_grad] + [over_plane(sent_grad, far) for far in (1, 2)]
    ups, parts = compose(index_of(places["z"]), keep, got, depth)
    ups = lax.all_to_all(ups, ("y", "x"), 0, 0, tiled=True)
    tokens_two, tokens_one, grads, parts, ups, sent_tokens, sent_grad = hold(
        (tokens_two, tokens_one, grads, parts, ups, tokens_in, out_grad)
    )

    along = [parts[0]] + [along_z(parts[far], far) for far in range(1, depth)]
    one_pair = pair(tokens_one)
    waiting["up1"] = (ups, on_line(1))
    waiting["ogd"] = (out_grad, on_plane(3))
    along, one_pair, tokens_two, sent_tokens, ups = stage("tokens", along, one_pair, tokens_two, sent_tokens, ups)

    middle, ends = middle_z(sent_tokens), lax.ppermute(tokens_two, "z", [(1, 0), (2, 3)])
    outs = jnp.stack([part[:, : D // 2] for part in along])
    along = jnp.stack([part[:, D // 2 :] for part in along])
    across = [along] + [over_plane(along, far) for far in range(1, 4)]
    across, middle, ends, ups, outs = stage("plane", across, middle, ends, ups, outs)
    group = [tokens_in, pair(sent_tokens), tokens_one, one_pair, tokens_two, pair(tokens_two)]
    group += [part for mine in (middle, ends) for part in (mine, pair(mine))]
    group, across, ups, outs = stage("pairs", group, across, ups, outs)

    qkv, normed, gains, turned_qkv = project(device, group, across)
    own_ups = ups
    up_two, up_three = along_z(ups, 2), along_z(ups, 3)
    outs = [outs] + [over_plane(outs, far) for far in range(1, 4)]
    attended_low, attended, recip, probs = attend(qkv)
    attended_low, up_two, up_three, outs = stage("attention", attended_low, up_two, up_three, outs)

    both = 2 * rows
    sides = [attended_low[:both]] + [
        along_z(attended_low[far * both : (far + 1) * both], far) for far in range(1, depth)
    ]
    outs = jnp.stack(outs)
    near_out = arrange(index_of(device, block, core), outs, pair(outs))
    own_out = near_out[:depth].reshape(depth * LANES, D)
    waiting["turned"] = (turned_qkv, pair)
    sides, near_out = stage("heads", sides, near_out)
    heads = [*sides, *(pair(part) for part in sides)]
    hidden, normed_two = out_project(gains, tokens_in, near_out, heads)
    normed_two, heads, sent_down = stage("hidden", normed_two, heads, w_down)

    plane_normed = [normed_two] + [over_plane(normed_two, far) for far in range(1, 4)]
    downs = [w_down] + [along_z(sent_down, far) for far in range(1, depth)]
    other_downs = [pair(part) for part in downs]
    waiting["oups0"], waiting["oups2"], waiting["oups3"] = (own_ups, pair), (up_two, pair), (up_three, pair)
    plane_normed, downs, other_downs = stage("units", plane_normed, downs, other_downs)
    ups = [own_ups, have["up1"], up_two, up_three]
    other_ups = [have["oups0"], pair(have["up1"]), have["oups2"], have["oups3"]]
    grads = [*grads, have["ogd"]]
    active, up_delta, two_delta, *part, own_down, down_keep, down_send = mlp(
        index_of(device, places["z"]), plane_normed, grads, ups, other_ups, downs, other_downs
    )

    two_sides = [over_plane(part[far - 1], far) for far in range(1, 4)]
    down_got = pair(down_send)
    down_term = [added(down_keep[far], down_got[far]) for far in range(depth)]
    waiting["dz2"], waiting["dz3"], waiting["dz1"] = ((down_term[far], on_line(far)) for far in (2, 3, 1))
    out_own, *out_parts, up_term, up_send = mlp_grads(
        index_of(places["z"]), plane_normed, active, up_delta, own_down, depth
    )
    waiting["lo1"], waiting["lo2"], waiting["lo3"] = ((out_parts[far - 1], on_plane(far)) for far in (1, 2, 3))
    two_sides, up_term, up_send = stage("sums", two_sides, up_term, up_send)
    hidden_delta, hidden_low, two_sums = norm_two(gains, hidden, out_grad, two_delta, two_sides)
    hidden_both = jnp.concatenate([hidden_low, pair(hidden_low)])
    att_delta = against(hidden_both, own_out).astype(low)
    att_delta, up_send, heads, up_term = stage("norm", att_delta, up_send, heads, up_term)

    far_delta = [att_delta[:, :LANES]] + [
        along_z(att_delta[:, far * LANES : (far + 1) * LANES], far) for far in range(1, depth)
    ]
    up_got = pair(up_send)
    out_terms = out_grads(index_of(plane, block, core), heads, hidden_both)
    up_term = [added(up_term[far], up_got[far]) for far in range(depth)]
    far_delta, out_terms, up_term = stage("delta", far_delta, out_terms, up_term)

    deltas = attend_back(qkv, probs, far_delta, attended, recip)
    up_sides = [up_term[0]] + [along_z(up_term[far], far) for far in range(1, depth)]
    deltas, up_sides = stage("back", deltas, up_sides)

    got = pair(deltas[1])
    one_delta, *part = back_project(deltas[0], got, turned_qkv, have["turned"])
    part, deltas, out_terms, up_sides = stage("project", part, deltas, out_terms, up_sides)

    waiting["upa"] = (
        up_sides,
        lambda parts: lax.all_to_all(
            sum(side.astype(jnp.float32) for side in parts).astype(low), ("y", "x"), 0, 0, tiled=True
        ),
    )
    ends, middle = lax.ppermute(part[2], "z", [(0, 1), (3, 2)]), middle_z(part[2])
    qkv_terms = qkv_gradient(index_of(plane), deltas, normed, turned_qkv, gains, two_sums, out_terms)
    ends, middle, qkv_terms = stage("middle", ends, middle, qkv_terms)

    one_sides = [along_z(added(part[1], ends), 2), along_z(part[0], 1), middle]
    terms = [qkv_terms[0]] + [over_plane(qkv_terms[far], far) for far in range(1, 4)]
    qkv_part = collect(index_of(places["z"]), terms, depth)
    one_sides, qkv_part = stage("rest", one_sides, qkv_part)
    out_sum = hidden + out_own
    for item in ("lo1", "lo2"):
        out_sum = out_sum + have[item].astype(jnp.float32)

    qkv_sides = [qkv_part[0]] + [along_z(qkv_part[far], far) for far in range(1, depth)]
    input_grad = norm_one(gains, tokens_in, hidden_delta, one_delta, one_sides)
    qkv_sides, input_grad, out_sum = stage("last", qkv_sides, input_grad, out_sum)
    up_sum = have["upa"]
    own_part = lax.dynamic_slice_in_dim(up_sum, core * share, share, 1)
    other_part = lax.dynamic_slice_in_dim(up_sum, (1 - core) * share, share, 1)
    up_grad = finish_up(index_of(core), own_part, pair(other_part))
    result = (out_sum + have["lo3"].astype(jnp.float32)).astype(low)
    down_sum = down_term[0].astype(jnp.float32)
    for item in ("dz1", "dz2", "dz3"):
        down_sum = down_sum + have[item].astype(jnp.float32)
    own_qkv, sent_qkv, own_out, sent_out = divide(index_of(core), qkv_sides)
    qkv_grad, vectors, out_weight_grad = finish(
        index_of(block, core), own_qkv, pair(sent_qkv), own_out, pair(sent_out)
    )
    vectors = lax.dynamic_slice_in_dim(vectors, (places["z"] * 2 + core) * share, share, 1)
    return (
        result,
        input_grad,
        qkv_grad,
        out_weight_grad,
        up_grad,
        down_sum,
        vectors[0],
        vectors[1],
        vectors[2],
        vectors[3],
    )


def solution(mesh):
    scenes, blocks = mesh.devices.shape

    def place(axes):
        matrix = P(axes, None)
        views = P(axes[: len(axes) // 2] if len(axes) > 2 else axes[0], None)
        vector = P(axes)
        ins = (matrix, views, views, views, matrix, matrix, matrix, matrix, matrix) + (vector,) * 4
        return ins, (matrix,) * 6 + (vector,) * 4

    def run(*arrays):
        one_scene = arrays[1].shape[1] == 4
        if scenes == 4 and blocks == 8 and one_scene and arrays[0].shape[0] == 8192:
            fine = Mesh(mesh.devices.reshape(2, 2, blocks // 2, 2), ALL)
            ins, outs = place(ALL)
            step = lambda tokens, heights, widths, labels, *rest: on_planes(tokens, *rest)
            return jax.shard_map(step, mesh=fine, in_specs=ins, out_specs=outs, check_vma=False)(*arrays)
        ins, outs = place(("scene", "blk"))
        return jax.shard_map(on_any_slice, mesh=mesh, in_specs=ins, out_specs=outs, check_vma=False)(*arrays)

    return run
```

```python
import functools
import math

import jax
import jax.numpy as jnp
from jax import lax
from jax.experimental import pallas as pl
from jax.experimental.pallas import tpu as pltpu
from jax.sharding import Mesh
from jax.sharding import PartitionSpec as P

D = 1024
HEADS = 16
HEAD_DIM = 64


EPSILON = 1e-05
MASKED = -1e30


def layer_norm(values, gain_row, bias_row):
    centred = values - jnp.mean(values, axis=1, keepdims=True)
    scaled = centred * lax.rsqrt(jnp.mean(centred * centred, axis=1, keepdims=True) + EPSILON)
    return scaled * gain_row + bias_row


def scene_rows(view_ends, labels, first_row, count_rows):
    places = first_row + jnp.arange(count_rows, dtype=jnp.int32)
    view_index = jnp.sum((places[:, None] >= view_ends[None, :]).astype(jnp.int32), axis=1)
    matches = view_index[:, None] == jnp.arange(labels.shape[0], dtype=jnp.int32)[None, :]
    return jnp.sum(jnp.where(matches, labels[None, :], 0), axis=1)


def in_blocks(update, carry, members):
    total_rows = members[0].shape[0]
    width_rows = math.gcd(total_rows, 1024)
    block_count = total_rows // width_rows
    stacked = tuple(
        (member.reshape((block_count, width_rows) + member.shape[1:]) for member in members)
    )

    def advance(state_now, indexed):
        block_index, block_parts = indexed
        return (update(state_now, block_parts, block_index * width_rows), None)

    carry, _ = lax.scan(advance, carry, (jnp.arange(block_count, dtype=jnp.int32), stacked))
    return carry


def heads_of(rows):
    return rows.reshape(rows.shape[0], HEADS, HEAD_DIM)


def pair_terms(
    query_heads, delta_heads, log_rows, probe_rows, allowed, key_heads, value_heads, score_scale
):
    raw = (
        jnp.einsum("qhe,khe->hqk", query_heads, key_heads, preferred_element_type=jnp.float32)
        * score_scale
    )
    weights_now = jnp.where(allowed, jnp.exp(raw - log_rows[:, :, None]), 0.0)
    backward = jnp.einsum(
        "qhe,khe->hqk", delta_heads, value_heads, preferred_element_type=jnp.float32
    )
    score_delta = (weights_now * (backward - probe_rows[:, :, None])).astype(jnp.bfloat16)
    return (weights_now.astype(jnp.bfloat16), score_delta)


def outer(left, right):
    return lax.dot_general(
        left, right, (((0,), (0,)), ((), ())), preferred_element_type=jnp.float32
    )


def against(left, right):
    return lax.dot_general(
        left, right, (((1,), (1,)), ((), ())), preferred_element_type=jnp.float32
    )


def on_any_slice(
    tokens_in,
    view_heights,
    view_widths,
    view_scenes,
    out_grad,
    w_qkv,
    w_out,
    w_up,
    w_down,
    norm1_gain,
    norm1_bias,
    norm2_gain,
    norm2_bias,
):
    gathered = (
        lax.all_gather(w_qkv, ("scene", "blk"), axis=0, tiled=True),
        lax.all_gather(w_out, ("scene", "blk"), axis=0, tiled=True),
        lax.all_gather(w_up, ("scene", "blk"), axis=0, tiled=True),
        lax.all_gather(w_down, ("scene", "blk"), axis=0, tiled=True),
        lax.all_gather(norm1_gain, ("scene", "blk"), axis=0, tiled=True),
        lax.all_gather(norm1_bias, ("scene", "blk"), axis=0, tiled=True),
        lax.all_gather(norm2_gain, ("scene", "blk"), axis=0, tiled=True),
        lax.all_gather(norm2_bias, ("scene", "blk"), axis=0, tiled=True),
    )
    full_qkv, full_out, full_up, full_down = (gathered[0], gathered[1], gathered[2], gathered[3])
    gain_one = gathered[4].astype(jnp.float32)
    bias_one = gathered[5].astype(jnp.float32)
    gain_two = gathered[6].astype(jnp.float32)
    bias_two = gathered[7].astype(jnp.float32)
    local_rows = tokens_in.shape[0]
    view_ends = jnp.cumsum(view_heights[0] * view_widths[0])
    labels = view_scenes[0]
    own_first = lax.axis_index("blk") * local_rows
    own_scene = scene_rows(view_ends, labels, own_first, local_rows)
    score_scale = HEAD_DIM ** (-0.5)
    inputs = tokens_in.astype(jnp.float32)
    normed, norm_one_pull = jax.vjp(layer_norm, inputs, gain_one, bias_one)
    normed_low = normed.astype(jnp.bfloat16)
    projected = jnp.dot(normed_low, full_qkv, preferred_element_type=jnp.float32).astype(
        jnp.bfloat16
    )
    query_rows = projected[:, :D]
    key_rows = projected[:, D : 2 * D]
    value_rows = projected[:, 2 * D :]
    query_heads = heads_of(query_rows)

    def forward_update(state_now, members, first_row):
        run_max, run_sum, run_total = state_now
        piece_keys, piece_values = members
        piece_rows = piece_keys.shape[0]
        key_scene = scene_rows(view_ends, labels, first_row, piece_rows)
        allowed = (own_scene[:, None] == key_scene[None, :])[None]
        raw = (
            jnp.einsum(
                "qhe,khe->hqk",
                query_heads,
                heads_of(piece_keys),
                preferred_element_type=jnp.float32,
            )
            * score_scale
        )
        new_max = jnp.maximum(run_max, jnp.max(jnp.where(allowed, raw, MASKED), axis=2))
        expo = jnp.where(allowed, jnp.exp(raw - new_max[:, :, None]), 0.0)
        factor = jnp.exp(run_max - new_max)
        run_sum = run_sum * factor + jnp.sum(expo, axis=2)
        mixed = jnp.einsum(
            "hqk,khe->qhe",
            expo.astype(jnp.bfloat16),
            heads_of(piece_values),
            preferred_element_type=jnp.float32,
        )
        run_total = run_total * jnp.transpose(factor)[:, :, None] + mixed
        return (new_max, run_sum, run_total)

    start_state = (
        jnp.full((HEADS, local_rows), MASKED, jnp.float32),
        jnp.zeros((HEADS, local_rows), jnp.float32),
        jnp.zeros((local_rows, HEADS, HEAD_DIM), jnp.float32),
    )
    run_max, run_sum, run_total = in_blocks(
        forward_update,
        start_state,
        (
            lax.all_gather(key_rows, "blk", axis=0, tiled=True),
            lax.all_gather(value_rows, "blk", axis=0, tiled=True),
        ),
    )
    log_total = run_max + jnp.log(run_sum)
    attended_heads = run_total / jnp.transpose(run_sum)[:, :, None]
    attended_low = attended_heads.reshape(local_rows, D).astype(jnp.bfloat16)
    hidden = inputs + jnp.dot(attended_low, full_out, preferred_element_type=jnp.float32)
    normed_two, norm_two_pull = jax.vjp(layer_norm, hidden, gain_two, bias_two)
    normed_two_low = normed_two.astype(jnp.bfloat16)
    upward = jnp.dot(normed_two_low, full_up, preferred_element_type=jnp.float32)
    active, gelu_pull = jax.vjp(jax.nn.gelu, upward)
    active_low = active.astype(jnp.bfloat16)
    result = (hidden + jnp.dot(active_low, full_down, preferred_element_type=jnp.float32)).astype(
        jnp.bfloat16
    )
    down_term = outer(active_low, out_grad)
    up_delta = gelu_pull(against(out_grad, full_down))[0].astype(jnp.bfloat16)
    up_term = outer(normed_two_low, up_delta)
    hidden_back, gain_two_term, bias_two_term = norm_two_pull(against(up_delta, full_up))
    hidden_delta = out_grad.astype(jnp.float32) + hidden_back
    hidden_low = hidden_delta.astype(jnp.bfloat16)
    out_term = outer(attended_low, hidden_low)
    att_delta = against(hidden_low, full_out).astype(jnp.bfloat16)
    delta_heads = heads_of(att_delta)
    row_probe = jnp.transpose(jnp.sum(delta_heads.astype(jnp.float32) * attended_heads, axis=2))
    query_start = jnp.zeros((local_rows, HEADS, HEAD_DIM), jnp.float32)
    every_key, every_value = (
        lax.all_gather(key_rows, "blk", axis=0, tiled=True),
        lax.all_gather(value_rows, "blk", axis=0, tiled=True),
    )
    group_rows = every_key.shape[0]
    width_rows = math.gcd(group_rows, 1024)
    block_count = group_rows // width_rows

    def joint_step(total, indexed):
        block_index, block_keys, block_values = indexed
        block_first = block_index * width_rows
        key_heads = heads_of(block_keys)
        value_heads = heads_of(block_values)
        key_scene = scene_rows(view_ends, labels, block_first, width_rows)
        allowed = (own_scene[:, None] == key_scene[None, :])[None]
        weights_low, score_delta = pair_terms(
            query_heads,
            delta_heads,
            log_total,
            row_probe,
            allowed,
            key_heads,
            value_heads,
            score_scale,
        )
        total = (
            total
            + jnp.einsum("hqk,khe->qhe", score_delta, key_heads, preferred_element_type=jnp.float32)
            * score_scale
        )
        value_part = jnp.einsum(
            "hqk,qhe->khe", weights_low, delta_heads, preferred_element_type=jnp.float32
        )
        key_part = (
            jnp.einsum("hqk,qhe->khe", score_delta, query_heads, preferred_element_type=jnp.float32)
            * score_scale
        )
        rows_out = jnp.concatenate(
            [key_part.reshape(width_rows, D), value_part.reshape(width_rows, D)], axis=1
        )
        return (total, rows_out)

    query_total, pair_rows = lax.scan(
        joint_step,
        query_start,
        (
            jnp.arange(block_count, dtype=jnp.int32),
            every_key.reshape(block_count, width_rows, D),
            every_value.reshape(block_count, width_rows, D),
        ),
    )
    pair_rows = pair_rows.reshape(group_rows, 2 * D)
    both_sums = lax.psum_scatter(
        pair_rows.astype(jnp.bfloat16), "blk", scatter_dimension=0, tiled=True
    ).astype(jnp.float32)
    key_total = both_sums[:, :D]
    value_total = both_sums[:, D:]
    qkv_delta = jnp.concatenate(
        [query_total.reshape(local_rows, D), key_total, value_total], axis=1
    ).astype(jnp.bfloat16)
    qkv_term = outer(normed_low, qkv_delta)
    input_back, gain_one_term, bias_one_term = norm_one_pull(against(qkv_delta, full_qkv))
    input_grad = hidden_delta + input_back
    summed = (
        lax.psum_scatter(qkv_term, ("scene", "blk"), scatter_dimension=0, tiled=True),
        lax.psum_scatter(out_term, ("scene", "blk"), scatter_dimension=0, tiled=True),
        lax.psum_scatter(up_term, ("scene", "blk"), scatter_dimension=0, tiled=True),
        lax.psum_scatter(down_term, ("scene", "blk"), scatter_dimension=0, tiled=True),
        lax.psum_scatter(gain_one_term, ("scene", "blk"), scatter_dimension=0, tiled=True),
        lax.psum_scatter(bias_one_term, ("scene", "blk"), scatter_dimension=0, tiled=True),
        lax.psum_scatter(gain_two_term, ("scene", "blk"), scatter_dimension=0, tiled=True),
        lax.psum_scatter(bias_two_term, ("scene", "blk"), scatter_dimension=0, tiled=True),
    )
    return (
        result,
        input_grad,
        summed[0],
        summed[1],
        summed[2],
        summed[3],
        summed[4],
        summed[5],
        summed[6],
        summed[7],
    )


ALL = ("y", "x", "z", "c")
LANES = 128
BESIDE = {
    "up1": "tokens", "ogd": "tokens", "turned": "delta", "oups0": "units", "oups2": "units", "oups3": "units",
    "dz2": "sums", "dz3": "sums", "dz1": "back", "lo1": "middle", "lo2": "middle", "lo3": "last", "upa": "rest",
}
ROOT = math.sqrt(2.0 / math.pi)
CUBIC = 0.044715
FREE = pl.CostEstimate(flops=0, bytes_accessed=0, transcendentals=0)


def swap(values, axis, size, distance):
    return lax.ppermute(values, axis, [(i, i ^ distance) for i in range(size)])


def pair(values):
    return swap(values, "c", 2, 1)


def whole(shape):
    return pl.BlockSpec(shape, lambda *_: (0,) * len(shape))


def params(megabytes=60):
    return pltpu.CompilerParams(vmem_limit_bytes=megabytes * 1024 * 1024)


def three_parts(column, lane, first):
    high = column.astype(jnp.bfloat16).astype(jnp.float32)
    rest = column - high
    middle = rest.astype(jnp.bfloat16).astype(jnp.float32)
    last = rest - middle
    zero = jnp.zeros_like(last)
    return jnp.where(
        lane == first,
        high,
        jnp.where(lane == first + 1, middle, jnp.where(lane == first + 2, last, zero)),
    )


def attend_kernel(q_ref, k_ref, v_ref, *refs, chunk):
    low_ref, att_ref, rl_ref, p_ref, s0, s1, m0, m1, vt_ref, hold_ref = refs
    unit = pl.program_id(0)
    last = pl.num_programs(0) - 1
    rows = k_ref.shape[0]
    block = q_ref.shape[0]
    lane = lax.broadcasted_iota(jnp.int32, (1, LANES), 1)
    line = lax.broadcasted_iota(jnp.int32, (LANES, 1), 0)

    @pl.when(unit == 0)
    def _():
        turned = v_ref[...].astype(jnp.float32).T
        vt_ref[0] = jnp.where(line < HEAD_DIM, turned, 1.0).astype(jnp.bfloat16)
        vt_ref[1] = jnp.where(line >= HEAD_DIM, turned, 1.0).astype(jnp.bfloat16)

    def work(head, fresh, scores, old):
        mine = (lane < HEAD_DIM) if head == 0 else (lane >= HEAD_DIM)
        query = jnp.where(mine, q_ref[...].astype(jnp.float32) * HEAD_DIM ** (-0.5), 0.0).astype(jnp.bfloat16)
        top = jnp.full((8, block), -jnp.inf, jnp.float32)
        high = old[0][0:1, :] if old is not None else None
        mixed = jnp.zeros((LANES, block), jnp.float32)
        for first in range(0, rows, chunk):
            part = slice(first, first + chunk)
            if fresh is not None:
                got = against(k_ref[part, :], query)
                scores[part, :] = got
                top = jnp.maximum(top, jnp.max(got.reshape(chunk // 8, 8, block), axis=0))
            if old is not None:
                expo = jnp.exp(old[1][part, :] - high).astype(jnp.bfloat16)
                p_ref[0, part, :] = expo
                mixed += jnp.dot(vt_ref[1 - head, :, part], expo, preferred_element_type=jnp.float32)
        if fresh is not None:
            fresh[...] = jnp.broadcast_to(jnp.max(top, axis=0, keepdims=True), (8, block))
        return mixed.T if old is not None else None

    @pl.when(unit == 0)
    def _():
        work(0, m0, s0, None)

    @pl.when((unit > 0) & (unit % 2 == 1))
    def _():
        hold_ref[...] = work(1, m1, s1, (m0, s0))

    def finish(second):
        first = hold_ref[...]
        low_lane = lane < HEAD_DIM
        recip = 1.0 / jnp.where(low_lane, pltpu.roll(first, HEAD_DIM, 1), pltpu.roll(second, HEAD_DIM, 1))
        attended = jnp.where(low_lane, first, second) * recip
        att_ref[...] = attended
        rl_ref[...] = recip
        low_ref[...] = attended.astype(jnp.bfloat16)

    @pl.when((unit > 0) & (unit % 2 == 0) & (unit < last))
    def _():
        finish(work(0, m0, s0, (m1, s1)))

    @pl.when(unit == last)
    def _():
        finish(work(0, None, None, (m1, s1)))

def attend(qkv):
    rows = qkv.shape[0]
    block, chunk = 512, 256
    units = 2 * rows // block

    def new(u):
        return jnp.minimum(u, units - 1) // 2

    def old(u):
        return jnp.maximum(u - 1, 0)

    part = pl.BlockSpec((block, LANES), lambda u: (old(u) // 2, 0))
    return pl.pallas_call(
        functools.partial(attend_kernel, chunk=chunk),
        grid=(units + 1,),
        in_specs=[
            pl.BlockSpec((block, LANES), lambda u: (new(u), 0)),
            pl.BlockSpec((rows, LANES), lambda u: (0, 1)),
            pl.BlockSpec((rows, LANES), lambda u: (0, 2)),
        ],
        out_specs=[part, part, part, pl.BlockSpec((1, rows, block), lambda u: (old(u) % 2, 0, old(u) // 2))],
        out_shape=[
            jax.ShapeDtypeStruct((rows, LANES), jnp.bfloat16),
            jax.ShapeDtypeStruct((rows, LANES), jnp.float32),
            jax.ShapeDtypeStruct((rows, LANES), jnp.float32),
            jax.ShapeDtypeStruct((2, rows, rows), jnp.bfloat16),
        ],
        scratch_shapes=[pltpu.VMEM((rows, block), jnp.float32)] * 2
        + [pltpu.VMEM((8, block), jnp.float32)] * 2
        + [pltpu.VMEM((2, LANES, rows), jnp.bfloat16), pltpu.VMEM((block, LANES), jnp.float32)],
        compiler_params=params(34),
        cost_estimate=FREE,
    )(qkv, qkv, qkv)


def attend_back_kernel(q_ref, k_ref, v_ref, p_ref, att_ref, rl_ref, *refs, chunk, count):
    deltas, outs = refs[:count], refs[count : count + 2]
    va_ref, kt_ref, dq_acc, dk_acc, dv_acc, do_ref = refs[count + 2 :]
    head, step = pl.program_id(0), pl.program_id(1)
    rows = k_ref.shape[0]
    block = do_ref.shape[0]
    lane = lax.broadcasted_iota(jnp.int32, (1, LANES), 1)
    spare = jnp.where(head == 0, HEAD_DIM, 0)
    mine = (lane < spare) | (lane >= spare + HEAD_DIM)

    @pl.when((head == 0) & (step == 0))
    def _():
        kt_ref[...] = (k_ref[...].astype(jnp.float32) * HEAD_DIM ** (-0.5)).T.astype(jnp.bfloat16)

    @pl.when(step == 0)
    def _():
        ones = jnp.where(lane < spare + 3, 1.0, 0.0)
        va_ref[...] = jnp.where(mine, v_ref[...].astype(jnp.float32), ones).astype(jnp.bfloat16)
        dk_acc[head] = jnp.zeros((rows, LANES), jnp.float32)
        dv_acc[head] = jnp.zeros((rows, LANES), jnp.float32)

    for index, ref in enumerate(deltas):

        @pl.when(step == index)
        def _():
            do_ref[...] = ref[...]

    delta = (do_ref[...].astype(jnp.float32) * rl_ref[...]).astype(jnp.bfloat16).astype(jnp.float32)
    probe = jnp.sum(jnp.where(mine, delta * att_ref[...], 0.0), axis=1, keepdims=True)
    own_delta = jnp.where(mine, delta, three_parts(-probe, lane, spare)).astype(jnp.bfloat16)
    query = (q_ref[...].astype(jnp.float32) * HEAD_DIM ** (-0.5)).astype(jnp.bfloat16)
    total = jnp.zeros((LANES, block), jnp.float32)
    for first in range(0, rows, chunk):
        part = slice(first, first + chunk)
        expo = p_ref[0, part, :]
        score_delta = (expo.astype(jnp.float32) * against(va_ref[part, :], own_delta)).astype(jnp.bfloat16)
        dv_acc[head, part, :] += jnp.dot(expo, own_delta, preferred_element_type=jnp.float32)
        dk_acc[head, part, :] += jnp.dot(score_delta, query, preferred_element_type=jnp.float32)
        total += jnp.dot(kt_ref[:, part], score_delta, preferred_element_type=jnp.float32)
    query_delta = total.T
    place = pl.ds(pl.multiple_of(step * block, block), block)

    @pl.when(head == 0)
    def _():
        dq_acc[place, :] = query_delta

    half = block // 2

    @pl.when(head == 1)
    def _():
        both = jnp.where(lane < HEAD_DIM, dq_acc[place, :], query_delta).astype(jnp.bfloat16)
        for side, ref in enumerate(outs):
            ref[step, :, :LANES] = both[side * half : (side + 1) * half]

    @pl.when((head == 1) & (step == pl.num_programs(1) - 1))
    def _():
        for index in range(count):
            for side, ref in enumerate(outs):
                part = slice(index * block + side * half, index * block + (side + 1) * half)
                for kind, acc in ((1, dk_acc), (2, dv_acc)):
                    own = jnp.where(lane < HEAD_DIM, acc[0, part, :], acc[1, part, :]).astype(jnp.bfloat16)
                    ref[index, :, kind * LANES : (kind + 1) * LANES] = own


def attend_back(qkv, probs, deltas, attended, recip):
    rows = qkv.shape[0]
    count = len(deltas)
    block, chunk = rows // count, 512
    part = pl.BlockSpec((block, LANES), lambda h, i: (i, 0))
    return pl.pallas_call(
        functools.partial(attend_back_kernel, chunk=chunk, count=count),
        grid=(2, count),
        in_specs=[
            part,
            pl.BlockSpec((rows, LANES), lambda h, i: (0, 1)),
            pl.BlockSpec((rows, LANES), lambda h, i: (0, 2)),
            pl.BlockSpec((1, rows, block), lambda h, i: (h, 0, i)),
            part,
            part,
        ]
        + [whole((block, LANES))] * count,
        out_specs=[whole((count, block // 2, 3 * LANES))] * 2,
        out_shape=[jax.ShapeDtypeStruct((count, block // 2, 3 * LANES), jnp.bfloat16)] * 2,
        scratch_shapes=[
            pltpu.VMEM((rows, LANES), jnp.bfloat16),
            pltpu.VMEM((LANES, rows), jnp.bfloat16),
            pltpu.VMEM((rows, LANES), jnp.float32),
            pltpu.VMEM((2, rows, LANES), jnp.float32),
            pltpu.VMEM((2, rows, LANES), jnp.float32),
            pltpu.VMEM((block, LANES), jnp.bfloat16),
        ],
        compiler_params=params(36),
        cost_estimate=FREE,
    )(qkv, qkv, qkv, probs, attended, recip, *deltas)


def qkv_kernel(place_ref, *refs):
    pieces, weights = refs[:10], refs[10:14]
    qkv_ref, normed_ref, gains_ref, turned_ref, own_ref, table_ref = refs[14:]
    depth, share = weights[0].shape[0], weights[0].shape[1] // 2

    @pl.when(pl.program_id(0) == 0)
    def _():
        device = place_ref[0]
        for far, part in enumerate(weights):
            for near in range(depth):
                for core in range(2):
                    owner = device ^ (far * 2 * depth + near * 2 + core)
                    row = pl.multiple_of(owner * share, share)
                    first = core * share
                    own_ref[pl.ds(row, share), :] = part[near, first : first + share, : 3 * LANES]
                    table = part[near, first : first + 16, 3 * LANES :].astype(jnp.float32)
                    table_ref[pl.ds(owner, 1), :] = table[0:1]
        devices = table_ref.shape[0]
        table = table_ref[...].astype(jnp.bfloat16)
        row = lax.broadcasted_iota(jnp.int32, (LANES, D), 0)
        col = lax.broadcasted_iota(jnp.int32, (LANES, D), 1)
        owner = lax.broadcasted_iota(jnp.int32, (devices, D), 0)
        own_col = lax.broadcasted_iota(jnp.int32, (devices, D), 1) // share
        for kind in range(4):
            spread = jnp.where(row == kind * share + col % share, 1.0, 0.0).astype(jnp.bfloat16)
            wide = jnp.dot(table, spread, preferred_element_type=jnp.float32)
            gains_ref[kind : kind + 1, :] = jnp.sum(jnp.where(owner == own_col, wide, 0.0), axis=0, keepdims=True)
        gains_ref[4:8, :] = jnp.zeros((4, D), jnp.float32)
        turned_ref[...] = own_ref[...].astype(jnp.float32).T.astype(jnp.bfloat16)

    gain, bias = gains_ref[0:1, :], gains_ref[1:2, :]
    for index in range(8):
        tokens = pieces[index][...].astype(jnp.float32)
        if index >= 6:
            tokens = tokens + pieces[index + 2][...].astype(jnp.float32)
        normal, _ = moments(tokens)
        normed = (normal * gain + bias).astype(jnp.bfloat16)
        normed_ref[index] = normed
        qkv_ref[index] = jnp.dot(normed, own_ref[...], preferred_element_type=jnp.float32).astype(jnp.bfloat16)


def project(device, pieces, weights):
    rows = pieces[0].shape[0]
    steps = 2
    block = rows // steps
    piece = pl.BlockSpec((block, D), lambda i, place: (i, 0))
    part = pl.BlockSpec(weights[0].shape, lambda i, place: (0, 0, 0))
    grid_spec = pltpu.PrefetchScalarGridSpec(
        num_scalar_prefetch=1,
        grid=(steps,),
        in_specs=[piece] * 10 + [part] * 4,
        out_specs=[
            pl.BlockSpec((8, block, 3 * LANES), lambda i, place: (0, i, 0)),
            pl.BlockSpec((8, block, D), lambda i, place: (0, i, 0)),
            pl.BlockSpec((8, D), lambda i, place: (0, 0)),
            pl.BlockSpec((3 * LANES, D), lambda i, place: (0, 0)),
        ],
        scratch_shapes=[
            pltpu.VMEM((D, 3 * LANES), jnp.bfloat16),
            pltpu.VMEM((32, LANES), jnp.float32),
        ],
    )
    qkv, normed, gains, turned = pl.pallas_call(
        qkv_kernel,
        grid_spec=grid_spec,
        out_shape=[
            jax.ShapeDtypeStruct((8, rows, 3 * LANES), jnp.bfloat16),
            jax.ShapeDtypeStruct((8, rows, D), jnp.bfloat16),
            jax.ShapeDtypeStruct((8, D), jnp.float32),
            jax.ShapeDtypeStruct((3 * LANES, D), jnp.bfloat16),
        ],
        compiler_params=params(60),
        cost_estimate=FREE,
    )(device.reshape(1).astype(jnp.int32), *pieces, *weights)
    return qkv.reshape(8 * rows, 3 * LANES), normed.reshape(8 * rows, D), gains, turned


def mlp_kernel(place_ref, *refs):
    device, own_z = place_ref[0], place_ref[1]
    nts, ogs, refs = refs[:4], refs[4:8], refs[8:]
    ups, other_ups, downs, other_downs = refs[:4], refs[4:8], refs[8:12], refs[12:16]
    act_ref, ud_ref, keep_ref, one_ref, two_ref, three_ref, down_ref, down_keep, down_send, up_ref, down_acc = refs[16:]
    depth, share, wide = len(ups), ups[0].shape[1] // 2, ups[0].shape[2]

    @pl.when(pl.program_id(0) == 0)
    def _():
        slab = downs[0].shape[0]
        for side, parts in enumerate((ups, other_ups)):
            for near, part in enumerate(parts):
                for far in range(part.shape[0]):
                    for core in range(2):
                        owner = far * 2 * depth + ((device % (2 * depth)) ^ (near * 2 + (core ^ side)))
                        row = pl.multiple_of(owner * share, share)
                        cols = slice(side * wide, (side + 1) * wide)
                        up_ref[pl.ds(row, share), cols] = part[far, core * share : (core + 1) * share, :]
        for side, parts in enumerate((downs, other_downs)):
            for near, part in enumerate(parts):
                row = pl.multiple_of(side * wide + (own_z ^ near) * slab, slab)
                down_ref[pl.ds(row, slab), :] = part[...]

    rows = nts[0].shape[0]
    normed = jnp.concatenate([ref[...] for ref in nts])
    grads = jnp.concatenate([ref[...] for ref in ogs])
    back = jnp.zeros((4 * rows, D), jnp.float32)
    for side in range(2):
        cols = slice(side * wide, (side + 1) * wide)
        upward = jnp.dot(normed, up_ref[:, cols], preferred_element_type=jnp.float32)
        square = upward * upward
        curve = jnp.tanh(ROOT * upward * (1.0 + CUBIC * square))
        active = (0.5 * upward * (1.0 + curve)).astype(jnp.bfloat16)
        slope = 0.5 * (1.0 + curve) + 0.5 * upward * (1.0 - curve * curve) * (ROOT * (1.0 + 3.0 * CUBIC * square))
        delta = (against(grads, down_ref[cols, :]) * slope).astype(jnp.bfloat16)
        back += against(delta, up_ref[:, cols])
        down_acc[cols, :] = outer(active, grads)
        for index in range(4):
            part = slice(index * rows, (index + 1) * rows)
            act_ref[index, :, cols] = active[part]
            ud_ref[index, :, cols] = delta[part]
    keep_ref[...] = back[:rows]
    for index, to in enumerate((one_ref, two_ref, three_ref)):
        to[...] = back[(index + 1) * rows : (index + 2) * rows].astype(jnp.bfloat16)

    slab = down_keep.shape[1]
    for side, to in enumerate((down_keep, down_send)):
        for near in range(depth):
            first = side * wide + near * slab
            to[near ^ own_z] = down_acc[first : first + slab, :].astype(jnp.bfloat16)


def mlp(place, normed, grads, ups, other_ups, downs, other_downs):
    rows = normed[0].shape[0]
    steps = 1
    block = rows // steps
    wide = 2 * ups[0].shape[2]
    low = jnp.bfloat16
    piece = pl.BlockSpec((block, D), lambda i, place: (i, 0))
    weights = (*ups, *other_ups, *downs, *other_downs)
    down_shape = (len(downs), *downs[0].shape)

    def full(shape):
        return pl.BlockSpec(shape, lambda i, place: (0,) * len(shape))

    units = pl.BlockSpec((4, block, wide), lambda i, place: (0, i, 0))
    grid_spec = pltpu.PrefetchScalarGridSpec(
        num_scalar_prefetch=1,
        grid=(steps,),
        in_specs=[piece] * 8 + [full(part.shape) for part in weights],
        out_specs=[units, units, piece, piece, piece, piece, full((wide, D))] + [full(down_shape)] * 2,
        scratch_shapes=[pltpu.VMEM((D, wide), low), pltpu.VMEM((wide, D), jnp.float32)],
    )
    return pl.pallas_call(
        mlp_kernel,
        grid_spec=grid_spec,
        out_shape=[
            jax.ShapeDtypeStruct((4, rows, wide), low),
            jax.ShapeDtypeStruct((4, rows, wide), low),
            jax.ShapeDtypeStruct((rows, D), jnp.float32),
            jax.ShapeDtypeStruct((rows, D), low),
            jax.ShapeDtypeStruct((rows, D), low),
            jax.ShapeDtypeStruct((rows, D), low),
            jax.ShapeDtypeStruct((wide, D), low),
        ]
        + [jax.ShapeDtypeStruct(down_shape, low)] * 2,
        compiler_params=params(40),
        cost_estimate=FREE,
    )(place, *normed, *grads, *weights)


def mlp_grads_kernel(place_ref, *refs):
    nts, refs = refs[:4], refs[4:]
    act_ref, ud_ref, down_ref, keep_ref, one_ref, two_ref, three_ref, up_keep, up_send, up_acc = refs
    step = pl.program_id(0)
    rows = nts[0].shape[0]
    normed = jnp.concatenate([ref[...] for ref in nts])
    wide = act_ref.shape[2]
    active = act_ref[...].reshape(4 * rows, wide)
    up = outer(normed, ud_ref[...].reshape(4 * rows, wide))
    out = jnp.dot(active, down_ref[...], preferred_element_type=jnp.float32)
    keep_ref[...] = out[:rows]
    for index, to in enumerate((one_ref, two_ref, three_ref)):
        to[...] = out[(index + 1) * rows : (index + 2) * rows].astype(jnp.bfloat16)

    @pl.when(step == 0)
    def _():
        up_acc[...] = up

    @pl.when(step > 0)
    def _():
        up_acc[...] += up

    @pl.when(step == pl.num_programs(0) - 1)
    def _():
        depth, _, share = up_keep.shape[:3]
        half = wide // 2
        for side, to in enumerate((up_keep, up_send)):
            for near in range(depth):
                for far in range(4):
                    first = (far * depth + near) * share
                    part = up_acc[first : first + share, side * half : (side + 1) * half]
                    to[near ^ place_ref[0], far] = part.astype(jnp.bfloat16)


def mlp_grads(place, normed, active, delta, w_down, depth):
    rows = normed[0].shape[0]
    steps = 4
    block = rows // steps
    wide = active.shape[2]
    low = jnp.bfloat16
    piece = pl.BlockSpec((block, D), lambda i, place: (i, 0))
    units = pl.BlockSpec((4, block, wide), lambda i, place: (0, i, 0))

    def full(shape):
        return pl.BlockSpec(shape, lambda i, place: (0,) * len(shape))

    shapes = [(depth, 4, D // (4 * depth), wide // 2)] * 2
    grid_spec = pltpu.PrefetchScalarGridSpec(
        num_scalar_prefetch=1,
        grid=(steps,),
        in_specs=[piece] * 4 + [units] * 2 + [full(w_down.shape)],
        out_specs=[piece] * 4 + [full(shape) for shape in shapes],
        scratch_shapes=[pltpu.VMEM((D, wide), jnp.float32)],
    )
    return pl.pallas_call(
        mlp_grads_kernel,
        grid_spec=grid_spec,
        out_shape=[jax.ShapeDtypeStruct((rows, D), jnp.float32)]
        + [jax.ShapeDtypeStruct((rows, D), low)] * 3
        + [jax.ShapeDtypeStruct(shape, low) for shape in shapes],
        compiler_params=params(36),
        cost_estimate=FREE,
    )(place, *normed, active, delta, w_down)


def prepare_kernel(core_ref, qkv_ref, up_ref, out_ref, gains_ref, keep_ref, send_ref):
    core = core_ref[0]
    chips = up_ref.shape[1] // (2 * LANES)
    half = out_ref.shape[1] // 2
    depth = chips // 4
    for side, to in ((core, keep_ref), (1 - core, send_ref)):
        for chip in range(chips):
            cols = pl.ds(pl.multiple_of((2 * chip + side) * LANES, LANES), LANES)
            to[:, chip * LANES : (chip + 1) * LANES] = up_ref[:, cols]
        first = chips * LANES
        to[:, first : first + half] = out_ref[:, pl.ds(pl.multiple_of(side * half, half), half)]
        first += half
        for near in range(depth):
            for kind in range(3):
                cols = pl.ds(pl.multiple_of(kind * D + (2 * near + side) * LANES, LANES), LANES)
                to[:, first : first + LANES] = qkv_ref[:, cols]
                first += LANES
        to[:, first:] = jnp.broadcast_to(gains_ref[...], (to.shape[0], LANES))


def prepare(core, w_qkv, w_up, w_out, gains):
    share = w_qkv.shape[0]
    wide = (w_up.shape[1] + w_out.shape[1] + w_qkv.shape[1]) // 2 + LANES
    return pl.pallas_call(
        prepare_kernel,
        in_specs=[pl.BlockSpec(memory_space=pltpu.SMEM)]
        + [whole(array.shape) for array in (w_qkv, w_up, w_out, gains)],
        out_specs=[whole((share, wide))] * 2,
        out_shape=[jax.ShapeDtypeStruct((share, wide), jnp.bfloat16)] * 2,
        compiler_params=params(8),
        cost_estimate=FREE,
    )(core, w_qkv, w_up, w_out, gains)


def compose_kernel(place_ref, keep_ref, got_ref, up_ref, *parts):
    own_z = place_ref[0]
    share = keep_ref.shape[0]
    depth = len(parts)
    wide = up_ref.shape[2]
    half = D // 2
    heads = 4 * wide + half
    for side, ref in ((0, keep_ref), (1, got_ref)):
        rows = slice(side * share, (side + 1) * share)
        for far in range(4):
            up_ref[far, rows, :] = ref[:, far * wide : (far + 1) * wide]
        for far, part in enumerate(parts):
            first = heads + (own_z ^ far) * 3 * LANES
            part[rows, :half] = ref[:, 4 * wide : heads]
            part[rows, half : half + 3 * LANES] = ref[:, pl.ds(pl.multiple_of(first, LANES), 3 * LANES)]
            part[rows, half + 3 * LANES :] = ref[:, heads + depth * 3 * LANES :]


def compose(place, keep, got, depth):
    share = keep.shape[0]
    shapes = [(4, 2 * share, D // 2)] + [(2 * share, D)] * depth
    ups, *parts = pl.pallas_call(
        compose_kernel,
        in_specs=[pl.BlockSpec(memory_space=pltpu.SMEM), whole(keep.shape), whole(got.shape)],
        out_specs=[whole(shape) for shape in shapes],
        out_shape=[jax.ShapeDtypeStruct(shape, jnp.bfloat16) for shape in shapes],
        compiler_params=params(8),
        cost_estimate=FREE,
    )(place, keep, got)
    return ups, parts


def arrange_kernel(place_ref, own_ref, other_ref, near_ref):
    device, block, core = place_ref[0], place_ref[1], place_ref[2]
    planes, depth, share, half = own_ref.shape
    share //= 2
    count = near_ref.shape[0]
    per_block = LANES // share
    for ref, swapped, col in ((own_ref, 0, core), (other_ref, 1, 1 - core)):
        cols = pl.ds(pl.multiple_of(col * half, half), half)
        for far in range(planes):
            for near in range(depth):
                for side in range(2):
                    owner = device ^ ((far * depth + near) * 2 + (side ^ swapped))
                    heads = (owner // per_block) ^ block
                    to = (heads % 2) * (count // 2) + heads // 2
                    row = pl.ds(pl.multiple_of((owner % per_block) * share, share), share)
                    near_ref[to, row, cols] = ref[far, near, side * share : (side + 1) * share, :]


def arrange(place, own, other):
    shape = (D // LANES, LANES, D)
    return pl.pallas_call(
        arrange_kernel,
        in_specs=[pl.BlockSpec(memory_space=pltpu.SMEM), whole(own.shape), whole(other.shape)],
        out_specs=whole(shape),
        out_shape=jax.ShapeDtypeStruct(shape, jnp.bfloat16),
        compiler_params=params(12),
        cost_estimate=FREE,
    )(place, own, other)


def collect_kernel(place_ref, *refs):
    parts, outs = refs[:4], refs[4:]
    total = sum(part[...].astype(jnp.float32) for part in parts)
    depth, (share, wide) = len(outs), outs[0].shape
    qkv = 3 * LANES
    tall = depth * share
    for natural in range(depth):
        part = total[natural * share : (natural + 1) * share, :].astype(jnp.bfloat16)
        for far, out_ref in enumerate(outs):

            @pl.when((place_ref[0] ^ far) == natural)
            def _():
                out_ref[:, :qkv] = part[:, :qkv]
                out_ref[:, qkv + LANES :] = part[:, qkv:]

    exact = total[tall : tall + 4, :tall] + total[tall + 4 : tall + 8, :tall]
    high = exact.astype(jnp.bfloat16).astype(jnp.float32)
    parts = jnp.concatenate([high, exact - high], axis=0)
    parts = jnp.concatenate([parts[:, :LANES], parts[:, LANES:]], axis=0).astype(jnp.bfloat16)
    for out_ref in outs:
        out_ref[:16, qkv : qkv + LANES] = parts
        out_ref[16:, qkv : qkv + LANES] = jnp.zeros((share - 16, LANES), jnp.bfloat16)


def collect(place, parts, depth):
    rows, wide = parts[0].shape
    shape = ((rows - 16) // depth, wide + LANES)
    return pl.pallas_call(
        collect_kernel,
        in_specs=[pl.BlockSpec(memory_space=pltpu.SMEM)] + [whole(part.shape) for part in parts],
        out_specs=[whole(shape)] * depth,
        out_shape=[jax.ShapeDtypeStruct(shape, jnp.bfloat16)] * depth,
        compiler_params=params(8),
        cost_estimate=FREE,
    )(place, *parts)


def divide_kernel(place_ref, *refs):
    parts, (own_ref, sent_ref, own_out, sent_out) = refs[:-4], refs[-4:]
    core = place_ref[0]
    qkv = 3 * LANES
    share = own_ref.shape[1]
    depth = len(parts)
    own_rows = pl.ds(pl.multiple_of(core * share, share), share)
    other_rows = pl.ds(pl.multiple_of((1 - core) * share, share), share)
    for far, part in enumerate(parts):
        own_ref[far] = part[own_rows, : 3 * LANES]
        sent_ref[far] = part[other_rows, : 3 * LANES]
    for rows, ref in ((own_rows, own_out), (other_rows, sent_out)):
        ref[...] = sum(part[rows, qkv + LANES :].astype(jnp.float32) for part in parts)
    vectors = sum(part[0:16, qkv : qkv + LANES].astype(jnp.float32) for part in parts)
    high = vectors.astype(jnp.bfloat16).astype(jnp.float32)
    zero = jnp.zeros((16, LANES), jnp.float32)
    both = jnp.concatenate([high, vectors - high, zero], axis=1).astype(jnp.bfloat16)
    for ref in (own_ref, sent_ref):
        ref[depth, :16, :] = both
        ref[depth, 16:, :] = jnp.zeros((share - 16, 3 * LANES), jnp.bfloat16)


def divide(core, parts):
    share = parts[0].shape[0] // 2
    shapes = [jax.ShapeDtypeStruct((len(parts) + 1, share, 3 * LANES), jnp.bfloat16)] * 2
    shapes += [jax.ShapeDtypeStruct((share, parts[0].shape[1] - 4 * LANES), jnp.float32)] * 2
    return pl.pallas_call(
        divide_kernel,
        in_specs=[pl.BlockSpec(memory_space=pltpu.SMEM)] + [whole(part.shape) for part in parts],
        out_specs=[whole(shape.shape) for shape in shapes],
        out_shape=shapes,
        compiler_params=params(8),
        cost_estimate=FREE,
    )(core, *parts)


def finish_kernel(place_ref, qkv_ref, got_qkv_ref, own_out, got_out, grad_ref, vector_ref, out_ref):
    block, core = place_ref[0], place_ref[1]
    half = out_ref.shape[1] // 2
    out_ref[:, pl.ds(pl.multiple_of(core * half, half), half)] = own_out[...]
    out_ref[:, pl.ds(pl.multiple_of((1 - core) * half, half), half)] = got_out[...]
    depth = qkv_ref.shape[0] - 1
    for near, qkv in enumerate((qkv_ref, got_qkv_ref)):
        for far in range(depth):
            first = (block ^ (2 * far + near)) * LANES
            for kind in range(3):
                to = pl.ds(pl.multiple_of(kind * D + first, LANES), LANES)
                grad_ref[:, to] = qkv[far, :, kind * LANES : (kind + 1) * LANES].astype(jnp.float32)
    both = qkv_ref[depth, :16, :].astype(jnp.float32) + got_qkv_ref[depth, :16, :].astype(jnp.float32)
    exact = both[:, :LANES] + both[:, LANES : 2 * LANES]
    vector_ref[:, :LANES] = exact[0:4] + exact[4:8]
    vector_ref[:, LANES:] = exact[8:12] + exact[12:16]


def finish(place, qkv, got_qkv, own_out, got_out):
    share = qkv.shape[1]
    shapes = [(share, 3 * D), (4, 2 * LANES), (share, D)]
    arrays = (qkv, got_qkv, own_out, got_out)
    return pl.pallas_call(
        finish_kernel,
        in_specs=[pl.BlockSpec(memory_space=pltpu.SMEM)] + [whole(array.shape) for array in arrays],
        out_specs=[whole(shape) for shape in shapes],
        out_shape=[jax.ShapeDtypeStruct(shape, jnp.float32) for shape in shapes],
        compiler_params=params(8),
        cost_estimate=FREE,
    )(place, *arrays)


def finish_up_kernel(core_ref, own_ref, got_ref, up_ref):
    depth = own_ref.shape[2] // LANES
    for near, ref in enumerate((own_ref, got_ref)):
        side = core_ref[0] ^ near
        for far in range(4):
            for chip in range(depth):
                to = pl.ds(pl.multiple_of(((far * depth + chip) * 2 + side) * LANES, LANES), LANES)
                up_ref[:, to] = ref[far, :, chip * LANES : (chip + 1) * LANES].astype(jnp.float32)


def finish_up(core, own, got):
    shape = (own.shape[1], 4 * D)
    return pl.pallas_call(
        finish_up_kernel,
        in_specs=[pl.BlockSpec(memory_space=pltpu.SMEM), whole(own.shape), whole(got.shape)],
        out_specs=whole(shape),
        out_shape=jax.ShapeDtypeStruct(shape, jnp.float32),
        compiler_params=params(8),
        cost_estimate=FREE,
    )(core, own, got)


def turned(values):
    return values.astype(jnp.float32).T.astype(jnp.bfloat16)


def out_project_kernel(gains_ref, tokens_ref, near_ref, *refs):
    heads, (hidden_ref, normed_ref) = refs[:-2], refs[-2:]
    rows = tokens_ref.shape[0]
    depth = len(heads) // 2
    parts = [ref[:rows, :] if far < depth else ref[rows:, :] for far, ref in enumerate(heads)]
    hidden = tokens_ref[...].astype(jnp.float32) + jnp.dot(
        jnp.concatenate(parts, axis=1), near_ref[...].reshape(D, D), preferred_element_type=jnp.float32
    )
    normal, _ = moments(hidden)
    hidden_ref[...] = hidden
    normed_ref[...] = (normal * gains_ref[2:3, :] + gains_ref[3:4, :]).astype(jnp.bfloat16)


def out_project(gains, tokens, near_out, heads):
    arrays = (gains, tokens, near_out, *heads)
    return pl.pallas_call(
        out_project_kernel,
        in_specs=[whole(array.shape) for array in arrays],
        out_specs=[whole(tokens.shape)] * 2,
        out_shape=[
            jax.ShapeDtypeStruct(tokens.shape, jnp.float32),
            jax.ShapeDtypeStruct(tokens.shape, jnp.bfloat16),
        ],
        compiler_params=params(12),
        cost_estimate=FREE,
    )(*arrays)


def norm_two_kernel(gains_ref, hidden_ref, grad_ref, own_ref, *refs):
    sides, (delta_ref, low_ref, sums_ref) = refs[:-3], refs[-3:]
    delta = own_ref[...]
    for side in sides:
        delta += side[...].astype(jnp.float32)
    normal, scale = moments(hidden_ref[...])
    sums = jnp.concatenate(
        [jnp.sum(delta * normal, axis=0, keepdims=True), jnp.sum(delta, axis=0, keepdims=True)], axis=0
    )

    @pl.when(pl.program_id(0) == 0)
    def _():
        sums_ref[...] = sums

    @pl.when(pl.program_id(0) > 0)
    def _():
        sums_ref[...] += sums

    hidden_delta = grad_ref[...].astype(jnp.float32) + norm_back(delta, gains_ref[2:3, :], normal, scale)
    delta_ref[...] = hidden_delta
    low_ref[...] = hidden_delta.astype(jnp.bfloat16)


def by_rows(shape, steps):
    return pl.BlockSpec((shape[0] // steps, shape[1]), lambda i: (i, 0))


def norm_two(gains, hidden, out_grad, own, sides):
    arrays = (hidden, out_grad, own, *sides)
    piece = by_rows(hidden.shape, 4)
    return pl.pallas_call(
        norm_two_kernel,
        grid=(4,),
        in_specs=[whole(gains.shape)] + [piece] * len(arrays),
        out_specs=[piece, piece, whole((2, D))],
        out_shape=[
            jax.ShapeDtypeStruct(hidden.shape, jnp.float32),
            jax.ShapeDtypeStruct(hidden.shape, jnp.bfloat16),
            jax.ShapeDtypeStruct((2, D), jnp.float32),
        ],
        compiler_params=params(10),
        cost_estimate=FREE,
    )(gains, *arrays)


def norm_one_kernel(gains_ref, tokens_ref, hidden_ref, own_ref, *refs):
    sides, out_ref = refs[:-1], refs[-1]
    delta = own_ref[...]
    for side in sides:
        delta += side[...].astype(jnp.float32)
    normal, scale = moments(tokens_ref[...].astype(jnp.float32))
    out_ref[...] = hidden_ref[...] + norm_back(delta, gains_ref[0:1, :], normal, scale)


def norm_one(gains, tokens, hidden_delta, own, sides):
    arrays = (tokens, hidden_delta, own, *sides)
    piece = by_rows(tokens.shape, 4)
    return pl.pallas_call(
        norm_one_kernel,
        grid=(4,),
        in_specs=[whole(gains.shape)] + [piece] * len(arrays),
        out_specs=piece,
        out_shape=jax.ShapeDtypeStruct(tokens.shape, jnp.float32),
        compiler_params=params(10),
        cost_estimate=FREE,
    )(gains, *arrays)


def out_grads_kernel(place_ref, cols_ref, *refs):
    heads, outs, heads_t = refs[:-5], refs[-5:-1], refs[-1]
    plane, own_block = place_ref[0], place_ref[1]
    depth = len(heads) // 2
    rows = cols_ref.shape[0] // 2
    for far, ref in enumerate(heads):
        core, near = far // depth, far % depth
        row = pl.multiple_of((own_block ^ (2 * near + core)) * LANES, LANES)
        part = ref[...] if core == 0 else jnp.concatenate([ref[rows:, :], ref[:rows, :]])
        heads_t[pl.ds(row, LANES), :] = turned(part)
    tall = D // 4
    for far, out in enumerate(outs):
        row = pl.multiple_of((plane ^ far) * tall, tall)
        left = heads_t[pl.ds(row, tall), :]
        out[:tall, :] = jnp.dot(left, cols_ref[...], preferred_element_type=jnp.float32).astype(jnp.bfloat16)
        out[tall:, :] = jnp.zeros((out.shape[0] - tall, out.shape[1]), jnp.bfloat16)


def out_grads(place, heads, hidden_both):
    rows = hidden_both.shape[0]
    low = jnp.bfloat16

    def full(shape):
        return pl.BlockSpec(shape, lambda i, place: (0,) * len(shape))

    shape = (D // 4 + 16, D // 2)
    grid_spec = pltpu.PrefetchScalarGridSpec(
        num_scalar_prefetch=1,
        grid=(1,),
        in_specs=[pl.BlockSpec((rows, D // 2), lambda i, place: (0, place[2]))]
        + [full(part.shape) for part in heads],
        out_specs=[full(shape)] * 4,
        scratch_shapes=[pltpu.VMEM((D, rows), low)],
    )
    return pl.pallas_call(
        out_grads_kernel,
        grid_spec=grid_spec,
        out_shape=[jax.ShapeDtypeStruct(shape, low)] * 4,
        compiler_params=params(12),
        cost_estimate=FREE,
    )(place, hidden_both, *heads)


def back_project_kernel(own_ref, other_ref, own_weights, other_weights, keep_ref, *outs):
    for far in range(own_ref.shape[0]):
        total = jnp.dot(own_ref[far], own_weights[...], preferred_element_type=jnp.float32)
        total += jnp.dot(other_ref[far], other_weights[...], preferred_element_type=jnp.float32)
        if far == 0:
            keep_ref[...] = total
        else:
            outs[far - 1][...] = total.astype(jnp.bfloat16)


def back_project(own, other, own_weights, other_weights):
    count, rows, _ = own.shape
    arrays = (own, other, own_weights, other_weights)
    return pl.pallas_call(
        back_project_kernel,
        in_specs=[whole(array.shape) for array in arrays],
        out_specs=[whole((rows, D))] * count,
        out_shape=[jax.ShapeDtypeStruct((rows, D), jnp.float32)]
        + [jax.ShapeDtypeStruct((rows, D), jnp.bfloat16)] * (count - 1),
        compiler_params=params(24),
        cost_estimate=FREE,
    )(*arrays)


def qkv_grad_kernel(place_ref, nm_ref, turned_ref, gains_ref, two_ref, *refs):
    deltas, terms, outs, (total, sums) = refs[:-10], refs[-10:-6], refs[-6:-2], refs[-2:]
    count, rows, _ = deltas[0].shape
    ones = jnp.ones((rows, LANES), jnp.bfloat16)
    for index in range(2 * count):
        delta = deltas[index % 2][index // 2]
        part = outer(delta, nm_ref[index * rows : (index + 1) * rows, :])
        column = outer(delta, ones)
        if index == 0:
            total[...] = part
            sums[...] = column
        else:
            total[...] += part
            sums[...] += column
    gain, bias = gains_ref[0:1, :], gains_ref[1:2, :]
    weights = turned_ref[...].astype(jnp.float32)
    column = sums[:, 0:1]
    bias_part = jnp.sum(weights * column, axis=0, keepdims=True)
    gain_part = (jnp.sum(weights * total[...], axis=0, keepdims=True) - bias * bias_part) / gain
    exact = jnp.concatenate([gain_part, bias_part, two_ref[0:2, :]], axis=0)
    high = exact.astype(jnp.bfloat16).astype(jnp.float32)
    parts = jnp.concatenate([high, exact - high, jnp.zeros((8, D), jnp.float32)], axis=0)
    total_parts = parts.astype(jnp.bfloat16)
    tall = D // 4
    for natural in range(4):
        for far in range(4):

            @pl.when((place_ref[0] ^ far) == natural)
            def _():
                cols = slice(natural * tall, (natural + 1) * tall)
                outs[far][:tall, : 3 * LANES] = total[:, cols].T.astype(jnp.bfloat16)
                outs[far][tall:, :tall] = total_parts[:, cols]
    for term, out in zip(terms, outs):
        wide = out.shape[1] - term.shape[1]
        out[:, wide:] = term[...]
        out[D // 4 :, D // 4 : wide] = jnp.zeros((16, wide - D // 4), jnp.bfloat16)


def qkv_gradient(place, deltas, normed, turned_weights, gains, two, terms):
    shape = (D // 4 + 16, 3 * LANES + terms[0].shape[1])
    arrays = (normed, turned_weights, gains, two, *deltas, *terms)
    return pl.pallas_call(
        qkv_grad_kernel,
        in_specs=[pl.BlockSpec(memory_space=pltpu.SMEM)] + [whole(array.shape) for array in arrays],
        out_specs=[whole(shape)] * 4,
        out_shape=[jax.ShapeDtypeStruct(shape, jnp.bfloat16)] * 4,
        scratch_shapes=[pltpu.VMEM((3 * LANES, D), jnp.float32), pltpu.VMEM((3 * LANES, LANES), jnp.float32)],
        compiler_params=params(28),
        cost_estimate=FREE,
    )(place, *arrays)


def moments(values):
    centred = values - jnp.mean(values, axis=1, keepdims=True)
    scale = lax.rsqrt(jnp.mean(centred * centred, axis=1, keepdims=True) + EPSILON)
    return centred * scale, scale


def norm_back(delta, gain, normal, scale):
    e = delta * gain
    return scale * (
        e - jnp.mean(e, axis=1, keepdims=True) - normal * jnp.mean(e * normal, axis=1, keepdims=True)
    )


def added(keep, got):
    return (keep.astype(jnp.float32) + got.astype(jnp.float32)).astype(jnp.bfloat16)


def on_planes(
    tokens_in,
    out_grad,
    w_qkv,
    w_out,
    w_up,
    w_down,
    norm1_gain,
    norm1_bias,
    norm2_gain,
    norm2_bias,
):
    depth = lax.axis_size("z")
    rows = tokens_in.shape[0]
    share = w_qkv.shape[0]
    low = jnp.bfloat16
    places = {axis: lax.axis_index(axis) for axis in ALL}
    core = places["c"]
    block = 2 * places["z"] + core
    device = ((2 * places["y"] + places["x"]) * depth + places["z"]) * 2 + core

    hold = lax.optimization_barrier
    plane = 2 * places["y"] + places["x"]

    def index_of(*values):
        return jnp.stack(values).astype(jnp.int32)

    def along_z(part, far):
        return swap(part, "z", depth, far)

    def middle_z(part):
        return lax.ppermute(part, "z", [(1, 2), (2, 1)])

    def over_plane(part, far):
        return swap(part, ("y", "x"), 4, far)

    waiting, have = {}, {}

    def stage(name, *main):
        extra = {}
        for item in list(waiting):
            if BESIDE[item] == name:
                operand, function = waiting.pop(item)
                extra[item] = function(operand)
        main, extra, left = hold((main, extra, {item: waiting[item][0] for item in waiting}))
        for item in waiting:
            waiting[item] = (left[item], waiting[item][1])
        have.update(extra)
        return main

    def on_line(far):
        return lambda part: along_z(part, far)

    def on_plane(far):
        return lambda part: over_plane(part, far)

    tokens_two = along_z(tokens_in, 2)
    gains = jnp.concatenate([norm1_gain, norm1_bias, norm2_gain, norm2_bias]).reshape(1, LANES)
    keep, send = prepare(core.reshape(1), w_qkv, w_up, w_out, gains)
    keep, sent_one, sent_grad = hold((keep, tokens_in, out_grad))
    got = pair(send)
    tokens_one = along_z(sent_one, 1)
    grads = [out_grad] + [over_plane(sent_grad, far) for far in (1, 2)]
    ups, parts = compose(index_of(places["z"]), keep, got, depth)
    ups = lax.all_to_all(ups, ("y", "x"), 0, 0, tiled=True)
    tokens_two, tokens_one, grads, parts, ups, sent_tokens, sent_grad = hold(
        (tokens_two, tokens_one, grads, parts, ups, tokens_in, out_grad)
    )

    along = [parts[0]] + [along_z(parts[far], far) for far in range(1, depth)]
    waiting["up1"] = (ups, on_line(1))
    waiting["ogd"] = (sent_grad, on_plane(3))
    along, tokens_one, tokens_two, sent_tokens, ups = stage("tokens", along, tokens_one, tokens_two, sent_tokens, ups)

    middle, ends = middle_z(sent_tokens), lax.ppermute(tokens_two, "z", [(1, 0), (2, 3)])
    outs = jnp.stack([part[:, : D // 2] for part in along])
    along = jnp.stack([part[:, D // 2 :] for part in along])
    across = [along] + [over_plane(along, far) for far in range(1, 4)]
    across, middle, ends, ups, outs = stage("plane", across, middle, ends, ups, outs)
    group = [tokens_in, pair(sent_tokens), tokens_one, pair(tokens_one), tokens_two, pair(tokens_two)]
    group += [part for mine in (middle, ends) for part in (mine, pair(mine))]
    group, across, ups, outs = stage("pairs", group, across, ups, outs)

    qkv, normed, gains, turned_qkv = project(device, group, across)
    own_ups = ups
    up_two, up_three = along_z(ups, 2), along_z(ups, 3)
    outs = [outs] + [over_plane(outs, far) for far in range(1, 4)]
    attended_low, attended, recip, probs = attend(qkv)
    attended_low, up_two, up_three, outs = stage("attention", attended_low, up_two, up_three, outs)

    both = 2 * rows
    sides = [attended_low[:both]] + [
        along_z(attended_low[far * both : (far + 1) * both], far) for far in range(1, depth)
    ]
    outs = jnp.stack(outs)
    near_out = arrange(index_of(device, block, core), outs, pair(outs))
    own_out = near_out[:depth].reshape(depth * LANES, D)
    waiting["turned"] = (turned_qkv, pair)
    sides, near_out = stage("heads", sides, near_out)
    heads = [*sides, *(pair(part) for part in sides)]
    hidden, normed_two = out_project(gains, tokens_in, near_out, heads)
    normed_two, heads, sent_down = stage("hidden", normed_two, heads, w_down)

    plane_normed = [normed_two] + [over_plane(normed_two, far) for far in range(1, 4)]
    downs = [w_down] + [along_z(sent_down, far) for far in range(1, depth)]
    other_downs = [pair(part) for part in downs]
    waiting["oups0"], waiting["oups2"], waiting["oups3"] = (own_ups, pair), (up_two, pair), (up_three, pair)
    plane_normed, downs, other_downs = stage("units", plane_normed, downs, other_downs)
    ups = [own_ups, have["up1"], up_two, up_three]
    other_ups = [have["oups0"], pair(have["up1"]), have["oups2"], have["oups3"]]
    grads = [*grads, have["ogd"]]
    active, up_delta, two_delta, *part, own_down, down_keep, down_send = mlp(
        index_of(device, places["z"]), plane_normed, grads, ups, other_ups, downs, other_downs
    )

    two_sides = [over_plane(part[far - 1], far) for far in range(1, 4)]
    down_got = pair(down_send)
    down_term = [added(down_keep[far], down_got[far]) for far in range(depth)]
    waiting["dz2"], waiting["dz3"], waiting["dz1"] = ((down_term[far], on_line(far)) for far in (2, 3, 1))
    out_own, *out_parts, up_term, up_send = mlp_grads(
        index_of(places["z"]), plane_normed, active, up_delta, own_down, depth
    )
    waiting["lo1"], waiting["lo2"], waiting["lo3"] = ((out_parts[far - 1], on_plane(far)) for far in (1, 2, 3))
    two_sides, up_term, up_send = stage("sums", two_sides, up_term, up_send)
    hidden_delta, hidden_low, two_sums = norm_two(gains, hidden, out_grad, two_delta, two_sides)
    hidden_both = jnp.concatenate([hidden_low, pair(hidden_low)])
    att_delta = against(hidden_both, own_out).astype(low)
    att_delta, up_send, heads, up_term = stage("norm", att_delta, up_send, heads, up_term)

    far_delta = [att_delta[:, :LANES]] + [
        along_z(att_delta[:, far * LANES : (far + 1) * LANES], far) for far in range(1, depth)
    ]
    up_got = pair(up_send)
    out_terms = out_grads(index_of(plane, block, core), heads, hidden_both)
    up_term = [added(up_term[far], up_got[far]) for far in range(depth)]
    far_delta, out_terms, up_term = stage("delta", far_delta, out_terms, up_term)

    deltas = attend_back(qkv, probs, far_delta, attended, recip)
    up_sides = [up_term[0]] + [along_z(up_term[far], far) for far in range(1, depth)]
    deltas, up_sides = stage("back", deltas, up_sides)

    got = pair(deltas[1])
    one_delta, *part = back_project(deltas[0], got, turned_qkv, have["turned"])
    part, deltas, out_terms, up_sides = stage("project", part, deltas, out_terms, up_sides)

    waiting["upa"] = (
        up_sides,
        lambda parts: lax.all_to_all(
            sum(side.astype(jnp.float32) for side in parts).astype(low), ("y", "x"), 0, 0, tiled=True
        ),
    )
    ends, middle = lax.ppermute(part[2], "z", [(0, 1), (3, 2)]), middle_z(part[2])
    qkv_terms = qkv_gradient(index_of(plane), deltas, normed, turned_qkv, gains, two_sums, out_terms)
    ends, middle, qkv_terms = stage("middle", ends, middle, qkv_terms)

    one_sides = [along_z(added(part[1], ends), 2), along_z(part[0], 1), middle]
    terms = [qkv_terms[0]] + [over_plane(qkv_terms[far], far) for far in range(1, 4)]
    qkv_part = collect(index_of(places["z"]), terms, depth)
    out_sum = hidden + out_own
    for item in ("lo1", "lo2"):
        out_sum = out_sum + have[item].astype(jnp.float32)
    one_sides, qkv_part, out_sum = stage("rest", one_sides, qkv_part, out_sum)

    qkv_sides = [qkv_part[0]] + [along_z(qkv_part[far], far) for far in range(1, depth)]
    input_grad = norm_one(gains, tokens_in, hidden_delta, one_delta, one_sides)
    qkv_sides, input_grad, out_sum = stage("last", qkv_sides, input_grad, out_sum)
    up_sum = have["upa"]
    own_part = lax.dynamic_slice_in_dim(up_sum, core * share, share, 1)
    other_part = lax.dynamic_slice_in_dim(up_sum, (1 - core) * share, share, 1)
    up_grad = finish_up(index_of(core), own_part, pair(other_part))
    result = (out_sum + have["lo3"].astype(jnp.float32)).astype(low)
    down_sum = down_term[0].astype(jnp.float32)
    for item in ("dz1", "dz2", "dz3"):
        down_sum = down_sum + have[item].astype(jnp.float32)
    own_qkv, sent_qkv, own_out, sent_out = divide(index_of(core), qkv_sides)
    qkv_grad, vectors, out_weight_grad = finish(
        index_of(block, core), own_qkv, pair(sent_qkv), own_out, pair(sent_out)
    )
    vectors = lax.dynamic_slice_in_dim(vectors, (places["z"] * 2 + core) * share, share, 1)
    return (
        result,
        input_grad,
        qkv_grad,
        out_weight_grad,
        up_grad,
        down_sum,
        vectors[0],
        vectors[1],
        vectors[2],
        vectors[3],
    )


def solution(mesh):
    scenes, blocks = mesh.devices.shape

    def place(axes):
        matrix = P(axes, None)
        views = P(axes[: len(axes) // 2] if len(axes) > 2 else axes[0], None)
        vector = P(axes)
        ins = (matrix, views, views, views, matrix, matrix, matrix, matrix, matrix) + (vector,) * 4
        return ins, (matrix,) * 6 + (vector,) * 4

    def run(*arrays):
        one_scene = arrays[1].shape[1] == 4
        if scenes == 4 and blocks == 8 and one_scene and arrays[0].shape[0] == 8192:
            fine = Mesh(mesh.devices.reshape(2, 2, blocks // 2, 2), ALL)
            ins, outs = place(ALL)
            step = lambda tokens, heights, widths, labels, *rest: on_planes(tokens, *rest)
            return jax.shard_map(step, mesh=fine, in_specs=ins, out_specs=outs, check_vma=False)(*arrays)
        ins, outs = place(("scene", "blk"))
        return jax.shard_map(on_any_slice, mesh=mesh, in_specs=ins, out_specs=outs, check_vma=False)(*arrays)

    return run
```

```python
import functools
import math

import jax
import jax.numpy as jnp
from jax import lax
from jax.experimental import pallas as pl
from jax.experimental.pallas import tpu as pltpu
from jax.sharding import Mesh
from jax.sharding import PartitionSpec as P

D = 1024
HEADS = 16
HEAD_DIM = 64


EPSILON = 1e-05
MASKED = -1e30


def layer_norm(values, gain_row, bias_row):
    centred = values - jnp.mean(values, axis=1, keepdims=True)
    scaled = centred * lax.rsqrt(jnp.mean(centred * centred, axis=1, keepdims=True) + EPSILON)
    return scaled * gain_row + bias_row


def scene_rows(view_ends, labels, first_row, count_rows):
    places = first_row + jnp.arange(count_rows, dtype=jnp.int32)
    view_index = jnp.sum((places[:, None] >= view_ends[None, :]).astype(jnp.int32), axis=1)
    matches = view_index[:, None] == jnp.arange(labels.shape[0], dtype=jnp.int32)[None, :]
    return jnp.sum(jnp.where(matches, labels[None, :], 0), axis=1)


def in_blocks(update, carry, members):
    total_rows = members[0].shape[0]
    width_rows = math.gcd(total_rows, 1024)
    block_count = total_rows // width_rows
    stacked = tuple(
        (member.reshape((block_count, width_rows) + member.shape[1:]) for member in members)
    )

    def advance(state_now, indexed):
        block_index, block_parts = indexed
        return (update(state_now, block_parts, block_index * width_rows), None)

    carry, _ = lax.scan(advance, carry, (jnp.arange(block_count, dtype=jnp.int32), stacked))
    return carry


def heads_of(rows):
    return rows.reshape(rows.shape[0], HEADS, HEAD_DIM)


def pair_terms(
    query_heads, delta_heads, log_rows, probe_rows, allowed, key_heads, value_heads, score_scale
):
    raw = (
        jnp.einsum("qhe,khe->hqk", query_heads, key_heads, preferred_element_type=jnp.float32)
        * score_scale
    )
    weights_now = jnp.where(allowed, jnp.exp(raw - log_rows[:, :, None]), 0.0)
    backward = jnp.einsum(
        "qhe,khe->hqk", delta_heads, value_heads, preferred_element_type=jnp.float32
    )
    score_delta = (weights_now * (backward - probe_rows[:, :, None])).astype(jnp.bfloat16)
    return (weights_now.astype(jnp.bfloat16), score_delta)


def outer(left, right):
    return lax.dot_general(
        left, right, (((0,), (0,)), ((), ())), preferred_element_type=jnp.float32
    )


def against(left, right):
    return lax.dot_general(
        left, right, (((1,), (1,)), ((), ())), preferred_element_type=jnp.float32
    )


def on_any_slice(
    tokens_in,
    view_heights,
    view_widths,
    view_scenes,
    out_grad,
    w_qkv,
    w_out,
    w_up,
    w_down,
    norm1_gain,
    norm1_bias,
    norm2_gain,
    norm2_bias,
):
    gathered = (
        lax.all_gather(w_qkv, ("scene", "blk"), axis=0, tiled=True),
        lax.all_gather(w_out, ("scene", "blk"), axis=0, tiled=True),
        lax.all_gather(w_up, ("scene", "blk"), axis=0, tiled=True),
        lax.all_gather(w_down, ("scene", "blk"), axis=0, tiled=True),
        lax.all_gather(norm1_gain, ("scene", "blk"), axis=0, tiled=True),
        lax.all_gather(norm1_bias, ("scene", "blk"), axis=0, tiled=True),
        lax.all_gather(norm2_gain, ("scene", "blk"), axis=0, tiled=True),
        lax.all_gather(norm2_bias, ("scene", "blk"), axis=0, tiled=True),
    )
    full_qkv, full_out, full_up, full_down = (gathered[0], gathered[1], gathered[2], gathered[3])
    gain_one = gathered[4].astype(jnp.float32)
    bias_one = gathered[5].astype(jnp.float32)
    gain_two = gathered[6].astype(jnp.float32)
    bias_two = gathered[7].astype(jnp.float32)
    local_rows = tokens_in.shape[0]
    view_ends = jnp.cumsum(view_heights[0] * view_widths[0])
    labels = view_scenes[0]
    own_first = lax.axis_index("blk") * local_rows
    own_scene = scene_rows(view_ends, labels, own_first, local_rows)
    score_scale = HEAD_DIM ** (-0.5)
    inputs = tokens_in.astype(jnp.float32)
    normed, norm_one_pull = jax.vjp(layer_norm, inputs, gain_one, bias_one)
    normed_low = normed.astype(jnp.bfloat16)
    projected = jnp.dot(normed_low, full_qkv, preferred_element_type=jnp.float32).astype(
        jnp.bfloat16
    )
    query_rows = projected[:, :D]
    key_rows = projected[:, D : 2 * D]
    value_rows = projected[:, 2 * D :]
    query_heads = heads_of(query_rows)

    def forward_update(state_now, members, first_row):
        run_max, run_sum, run_total = state_now
        piece_keys, piece_values = members
        piece_rows = piece_keys.shape[0]
        key_scene = scene_rows(view_ends, labels, first_row, piece_rows)
        allowed = (own_scene[:, None] == key_scene[None, :])[None]
        raw = (
            jnp.einsum(
                "qhe,khe->hqk",
                query_heads,
                heads_of(piece_keys),
                preferred_element_type=jnp.float32,
            )
            * score_scale
        )
        new_max = jnp.maximum(run_max, jnp.max(jnp.where(allowed, raw, MASKED), axis=2))
        expo = jnp.where(allowed, jnp.exp(raw - new_max[:, :, None]), 0.0)
        factor = jnp.exp(run_max - new_max)
        run_sum = run_sum * factor + jnp.sum(expo, axis=2)
        mixed = jnp.einsum(
            "hqk,khe->qhe",
            expo.astype(jnp.bfloat16),
            heads_of(piece_values),
            preferred_element_type=jnp.float32,
        )
        run_total = run_total * jnp.transpose(factor)[:, :, None] + mixed
        return (new_max, run_sum, run_total)

    start_state = (
        jnp.full((HEADS, local_rows), MASKED, jnp.float32),
        jnp.zeros((HEADS, local_rows), jnp.float32),
        jnp.zeros((local_rows, HEADS, HEAD_DIM), jnp.float32),
    )
    run_max, run_sum, run_total = in_blocks(
        forward_update,
        start_state,
        (
            lax.all_gather(key_rows, "blk", axis=0, tiled=True),
            lax.all_gather(value_rows, "blk", axis=0, tiled=True),
        ),
    )
    log_total = run_max + jnp.log(run_sum)
    attended_heads = run_total / jnp.transpose(run_sum)[:, :, None]
    attended_low = attended_heads.reshape(local_rows, D).astype(jnp.bfloat16)
    hidden = inputs + jnp.dot(attended_low, full_out, preferred_element_type=jnp.float32)
    normed_two, norm_two_pull = jax.vjp(layer_norm, hidden, gain_two, bias_two)
    normed_two_low = normed_two.astype(jnp.bfloat16)
    upward = jnp.dot(normed_two_low, full_up, preferred_element_type=jnp.float32)
    active, gelu_pull = jax.vjp(jax.nn.gelu, upward)
    active_low = active.astype(jnp.bfloat16)
    result = (hidden + jnp.dot(active_low, full_down, preferred_element_type=jnp.float32)).astype(
        jnp.bfloat16
    )
    down_term = outer(active_low, out_grad)
    up_delta = gelu_pull(against(out_grad, full_down))[0].astype(jnp.bfloat16)
    up_term = outer(normed_two_low, up_delta)
    hidden_back, gain_two_term, bias_two_term = norm_two_pull(against(up_delta, full_up))
    hidden_delta = out_grad.astype(jnp.float32) + hidden_back
    hidden_low = hidden_delta.astype(jnp.bfloat16)
    out_term = outer(attended_low, hidden_low)
    att_delta = against(hidden_low, full_out).astype(jnp.bfloat16)
    delta_heads = heads_of(att_delta)
    row_probe = jnp.transpose(jnp.sum(delta_heads.astype(jnp.float32) * attended_heads, axis=2))
    query_start = jnp.zeros((local_rows, HEADS, HEAD_DIM), jnp.float32)
    every_key, every_value = (
        lax.all_gather(key_rows, "blk", axis=0, tiled=True),
        lax.all_gather(value_rows, "blk", axis=0, tiled=True),
    )
    group_rows = every_key.shape[0]
    width_rows = math.gcd(group_rows, 1024)
    block_count = group_rows // width_rows

    def joint_step(total, indexed):
        block_index, block_keys, block_values = indexed
        block_first = block_index * width_rows
        key_heads = heads_of(block_keys)
        value_heads = heads_of(block_values)
        key_scene = scene_rows(view_ends, labels, block_first, width_rows)
        allowed = (own_scene[:, None] == key_scene[None, :])[None]
        weights_low, score_delta = pair_terms(
            query_heads,
            delta_heads,
            log_total,
            row_probe,
            allowed,
            key_heads,
            value_heads,
            score_scale,
        )
        total = (
            total
            + jnp.einsum("hqk,khe->qhe", score_delta, key_heads, preferred_element_type=jnp.float32)
            * score_scale
        )
        value_part = jnp.einsum(
            "hqk,qhe->khe", weights_low, delta_heads, preferred_element_type=jnp.float32
        )
        key_part = (
            jnp.einsum("hqk,qhe->khe", score_delta, query_heads, preferred_element_type=jnp.float32)
            * score_scale
        )
        rows_out = jnp.concatenate(
            [key_part.reshape(width_rows, D), value_part.reshape(width_rows, D)], axis=1
        )
        return (total, rows_out)

    query_total, pair_rows = lax.scan(
        joint_step,
        query_start,
        (
            jnp.arange(block_count, dtype=jnp.int32),
            every_key.reshape(block_count, width_rows, D),
            every_value.reshape(block_count, width_rows, D),
        ),
    )
    pair_rows = pair_rows.reshape(group_rows, 2 * D)
    both_sums = lax.psum_scatter(
        pair_rows.astype(jnp.bfloat16), "blk", scatter_dimension=0, tiled=True
    ).astype(jnp.float32)
    key_total = both_sums[:, :D]
    value_total = both_sums[:, D:]
    qkv_delta = jnp.concatenate(
        [query_total.reshape(local_rows, D), key_total, value_total], axis=1
    ).astype(jnp.bfloat16)
    qkv_term = outer(normed_low, qkv_delta)
    input_back, gain_one_term, bias_one_term = norm_one_pull(against(qkv_delta, full_qkv))
    input_grad = hidden_delta + input_back
    summed = (
        lax.psum_scatter(qkv_term, ("scene", "blk"), scatter_dimension=0, tiled=True),
        lax.psum_scatter(out_term, ("scene", "blk"), scatter_dimension=0, tiled=True),
        lax.psum_scatter(up_term, ("scene", "blk"), scatter_dimension=0, tiled=True),
        lax.psum_scatter(down_term, ("scene", "blk"), scatter_dimension=0, tiled=True),
        lax.psum_scatter(gain_one_term, ("scene", "blk"), scatter_dimension=0, tiled=True),
        lax.psum_scatter(bias_one_term, ("scene", "blk"), scatter_dimension=0, tiled=True),
        lax.psum_scatter(gain_two_term, ("scene", "blk"), scatter_dimension=0, tiled=True),
        lax.psum_scatter(bias_two_term, ("scene", "blk"), scatter_dimension=0, tiled=True),
    )
    return (
        result,
        input_grad,
        summed[0],
        summed[1],
        summed[2],
        summed[3],
        summed[4],
        summed[5],
        summed[6],
        summed[7],
    )


ALL = ("y", "x", "z", "c")
LANES = 128
BESIDE = {
    "up1": "tokens", "ogd": "tokens", "turned": "delta", "oups0": "units", "oups2": "units", "oups3": "units",
    "dz2": "sums", "dz3": "sums", "dz1": "back", "lo1": "middle", "lo2": "middle", "lo3": "back", "upa": "rest",
}
ROOT = math.sqrt(2.0 / math.pi)
CUBIC = 0.044715
FREE = pl.CostEstimate(flops=0, bytes_accessed=0, transcendentals=0)


def swap(values, axis, size, distance):
    return lax.ppermute(values, axis, [(i, i ^ distance) for i in range(size)])


def pair(values):
    return swap(values, "c", 2, 1)


def whole(shape):
    return pl.BlockSpec(shape, lambda *_: (0,) * len(shape))


def params(megabytes=60):
    return pltpu.CompilerParams(vmem_limit_bytes=megabytes * 1024 * 1024)


def three_parts(column, lane, first):
    high = column.astype(jnp.bfloat16).astype(jnp.float32)
    rest = column - high
    middle = rest.astype(jnp.bfloat16).astype(jnp.float32)
    last = rest - middle
    zero = jnp.zeros_like(last)
    return jnp.where(
        lane == first,
        high,
        jnp.where(lane == first + 1, middle, jnp.where(lane == first + 2, last, zero)),
    )


def attend_kernel(q_ref, k_ref, v_ref, *refs, chunk):
    low_ref, att_ref, rl_ref, p_ref, s0, s1, m0, m1, vt_ref, hold_ref = refs
    unit = pl.program_id(0)
    last = pl.num_programs(0) - 1
    rows = k_ref.shape[0]
    block = q_ref.shape[0]
    lane = lax.broadcasted_iota(jnp.int32, (1, LANES), 1)
    line = lax.broadcasted_iota(jnp.int32, (LANES, 1), 0)

    @pl.when(unit == 0)
    def _():
        turned = v_ref[...].astype(jnp.float32).T
        vt_ref[0] = jnp.where(line < HEAD_DIM, turned, 1.0).astype(jnp.bfloat16)
        vt_ref[1] = jnp.where(line >= HEAD_DIM, turned, 1.0).astype(jnp.bfloat16)

    def work(head, fresh, scores, old):
        mine = (lane < HEAD_DIM) if head == 0 else (lane >= HEAD_DIM)
        query = jnp.where(mine, q_ref[...].astype(jnp.float32) * HEAD_DIM ** (-0.5), 0.0).astype(jnp.bfloat16)
        top = jnp.full((8, block), -jnp.inf, jnp.float32)
        high = old[0][0:1, :] if old is not None else None
        mixed = jnp.zeros((LANES, block), jnp.float32)
        for first in range(0, rows, chunk):
            part = slice(first, first + chunk)
            if fresh is not None:
                got = against(k_ref[part, :], query)
                scores[part, :] = got
                top = jnp.maximum(top, jnp.max(got.reshape(chunk // 8, 8, block), axis=0))
            if old is not None:
                expo = jnp.exp(old[1][part, :] - high).astype(jnp.bfloat16)
                p_ref[0, part, :] = expo
                mixed += jnp.dot(vt_ref[1 - head, :, part], expo, preferred_element_type=jnp.float32)
        if fresh is not None:
            fresh[...] = jnp.broadcast_to(jnp.max(top, axis=0, keepdims=True), (8, block))
        return mixed.T if old is not None else None

    @pl.when(unit == 0)
    def _():
        work(0, m0, s0, None)

    @pl.when((unit > 0) & (unit % 2 == 1))
    def _():
        hold_ref[...] = work(1, m1, s1, (m0, s0))

    def finish(second):
        first = hold_ref[...]
        low_lane = lane < HEAD_DIM
        recip = 1.0 / jnp.where(low_lane, pltpu.roll(first, HEAD_DIM, 1), pltpu.roll(second, HEAD_DIM, 1))
        attended = jnp.where(low_lane, first, second) * recip
        att_ref[...] = attended
        rl_ref[...] = recip
        low_ref[...] = attended.astype(jnp.bfloat16)

    @pl.when((unit > 0) & (unit % 2 == 0) & (unit < last))
    def _():
        finish(work(0, m0, s0, (m1, s1)))

    @pl.when(unit == last)
    def _():
        finish(work(0, None, None, (m1, s1)))

def attend(qkv):
    rows = qkv.shape[0]
    block, chunk = 512, 256
    units = 2 * rows // block

    def new(u):
        return jnp.minimum(u, units - 1) // 2

    def old(u):
        return jnp.maximum(u - 1, 0)

    part = pl.BlockSpec((block, LANES), lambda u: (old(u) // 2, 0))
    return pl.pallas_call(
        functools.partial(attend_kernel, chunk=chunk),
        grid=(units + 1,),
        in_specs=[
            pl.BlockSpec((block, LANES), lambda u: (new(u), 0)),
            pl.BlockSpec((rows, LANES), lambda u: (0, 1)),
            pl.BlockSpec((rows, LANES), lambda u: (0, 2)),
        ],
        out_specs=[part, part, part, pl.BlockSpec((1, rows, block), lambda u: (old(u) % 2, 0, old(u) // 2))],
        out_shape=[
            jax.ShapeDtypeStruct((rows, LANES), jnp.bfloat16),
            jax.ShapeDtypeStruct((rows, LANES), jnp.float32),
            jax.ShapeDtypeStruct((rows, LANES), jnp.float32),
            jax.ShapeDtypeStruct((2, rows, rows), jnp.bfloat16),
        ],
        scratch_shapes=[pltpu.VMEM((rows, block), jnp.float32)] * 2
        + [pltpu.VMEM((8, block), jnp.float32)] * 2
        + [pltpu.VMEM((2, LANES, rows), jnp.bfloat16), pltpu.VMEM((block, LANES), jnp.float32)],
        compiler_params=params(34),
        cost_estimate=FREE,
    )(qkv, qkv, qkv)


def attend_back_kernel(q_ref, k_ref, v_ref, p_ref, att_ref, rl_ref, *refs, chunk, count):
    deltas, outs = refs[:count], refs[count : count + 2]
    va_ref, kt_ref, dq_acc, dk_acc, dv_acc, do_ref = refs[count + 2 :]
    head, step = pl.program_id(0), pl.program_id(1)
    rows = k_ref.shape[0]
    block = do_ref.shape[0]
    lane = lax.broadcasted_iota(jnp.int32, (1, LANES), 1)
    spare = jnp.where(head == 0, HEAD_DIM, 0)
    mine = (lane < spare) | (lane >= spare + HEAD_DIM)

    @pl.when((head == 0) & (step == 0))
    def _():
        kt_ref[...] = (k_ref[...].astype(jnp.float32) * HEAD_DIM ** (-0.5)).T.astype(jnp.bfloat16)

    @pl.when(step == 0)
    def _():
        ones = jnp.where(lane < spare + 3, 1.0, 0.0)
        va_ref[...] = jnp.where(mine, v_ref[...].astype(jnp.float32), ones).astype(jnp.bfloat16)
        dk_acc[head] = jnp.zeros((rows, LANES), jnp.float32)
        dv_acc[head] = jnp.zeros((rows, LANES), jnp.float32)

    for index, ref in enumerate(deltas):

        @pl.when(step == index)
        def _():
            do_ref[...] = ref[...]

    delta = (do_ref[...].astype(jnp.float32) * rl_ref[...]).astype(jnp.bfloat16).astype(jnp.float32)
    probe = jnp.sum(jnp.where(mine, delta * att_ref[...], 0.0), axis=1, keepdims=True)
    own_delta = jnp.where(mine, delta, three_parts(-probe, lane, spare)).astype(jnp.bfloat16)
    query = (q_ref[...].astype(jnp.float32) * HEAD_DIM ** (-0.5)).astype(jnp.bfloat16)
    total = jnp.zeros((LANES, block), jnp.float32)
    for first in range(0, rows, chunk):
        part = slice(first, first + chunk)
        expo = p_ref[0, part, :]
        score_delta = (expo.astype(jnp.float32) * against(va_ref[part, :], own_delta)).astype(jnp.bfloat16)
        dv_acc[head, part, :] += jnp.dot(expo, own_delta, preferred_element_type=jnp.float32)
        dk_acc[head, part, :] += jnp.dot(score_delta, query, preferred_element_type=jnp.float32)
        total += jnp.dot(kt_ref[:, part], score_delta, preferred_element_type=jnp.float32)
    query_delta = total.T
    place = pl.ds(pl.multiple_of(step * block, block), block)

    @pl.when(head == 0)
    def _():
        dq_acc[place, :] = query_delta

    half = block // 2

    @pl.when(head == 1)
    def _():
        both = jnp.where(lane < HEAD_DIM, dq_acc[place, :], query_delta).astype(jnp.bfloat16)
        for side, ref in enumerate(outs):
            ref[step, :, :LANES] = both[side * half : (side + 1) * half]

    @pl.when((head == 1) & (step == pl.num_programs(1) - 1))
    def _():
        for index in range(count):
            for side, ref in enumerate(outs):
                part = slice(index * block + side * half, index * block + (side + 1) * half)
                for kind, acc in ((1, dk_acc), (2, dv_acc)):
                    own = jnp.where(lane < HEAD_DIM, acc[0, part, :], acc[1, part, :]).astype(jnp.bfloat16)
                    ref[index, :, kind * LANES : (kind + 1) * LANES] = own


def attend_back(qkv, probs, deltas, attended, recip):
    rows = qkv.shape[0]
    count = len(deltas)
    block, chunk = rows // count, 512
    part = pl.BlockSpec((block, LANES), lambda h, i: (i, 0))
    return pl.pallas_call(
        functools.partial(attend_back_kernel, chunk=chunk, count=count),
        grid=(2, count),
        in_specs=[
            part,
            pl.BlockSpec((rows, LANES), lambda h, i: (0, 1)),
            pl.BlockSpec((rows, LANES), lambda h, i: (0, 2)),
            pl.BlockSpec((1, rows, block), lambda h, i: (h, 0, i)),
            part,
            part,
        ]
        + [whole((block, LANES))] * count,
        out_specs=[whole((count, block // 2, 3 * LANES))] * 2,
        out_shape=[jax.ShapeDtypeStruct((count, block // 2, 3 * LANES), jnp.bfloat16)] * 2,
        scratch_shapes=[
            pltpu.VMEM((rows, LANES), jnp.bfloat16),
            pltpu.VMEM((LANES, rows), jnp.bfloat16),
            pltpu.VMEM((rows, LANES), jnp.float32),
            pltpu.VMEM((2, rows, LANES), jnp.float32),
            pltpu.VMEM((2, rows, LANES), jnp.float32),
            pltpu.VMEM((block, LANES), jnp.bfloat16),
        ],
        compiler_params=params(36),
        cost_estimate=FREE,
    )(qkv, qkv, qkv, probs, attended, recip, *deltas)


def qkv_kernel(place_ref, *refs):
    pieces, weights = refs[:10], refs[10:14]
    qkv_ref, normed_ref, gains_ref, turned_ref, own_ref, table_ref = refs[14:]
    depth, share = weights[0].shape[0], weights[0].shape[1] // 2

    @pl.when(pl.program_id(0) == 0)
    def _():
        device = place_ref[0]
        for far, part in enumerate(weights):
            for near in range(depth):
                for core in range(2):
                    owner = device ^ (far * 2 * depth + near * 2 + core)
                    row = pl.multiple_of(owner * share, share)
                    first = core * share
                    own_ref[pl.ds(row, share), :] = part[near, first : first + share, : 3 * LANES]
                    table = part[near, first : first + 16, 3 * LANES :].astype(jnp.float32)
                    table_ref[pl.ds(owner, 1), :] = table[0:1]
        devices = table_ref.shape[0]
        table = table_ref[...].astype(jnp.bfloat16)
        row = lax.broadcasted_iota(jnp.int32, (LANES, D), 0)
        col = lax.broadcasted_iota(jnp.int32, (LANES, D), 1)
        owner = lax.broadcasted_iota(jnp.int32, (devices, D), 0)
        own_col = lax.broadcasted_iota(jnp.int32, (devices, D), 1) // share
        for kind in range(4):
            spread = jnp.where(row == kind * share + col % share, 1.0, 0.0).astype(jnp.bfloat16)
            wide = jnp.dot(table, spread, preferred_element_type=jnp.float32)
            gains_ref[kind : kind + 1, :] = jnp.sum(jnp.where(owner == own_col, wide, 0.0), axis=0, keepdims=True)
        gains_ref[4:8, :] = jnp.zeros((4, D), jnp.float32)
        turned_ref[...] = own_ref[...].astype(jnp.float32).T.astype(jnp.bfloat16)

    gain, bias = gains_ref[0:1, :], gains_ref[1:2, :]
    for index in range(8):
        tokens = pieces[index][...].astype(jnp.float32)
        if index >= 6:
            tokens = tokens + pieces[index + 2][...].astype(jnp.float32)
        normal, _ = moments(tokens)
        normed = (normal * gain + bias).astype(jnp.bfloat16)
        normed_ref[index] = normed
        qkv_ref[index] = jnp.dot(normed, own_ref[...], preferred_element_type=jnp.float32).astype(jnp.bfloat16)


def project(device, pieces, weights):
    rows = pieces[0].shape[0]
    steps = 2
    block = rows // steps
    piece = pl.BlockSpec((block, D), lambda i, place: (i, 0))
    part = pl.BlockSpec(weights[0].shape, lambda i, place: (0, 0, 0))
    grid_spec = pltpu.PrefetchScalarGridSpec(
        num_scalar_prefetch=1,
        grid=(steps,),
        in_specs=[piece] * 10 + [part] * 4,
        out_specs=[
            pl.BlockSpec((8, block, 3 * LANES), lambda i, place: (0, i, 0)),
            pl.BlockSpec((8, block, D), lambda i, place: (0, i, 0)),
            pl.BlockSpec((8, D), lambda i, place: (0, 0)),
            pl.BlockSpec((3 * LANES, D), lambda i, place: (0, 0)),
        ],
        scratch_shapes=[
            pltpu.VMEM((D, 3 * LANES), jnp.bfloat16),
            pltpu.VMEM((32, LANES), jnp.float32),
        ],
    )
    qkv, normed, gains, turned = pl.pallas_call(
        qkv_kernel,
        grid_spec=grid_spec,
        out_shape=[
            jax.ShapeDtypeStruct((8, rows, 3 * LANES), jnp.bfloat16),
            jax.ShapeDtypeStruct((8, rows, D), jnp.bfloat16),
            jax.ShapeDtypeStruct((8, D), jnp.float32),
            jax.ShapeDtypeStruct((3 * LANES, D), jnp.bfloat16),
        ],
        compiler_params=params(60),
        cost_estimate=FREE,
    )(device.reshape(1).astype(jnp.int32), *pieces, *weights)
    return qkv.reshape(8 * rows, 3 * LANES), normed.reshape(8 * rows, D), gains, turned


def mlp_kernel(place_ref, *refs):
    device, own_z = place_ref[0], place_ref[1]
    nts, ogs, refs = refs[:4], refs[4:8], refs[8:]
    ups, other_ups, downs, other_downs = refs[:4], refs[4:8], refs[8:12], refs[12:16]
    act_ref, ud_ref, keep_ref, one_ref, two_ref, three_ref, down_ref, down_keep, down_send, up_ref, down_acc = refs[16:]
    depth, share, wide = len(ups), ups[0].shape[1] // 2, ups[0].shape[2]

    @pl.when(pl.program_id(0) == 0)
    def _():
        slab = downs[0].shape[0]
        for side, parts in enumerate((ups, other_ups)):
            for near, part in enumerate(parts):
                for far in range(part.shape[0]):
                    for core in range(2):
                        owner = far * 2 * depth + ((device % (2 * depth)) ^ (near * 2 + (core ^ side)))
                        row = pl.multiple_of(owner * share, share)
                        cols = slice(side * wide, (side + 1) * wide)
                        up_ref[pl.ds(row, share), cols] = part[far, core * share : (core + 1) * share, :]
        for side, parts in enumerate((downs, other_downs)):
            for near, part in enumerate(parts):
                row = pl.multiple_of(side * wide + (own_z ^ near) * slab, slab)
                down_ref[pl.ds(row, slab), :] = part[...]

    rows = nts[0].shape[0]
    normed = jnp.concatenate([ref[...] for ref in nts])
    grads = jnp.concatenate([ref[...] for ref in ogs])
    back = jnp.zeros((4 * rows, D), jnp.float32)
    for side in range(2):
        cols = slice(side * wide, (side + 1) * wide)
        upward = jnp.dot(normed, up_ref[:, cols], preferred_element_type=jnp.float32)
        square = upward * upward
        curve = jnp.tanh(ROOT * upward * (1.0 + CUBIC * square))
        active = (0.5 * upward * (1.0 + curve)).astype(jnp.bfloat16)
        slope = 0.5 * (1.0 + curve) + 0.5 * upward * (1.0 - curve * curve) * (ROOT * (1.0 + 3.0 * CUBIC * square))
        delta = (against(grads, down_ref[cols, :]) * slope).astype(jnp.bfloat16)
        back += against(delta, up_ref[:, cols])
        down_acc[cols, :] = outer(active, grads)
        for index in range(4):
            part = slice(index * rows, (index + 1) * rows)
            act_ref[index, :, cols] = active[part]
            ud_ref[index, :, cols] = delta[part]
    keep_ref[...] = back[:rows]
    for index, to in enumerate((one_ref, two_ref, three_ref)):
        to[...] = back[(index + 1) * rows : (index + 2) * rows].astype(jnp.bfloat16)

    slab = down_keep.shape[1]
    for side, to in enumerate((down_keep, down_send)):
        for near in range(depth):
            first = side * wide + near * slab
            to[near ^ own_z] = down_acc[first : first + slab, :].astype(jnp.bfloat16)


def mlp(place, normed, grads, ups, other_ups, downs, other_downs):
    rows = normed[0].shape[0]
    steps = 1
    block = rows // steps
    wide = 2 * ups[0].shape[2]
    low = jnp.bfloat16
    piece = pl.BlockSpec((block, D), lambda i, place: (i, 0))
    weights = (*ups, *other_ups, *downs, *other_downs)
    down_shape = (len(downs), *downs[0].shape)

    def full(shape):
        return pl.BlockSpec(shape, lambda i, place: (0,) * len(shape))

    units = pl.BlockSpec((4, block, wide), lambda i, place: (0, i, 0))
    grid_spec = pltpu.PrefetchScalarGridSpec(
        num_scalar_prefetch=1,
        grid=(steps,),
        in_specs=[piece] * 8 + [full(part.shape) for part in weights],
        out_specs=[units, units, piece, piece, piece, piece, full((wide, D))] + [full(down_shape)] * 2,
        scratch_shapes=[pltpu.VMEM((D, wide), low), pltpu.VMEM((wide, D), jnp.float32)],
    )
    return pl.pallas_call(
        mlp_kernel,
        grid_spec=grid_spec,
        out_shape=[
            jax.ShapeDtypeStruct((4, rows, wide), low),
            jax.ShapeDtypeStruct((4, rows, wide), low),
            jax.ShapeDtypeStruct((rows, D), jnp.float32),
            jax.ShapeDtypeStruct((rows, D), low),
            jax.ShapeDtypeStruct((rows, D), low),
            jax.ShapeDtypeStruct((rows, D), low),
            jax.ShapeDtypeStruct((wide, D), low),
        ]
        + [jax.ShapeDtypeStruct(down_shape, low)] * 2,
        compiler_params=params(40),
        cost_estimate=FREE,
    )(place, *normed, *grads, *weights)


def mlp_grads_kernel(place_ref, *refs):
    nts, refs = refs[:4], refs[4:]
    act_ref, ud_ref, down_ref, keep_ref, one_ref, two_ref, three_ref, up_keep, up_send, up_acc = refs
    step = pl.program_id(0)
    rows = nts[0].shape[0]
    normed = jnp.concatenate([ref[...] for ref in nts])
    wide = act_ref.shape[2]
    active = act_ref[...].reshape(4 * rows, wide)
    up = outer(normed, ud_ref[...].reshape(4 * rows, wide))
    out = jnp.dot(active, down_ref[...], preferred_element_type=jnp.float32)
    keep_ref[...] = out[:rows]
    for index, to in enumerate((one_ref, two_ref, three_ref)):
        to[...] = out[(index + 1) * rows : (index + 2) * rows].astype(jnp.bfloat16)

    @pl.when(step == 0)
    def _():
        up_acc[...] = up

    @pl.when(step > 0)
    def _():
        up_acc[...] += up

    @pl.when(step == pl.num_programs(0) - 1)
    def _():
        depth, _, share = up_keep.shape[:3]
        half = wide // 2
        for side, to in enumerate((up_keep, up_send)):
            for near in range(depth):
                for far in range(4):
                    first = (far * depth + near) * share
                    part = up_acc[first : first + share, side * half : (side + 1) * half]
                    to[near ^ place_ref[0], far] = part.astype(jnp.bfloat16)


def mlp_grads(place, normed, active, delta, w_down, depth):
    rows = normed[0].shape[0]
    steps = 4
    block = rows // steps
    wide = active.shape[2]
    low = jnp.bfloat16
    piece = pl.BlockSpec((block, D), lambda i, place: (i, 0))
    units = pl.BlockSpec((4, block, wide), lambda i, place: (0, i, 0))

    def full(shape):
        return pl.BlockSpec(shape, lambda i, place: (0,) * len(shape))

    shapes = [(depth, 4, D // (4 * depth), wide // 2)] * 2
    grid_spec = pltpu.PrefetchScalarGridSpec(
        num_scalar_prefetch=1,
        grid=(steps,),
        in_specs=[piece] * 4 + [units] * 2 + [full(w_down.shape)],
        out_specs=[piece] * 4 + [full(shape) for shape in shapes],
        scratch_shapes=[pltpu.VMEM((D, wide), jnp.float32)],
    )
    return pl.pallas_call(
        mlp_grads_kernel,
        grid_spec=grid_spec,
        out_shape=[jax.ShapeDtypeStruct((rows, D), jnp.float32)]
        + [jax.ShapeDtypeStruct((rows, D), low)] * 3
        + [jax.ShapeDtypeStruct(shape, low) for shape in shapes],
        compiler_params=params(36),
        cost_estimate=FREE,
    )(place, *normed, active, delta, w_down)


def prepare_kernel(core_ref, qkv_ref, up_ref, out_ref, gains_ref, keep_ref, send_ref):
    core = core_ref[0]
    chips = up_ref.shape[1] // (2 * LANES)
    half = out_ref.shape[1] // 2
    depth = chips // 4
    for side, to in ((core, keep_ref), (1 - core, send_ref)):
        for chip in range(chips):
            cols = pl.ds(pl.multiple_of((2 * chip + side) * LANES, LANES), LANES)
            to[:, chip * LANES : (chip + 1) * LANES] = up_ref[:, cols]
        first = chips * LANES
        to[:, first : first + half] = out_ref[:, pl.ds(pl.multiple_of(side * half, half), half)]
        first += half
        for near in range(depth):
            for kind in range(3):
                cols = pl.ds(pl.multiple_of(kind * D + (2 * near + side) * LANES, LANES), LANES)
                to[:, first : first + LANES] = qkv_ref[:, cols]
                first += LANES
        to[:, first:] = jnp.broadcast_to(gains_ref[...], (to.shape[0], LANES))


def prepare(core, w_qkv, w_up, w_out, gains):
    share = w_qkv.shape[0]
    wide = (w_up.shape[1] + w_out.shape[1] + w_qkv.shape[1]) // 2 + LANES
    return pl.pallas_call(
        prepare_kernel,
        in_specs=[pl.BlockSpec(memory_space=pltpu.SMEM)]
        + [whole(array.shape) for array in (w_qkv, w_up, w_out, gains)],
        out_specs=[whole((share, wide))] * 2,
        out_shape=[jax.ShapeDtypeStruct((share, wide), jnp.bfloat16)] * 2,
        compiler_params=params(8),
        cost_estimate=FREE,
    )(core, w_qkv, w_up, w_out, gains)


def compose_kernel(place_ref, keep_ref, got_ref, up_ref, *parts):
    own_z = place_ref[0]
    share = keep_ref.shape[0]
    depth = len(parts)
    wide = up_ref.shape[2]
    half = D // 2
    heads = 4 * wide + half
    for side, ref in ((0, keep_ref), (1, got_ref)):
        rows = slice(side * share, (side + 1) * share)
        for far in range(4):
            up_ref[far, rows, :] = ref[:, far * wide : (far + 1) * wide]
        for far, part in enumerate(parts):
            first = heads + (own_z ^ far) * 3 * LANES
            part[rows, :half] = ref[:, 4 * wide : heads]
            part[rows, half : half + 3 * LANES] = ref[:, pl.ds(pl.multiple_of(first, LANES), 3 * LANES)]
            part[rows, half + 3 * LANES :] = ref[:, heads + depth * 3 * LANES :]


def compose(place, keep, got, depth):
    share = keep.shape[0]
    shapes = [(4, 2 * share, D // 2)] + [(2 * share, D)] * depth
    ups, *parts = pl.pallas_call(
        compose_kernel,
        in_specs=[pl.BlockSpec(memory_space=pltpu.SMEM), whole(keep.shape), whole(got.shape)],
        out_specs=[whole(shape) for shape in shapes],
        out_shape=[jax.ShapeDtypeStruct(shape, jnp.bfloat16) for shape in shapes],
        compiler_params=params(8),
        cost_estimate=FREE,
    )(place, keep, got)
    return ups, parts


def arrange_kernel(place_ref, own_ref, other_ref, near_ref):
    device, block, core = place_ref[0], place_ref[1], place_ref[2]
    planes, depth, share, half = own_ref.shape
    share //= 2
    count = near_ref.shape[0]
    per_block = LANES // share
    for ref, swapped, col in ((own_ref, 0, core), (other_ref, 1, 1 - core)):
        cols = pl.ds(pl.multiple_of(col * half, half), half)
        for far in range(planes):
            for near in range(depth):
                for side in range(2):
                    owner = device ^ ((far * depth + near) * 2 + (side ^ swapped))
                    heads = (owner // per_block) ^ block
                    to = (heads % 2) * (count // 2) + heads // 2
                    row = pl.ds(pl.multiple_of((owner % per_block) * share, share), share)
                    near_ref[to, row, cols] = ref[far, near, side * share : (side + 1) * share, :]


def arrange(place, own, other):
    shape = (D // LANES, LANES, D)
    return pl.pallas_call(
        arrange_kernel,
        in_specs=[pl.BlockSpec(memory_space=pltpu.SMEM), whole(own.shape), whole(other.shape)],
        out_specs=whole(shape),
        out_shape=jax.ShapeDtypeStruct(shape, jnp.bfloat16),
        compiler_params=params(12),
        cost_estimate=FREE,
    )(place, own, other)


def collect_kernel(place_ref, *refs):
    parts, outs = refs[:4], refs[4:]
    total = sum(part[...].astype(jnp.float32) for part in parts)
    depth, (share, wide) = len(outs), outs[0].shape
    qkv = 3 * LANES
    tall = depth * share
    for natural in range(depth):
        part = total[natural * share : (natural + 1) * share, :].astype(jnp.bfloat16)
        for far, out_ref in enumerate(outs):

            @pl.when((place_ref[0] ^ far) == natural)
            def _():
                out_ref[:, :qkv] = part[:, :qkv]
                out_ref[:, qkv + LANES :] = part[:, qkv:]

    exact = total[tall : tall + 4, :tall] + total[tall + 4 : tall + 8, :tall]
    high = exact.astype(jnp.bfloat16).astype(jnp.float32)
    parts = jnp.concatenate([high, exact - high], axis=0)
    parts = jnp.concatenate([parts[:, :LANES], parts[:, LANES:]], axis=0).astype(jnp.bfloat16)
    for out_ref in outs:
        out_ref[:16, qkv : qkv + LANES] = parts
        out_ref[16:, qkv : qkv + LANES] = jnp.zeros((share - 16, LANES), jnp.bfloat16)


def collect(place, parts, depth):
    rows, wide = parts[0].shape
    shape = ((rows - 16) // depth, wide + LANES)
    return pl.pallas_call(
        collect_kernel,
        in_specs=[pl.BlockSpec(memory_space=pltpu.SMEM)] + [whole(part.shape) for part in parts],
        out_specs=[whole(shape)] * depth,
        out_shape=[jax.ShapeDtypeStruct(shape, jnp.bfloat16)] * depth,
        compiler_params=params(8),
        cost_estimate=FREE,
    )(place, *parts)


def divide_kernel(place_ref, *refs):
    parts, (own_ref, sent_ref, own_out, sent_out) = refs[:-4], refs[-4:]
    core = place_ref[0]
    qkv = 3 * LANES
    share = own_ref.shape[1]
    depth = len(parts)
    own_rows = pl.ds(pl.multiple_of(core * share, share), share)
    other_rows = pl.ds(pl.multiple_of((1 - core) * share, share), share)
    for far, part in enumerate(parts):
        own_ref[far] = part[own_rows, : 3 * LANES]
        sent_ref[far] = part[other_rows, : 3 * LANES]
    for rows, ref in ((own_rows, own_out), (other_rows, sent_out)):
        ref[...] = sum(part[rows, qkv + LANES :].astype(jnp.float32) for part in parts)
    vectors = sum(part[0:16, qkv : qkv + LANES].astype(jnp.float32) for part in parts)
    high = vectors.astype(jnp.bfloat16).astype(jnp.float32)
    zero = jnp.zeros((16, LANES), jnp.float32)
    both = jnp.concatenate([high, vectors - high, zero], axis=1).astype(jnp.bfloat16)
    for ref in (own_ref, sent_ref):
        ref[depth, :16, :] = both
        ref[depth, 16:, :] = jnp.zeros((share - 16, 3 * LANES), jnp.bfloat16)


def divide(core, parts):
    share = parts[0].shape[0] // 2
    shapes = [jax.ShapeDtypeStruct((len(parts) + 1, share, 3 * LANES), jnp.bfloat16)] * 2
    shapes += [jax.ShapeDtypeStruct((share, parts[0].shape[1] - 4 * LANES), jnp.float32)] * 2
    return pl.pallas_call(
        divide_kernel,
        in_specs=[pl.BlockSpec(memory_space=pltpu.SMEM)] + [whole(part.shape) for part in parts],
        out_specs=[whole(shape.shape) for shape in shapes],
        out_shape=shapes,
        compiler_params=params(8),
        cost_estimate=FREE,
    )(core, *parts)


def finish_kernel(place_ref, qkv_ref, got_qkv_ref, own_out, got_out, grad_ref, vector_ref, out_ref):
    block, core = place_ref[0], place_ref[1]
    half = out_ref.shape[1] // 2
    out_ref[:, pl.ds(pl.multiple_of(core * half, half), half)] = own_out[...]
    out_ref[:, pl.ds(pl.multiple_of((1 - core) * half, half), half)] = got_out[...]
    depth = qkv_ref.shape[0] - 1
    for near, qkv in enumerate((qkv_ref, got_qkv_ref)):
        for far in range(depth):
            first = (block ^ (2 * far + near)) * LANES
            for kind in range(3):
                to = pl.ds(pl.multiple_of(kind * D + first, LANES), LANES)
                grad_ref[:, to] = qkv[far, :, kind * LANES : (kind + 1) * LANES].astype(jnp.float32)
    both = qkv_ref[depth, :16, :].astype(jnp.float32) + got_qkv_ref[depth, :16, :].astype(jnp.float32)
    exact = both[:, :LANES] + both[:, LANES : 2 * LANES]
    vector_ref[:, :LANES] = exact[0:4] + exact[4:8]
    vector_ref[:, LANES:] = exact[8:12] + exact[12:16]


def finish(place, qkv, got_qkv, own_out, got_out):
    share = qkv.shape[1]
    shapes = [(share, 3 * D), (4, 2 * LANES), (share, D)]
    arrays = (qkv, got_qkv, own_out, got_out)
    return pl.pallas_call(
        finish_kernel,
        in_specs=[pl.BlockSpec(memory_space=pltpu.SMEM)] + [whole(array.shape) for array in arrays],
        out_specs=[whole(shape) for shape in shapes],
        out_shape=[jax.ShapeDtypeStruct(shape, jnp.float32) for shape in shapes],
        compiler_params=params(8),
        cost_estimate=FREE,
    )(place, *arrays)


def finish_up_kernel(core_ref, own_ref, got_ref, up_ref):
    depth = own_ref.shape[2] // LANES
    for near, ref in enumerate((own_ref, got_ref)):
        side = core_ref[0] ^ near
        for far in range(4):
            for chip in range(depth):
                to = pl.ds(pl.multiple_of(((far * depth + chip) * 2 + side) * LANES, LANES), LANES)
                up_ref[:, to] = ref[far, :, chip * LANES : (chip + 1) * LANES].astype(jnp.float32)


def finish_up(core, own, got):
    shape = (own.shape[1], 4 * D)
    return pl.pallas_call(
        finish_up_kernel,
        in_specs=[pl.BlockSpec(memory_space=pltpu.SMEM), whole(own.shape), whole(got.shape)],
        out_specs=whole(shape),
        out_shape=jax.ShapeDtypeStruct(shape, jnp.float32),
        compiler_params=params(8),
        cost_estimate=FREE,
    )(core, own, got)


def turned(values):
    return values.astype(jnp.float32).T.astype(jnp.bfloat16)


def out_project_kernel(gains_ref, tokens_ref, near_ref, *refs):
    heads, (hidden_ref, normed_ref) = refs[:-2], refs[-2:]
    rows = tokens_ref.shape[0]
    depth = len(heads) // 2
    parts = [ref[:rows, :] if far < depth else ref[rows:, :] for far, ref in enumerate(heads)]
    hidden = tokens_ref[...].astype(jnp.float32) + jnp.dot(
        jnp.concatenate(parts, axis=1), near_ref[...].reshape(D, D), preferred_element_type=jnp.float32
    )
    normal, _ = moments(hidden)
    hidden_ref[...] = hidden
    normed_ref[...] = (normal * gains_ref[2:3, :] + gains_ref[3:4, :]).astype(jnp.bfloat16)


def out_project(gains, tokens, near_out, heads):
    arrays = (gains, tokens, near_out, *heads)
    return pl.pallas_call(
        out_project_kernel,
        in_specs=[whole(array.shape) for array in arrays],
        out_specs=[whole(tokens.shape)] * 2,
        out_shape=[
            jax.ShapeDtypeStruct(tokens.shape, jnp.float32),
            jax.ShapeDtypeStruct(tokens.shape, jnp.bfloat16),
        ],
        compiler_params=params(12),
        cost_estimate=FREE,
    )(*arrays)


def norm_two_kernel(gains_ref, hidden_ref, grad_ref, own_ref, *refs):
    sides, (delta_ref, low_ref, sums_ref) = refs[:-3], refs[-3:]
    delta = own_ref[...]
    for side in sides:
        delta += side[...].astype(jnp.float32)
    normal, scale = moments(hidden_ref[...])
    sums = jnp.concatenate(
        [jnp.sum(delta * normal, axis=0, keepdims=True), jnp.sum(delta, axis=0, keepdims=True)], axis=0
    )

    @pl.when(pl.program_id(0) == 0)
    def _():
        sums_ref[...] = sums

    @pl.when(pl.program_id(0) > 0)
    def _():
        sums_ref[...] += sums

    hidden_delta = grad_ref[...].astype(jnp.float32) + norm_back(delta, gains_ref[2:3, :], normal, scale)
    delta_ref[...] = hidden_delta
    low_ref[...] = hidden_delta.astype(jnp.bfloat16)


def by_rows(shape, steps):
    return pl.BlockSpec((shape[0] // steps, shape[1]), lambda i: (i, 0))


def norm_two(gains, hidden, out_grad, own, sides):
    arrays = (hidden, out_grad, own, *sides)
    piece = by_rows(hidden.shape, 4)
    return pl.pallas_call(
        norm_two_kernel,
        grid=(4,),
        in_specs=[whole(gains.shape)] + [piece] * len(arrays),
        out_specs=[piece, piece, whole((2, D))],
        out_shape=[
            jax.ShapeDtypeStruct(hidden.shape, jnp.float32),
            jax.ShapeDtypeStruct(hidden.shape, jnp.bfloat16),
            jax.ShapeDtypeStruct((2, D), jnp.float32),
        ],
        compiler_params=params(10),
        cost_estimate=FREE,
    )(gains, *arrays)


def norm_one_kernel(gains_ref, tokens_ref, hidden_ref, own_ref, *refs):
    sides, out_ref = refs[:-1], refs[-1]
    delta = own_ref[...]
    for side in sides:
        delta += side[...].astype(jnp.float32)
    normal, scale = moments(tokens_ref[...].astype(jnp.float32))
    out_ref[...] = hidden_ref[...] + norm_back(delta, gains_ref[0:1, :], normal, scale)


def norm_one(gains, tokens, hidden_delta, own, sides):
    arrays = (tokens, hidden_delta, own, *sides)
    piece = by_rows(tokens.shape, 4)
    return pl.pallas_call(
        norm_one_kernel,
        grid=(4,),
        in_specs=[whole(gains.shape)] + [piece] * len(arrays),
        out_specs=piece,
        out_shape=jax.ShapeDtypeStruct(tokens.shape, jnp.float32),
        compiler_params=params(10),
        cost_estimate=FREE,
    )(gains, *arrays)


def out_grads_kernel(place_ref, cols_ref, *refs):
    heads, outs, heads_t = refs[:-5], refs[-5:-1], refs[-1]
    plane, own_block = place_ref[0], place_ref[1]
    depth = len(heads) // 2
    rows = cols_ref.shape[0] // 2
    for far, ref in enumerate(heads):
        core, near = far // depth, far % depth
        row = pl.multiple_of((own_block ^ (2 * near + core)) * LANES, LANES)
        part = ref[...] if core == 0 else jnp.concatenate([ref[rows:, :], ref[:rows, :]])
        heads_t[pl.ds(row, LANES), :] = turned(part)
    tall = D // 4
    for far, out in enumerate(outs):
        row = pl.multiple_of((plane ^ far) * tall, tall)
        left = heads_t[pl.ds(row, tall), :]
        out[:tall, :] = jnp.dot(left, cols_ref[...], preferred_element_type=jnp.float32).astype(jnp.bfloat16)
        out[tall:, :] = jnp.zeros((out.shape[0] - tall, out.shape[1]), jnp.bfloat16)


def out_grads(place, heads, hidden_both):
    rows = hidden_both.shape[0]
    low = jnp.bfloat16

    def full(shape):
        return pl.BlockSpec(shape, lambda i, place: (0,) * len(shape))

    shape = (D // 4 + 16, D // 2)
    grid_spec = pltpu.PrefetchScalarGridSpec(
        num_scalar_prefetch=1,
        grid=(1,),
        in_specs=[pl.BlockSpec((rows, D // 2), lambda i, place: (0, place[2]))]
        + [full(part.shape) for part in heads],
        out_specs=[full(shape)] * 4,
        scratch_shapes=[pltpu.VMEM((D, rows), low)],
    )
    return pl.pallas_call(
        out_grads_kernel,
        grid_spec=grid_spec,
        out_shape=[jax.ShapeDtypeStruct(shape, low)] * 4,
        compiler_params=params(12),
        cost_estimate=FREE,
    )(place, hidden_both, *heads)


def back_project_kernel(own_ref, other_ref, own_weights, other_weights, keep_ref, *outs):
    for far in range(own_ref.shape[0]):
        total = jnp.dot(own_ref[far], own_weights[...], preferred_element_type=jnp.float32)
        total += jnp.dot(other_ref[far], other_weights[...], preferred_element_type=jnp.float32)
        if far == 0:
            keep_ref[...] = total
        else:
            outs[far - 1][...] = total.astype(jnp.bfloat16)


def back_project(own, other, own_weights, other_weights):
    count, rows, _ = own.shape
    arrays = (own, other, own_weights, other_weights)
    return pl.pallas_call(
        back_project_kernel,
        in_specs=[whole(array.shape) for array in arrays],
        out_specs=[whole((rows, D))] * count,
        out_shape=[jax.ShapeDtypeStruct((rows, D), jnp.float32)]
        + [jax.ShapeDtypeStruct((rows, D), jnp.bfloat16)] * (count - 1),
        compiler_params=params(24),
        cost_estimate=FREE,
    )(*arrays)


def qkv_grad_kernel(place_ref, nm_ref, turned_ref, gains_ref, two_ref, *refs):
    deltas, terms, outs, (total, sums) = refs[:-10], refs[-10:-6], refs[-6:-2], refs[-2:]
    count, rows, _ = deltas[0].shape
    ones = jnp.ones((rows, LANES), jnp.bfloat16)
    for index in range(2 * count):
        delta = deltas[index % 2][index // 2]
        part = outer(delta, nm_ref[index * rows : (index + 1) * rows, :])
        column = outer(delta, ones)
        if index == 0:
            total[...] = part
            sums[...] = column
        else:
            total[...] += part
            sums[...] += column
    gain, bias = gains_ref[0:1, :], gains_ref[1:2, :]
    weights = turned_ref[...].astype(jnp.float32)
    column = sums[:, 0:1]
    bias_part = jnp.sum(weights * column, axis=0, keepdims=True)
    gain_part = (jnp.sum(weights * total[...], axis=0, keepdims=True) - bias * bias_part) / gain
    exact = jnp.concatenate([gain_part, bias_part, two_ref[0:2, :]], axis=0)
    high = exact.astype(jnp.bfloat16).astype(jnp.float32)
    parts = jnp.concatenate([high, exact - high, jnp.zeros((8, D), jnp.float32)], axis=0)
    total_parts = parts.astype(jnp.bfloat16)
    tall = D // 4
    for natural in range(4):
        for far in range(4):

            @pl.when((place_ref[0] ^ far) == natural)
            def _():
                cols = slice(natural * tall, (natural + 1) * tall)
                outs[far][:tall, : 3 * LANES] = total[:, cols].T.astype(jnp.bfloat16)
                outs[far][tall:, :tall] = total_parts[:, cols]
    for term, out in zip(terms, outs):
        wide = out.shape[1] - term.shape[1]
        out[:, wide:] = term[...]
        out[D // 4 :, D // 4 : wide] = jnp.zeros((16, wide - D // 4), jnp.bfloat16)


def qkv_gradient(place, deltas, normed, turned_weights, gains, two, terms):
    shape = (D // 4 + 16, 3 * LANES + terms[0].shape[1])
    arrays = (normed, turned_weights, gains, two, *deltas, *terms)
    return pl.pallas_call(
        qkv_grad_kernel,
        in_specs=[pl.BlockSpec(memory_space=pltpu.SMEM)] + [whole(array.shape) for array in arrays],
        out_specs=[whole(shape)] * 4,
        out_shape=[jax.ShapeDtypeStruct(shape, jnp.bfloat16)] * 4,
        scratch_shapes=[pltpu.VMEM((3 * LANES, D), jnp.float32), pltpu.VMEM((3 * LANES, LANES), jnp.float32)],
        compiler_params=params(28),
        cost_estimate=FREE,
    )(place, *arrays)


def moments(values):
    centred = values - jnp.mean(values, axis=1, keepdims=True)
    scale = lax.rsqrt(jnp.mean(centred * centred, axis=1, keepdims=True) + EPSILON)
    return centred * scale, scale


def norm_back(delta, gain, normal, scale):
    e = delta * gain
    return scale * (
        e - jnp.mean(e, axis=1, keepdims=True) - normal * jnp.mean(e * normal, axis=1, keepdims=True)
    )


def added(keep, got):
    return (keep.astype(jnp.float32) + got.astype(jnp.float32)).astype(jnp.bfloat16)


def on_planes(
    tokens_in,
    out_grad,
    w_qkv,
    w_out,
    w_up,
    w_down,
    norm1_gain,
    norm1_bias,
    norm2_gain,
    norm2_bias,
):
    depth = lax.axis_size("z")
    rows = tokens_in.shape[0]
    share = w_qkv.shape[0]
    low = jnp.bfloat16
    places = {axis: lax.axis_index(axis) for axis in ALL}
    core = places["c"]
    block = 2 * places["z"] + core
    device = ((2 * places["y"] + places["x"]) * depth + places["z"]) * 2 + core

    hold = lax.optimization_barrier
    plane = 2 * places["y"] + places["x"]

    def index_of(*values):
        return jnp.stack(values).astype(jnp.int32)

    def along_z(part, far):
        return swap(part, "z", depth, far)

    def middle_z(part):
        return lax.ppermute(part, "z", [(1, 2), (2, 1)])

    def over_plane(part, far):
        return swap(part, ("y", "x"), 4, far)

    waiting, have = {}, {}

    def stage(name, *main):
        extra = {}
        for item in list(waiting):
            if BESIDE[item] == name:
                operand, function = waiting.pop(item)
                extra[item] = function(operand)
        main, extra, left = hold((main, extra, {item: waiting[item][0] for item in waiting}))
        for item in waiting:
            waiting[item] = (left[item], waiting[item][1])
        have.update(extra)
        return main

    def on_line(far):
        return lambda part: along_z(part, far)

    def on_plane(far):
        return lambda part: over_plane(part, far)

    tokens_two = along_z(tokens_in, 2)
    gains = jnp.concatenate([norm1_gain, norm1_bias, norm2_gain, norm2_bias]).reshape(1, LANES)
    keep, send = prepare(core.reshape(1), w_qkv, w_up, w_out, gains)
    keep, sent_one, sent_grad = hold((keep, tokens_in, out_grad))
    got = pair(send)
    tokens_one = along_z(sent_one, 1)
    grads = [out_grad] + [over_plane(sent_grad, far) for far in (1, 2)]
    ups, parts = compose(index_of(places["z"]), keep, got, depth)
    ups = lax.all_to_all(ups, ("y", "x"), 0, 0, tiled=True)
    tokens_two, tokens_one, grads, parts, ups, sent_tokens, sent_grad = hold(
        (tokens_two, tokens_one, grads, parts, ups, tokens_in, out_grad)
    )

    along = [parts[0]] + [along_z(parts[far], far) for far in range(1, depth)]
    waiting["up1"] = (ups, on_line(1))
    waiting["ogd"] = (sent_grad, on_plane(3))
    along, tokens_one, tokens_two, sent_tokens, ups = stage("tokens", along, tokens_one, tokens_two, sent_tokens, ups)

    middle, ends = middle_z(sent_tokens), lax.ppermute(tokens_two, "z", [(1, 0), (2, 3)])
    outs = jnp.stack([part[:, : D // 2] for part in along])
    along = jnp.stack([part[:, D // 2 :] for part in along])
    across = [along] + [over_plane(along, far) for far in range(1, 4)]
    across, middle, ends, ups, outs = stage("plane", across, middle, ends, ups, outs)
    group = [tokens_in, pair(sent_tokens), tokens_one, pair(tokens_one), tokens_two, pair(tokens_two)]
    group += [part for mine in (middle, ends) for part in (mine, pair(mine))]
    group, across, ups, outs = stage("pairs", group, across, ups, outs)

    qkv, normed, gains, turned_qkv = project(device, group, across)
    own_ups = ups
    up_two, up_three = along_z(ups, 2), along_z(ups, 3)
    outs = [outs] + [over_plane(outs, far) for far in range(1, 4)]
    attended_low, attended, recip, probs = attend(qkv)
    attended_low, up_two, up_three, outs = stage("attention", attended_low, up_two, up_three, outs)

    both = 2 * rows
    sides = [attended_low[:both]] + [
        along_z(attended_low[far * both : (far + 1) * both], far) for far in range(1, depth)
    ]
    outs = jnp.stack(outs)
    near_out = arrange(index_of(device, block, core), outs, pair(outs))
    own_out = near_out[:depth].reshape(depth * LANES, D)
    waiting["turned"] = (turned_qkv, pair)
    sides, near_out = stage("heads", sides, near_out)
    heads = [*sides, *(pair(part) for part in sides)]
    hidden, normed_two = out_project(gains, tokens_in, near_out, heads)
    normed_two, heads, sent_down = stage("hidden", normed_two, heads, w_down)

    plane_normed = [normed_two] + [over_plane(normed_two, far) for far in range(1, 4)]
    downs = [w_down] + [along_z(sent_down, far) for far in range(1, depth)]
    other_downs = [pair(part) for part in downs]
    waiting["oups0"], waiting["oups2"], waiting["oups3"] = (own_ups, pair), (up_two, pair), (up_three, pair)
    plane_normed, downs, other_downs = stage("units", plane_normed, downs, other_downs)
    ups = [own_ups, have["up1"], up_two, up_three]
    other_ups = [have["oups0"], pair(have["up1"]), have["oups2"], have["oups3"]]
    grads = [*grads, have["ogd"]]
    active, up_delta, two_delta, *part, own_down, down_keep, down_send = mlp(
        index_of(device, places["z"]), plane_normed, grads, ups, other_ups, downs, other_downs
    )

    two_sides = [over_plane(part[far - 1], far) for far in range(1, 4)]
    down_got = pair(down_send)
    down_term = [added(down_keep[far], down_got[far]) for far in range(depth)]
    waiting["dz2"], waiting["dz3"], waiting["dz1"] = ((down_term[far], on_line(far)) for far in (2, 3, 1))
    out_own, *out_parts, up_term, up_send = mlp_grads(
        index_of(places["z"]), plane_normed, active, up_delta, own_down, depth
    )
    waiting["lo1"], waiting["lo2"], waiting["lo3"] = ((out_parts[far - 1], on_plane(far)) for far in (1, 2, 3))
    two_sides, up_term, up_send = stage("sums", two_sides, up_term, up_send)
    hidden_delta, hidden_low, two_sums = norm_two(gains, hidden, out_grad, two_delta, two_sides)
    hidden_both = jnp.concatenate([hidden_low, pair(hidden_low)])
    att_delta = against(hidden_both, own_out).astype(low)
    att_delta, up_send, heads, up_term = stage("norm", att_delta, up_send, heads, up_term)

    far_delta = [att_delta[:, :LANES]] + [
        along_z(att_delta[:, far * LANES : (far + 1) * LANES], far) for far in range(1, depth)
    ]
    up_got = pair(up_send)
    out_terms = out_grads(index_of(plane, block, core), heads, hidden_both)
    up_term = [added(up_term[far], up_got[far]) for far in range(depth)]
    far_delta, out_terms, up_term = stage("delta", far_delta, out_terms, up_term)

    deltas = attend_back(qkv, probs, far_delta, attended, recip)
    up_sides = [up_term[0]] + [along_z(up_term[far], far) for far in range(1, depth)]
    deltas, up_sides = stage("back", deltas, up_sides)

    got = pair(deltas[1])
    one_delta, *part = back_project(deltas[0], got, turned_qkv, have["turned"])
    part, deltas, out_terms, up_sides = stage("project", part, deltas, out_terms, up_sides)

    waiting["upa"] = (
        up_sides,
        lambda parts: lax.all_to_all(
            sum(side.astype(jnp.float32) for side in parts).astype(low), ("y", "x"), 0, 0, tiled=True
        ),
    )
    ends, middle = lax.ppermute(part[2], "z", [(0, 1), (3, 2)]), middle_z(part[2])
    qkv_terms = qkv_gradient(index_of(plane), deltas, normed, turned_qkv, gains, two_sums, out_terms)
    ends, middle, qkv_terms = stage("middle", ends, middle, qkv_terms)

    one_sides = [along_z(added(part[1], ends), 2), along_z(part[0], 1), middle]
    terms = [qkv_terms[0]] + [over_plane(qkv_terms[far], far) for far in range(1, 4)]
    qkv_part = collect(index_of(places["z"]), terms, depth)
    out_sum = hidden + out_own
    for item in ("lo1", "lo2", "lo3"):
        out_sum = out_sum + have[item].astype(jnp.float32)
    one_sides, qkv_part, out_sum = stage("rest", one_sides, qkv_part, out_sum)

    qkv_sides = [qkv_part[0]] + [along_z(qkv_part[far], far) for far in range(1, depth)]
    input_grad = norm_one(gains, tokens_in, hidden_delta, one_delta, one_sides)
    qkv_sides, input_grad, out_sum = stage("last", qkv_sides, input_grad, out_sum)
    up_sum = have["upa"]
    own_part = lax.dynamic_slice_in_dim(up_sum, core * share, share, 1)
    other_part = lax.dynamic_slice_in_dim(up_sum, (1 - core) * share, share, 1)
    up_grad = finish_up(index_of(core), own_part, pair(other_part))
    result = out_sum.astype(low)
    down_sum = down_term[0].astype(jnp.float32)
    for item in ("dz1", "dz2", "dz3"):
        down_sum = down_sum + have[item].astype(jnp.float32)
    own_qkv, sent_qkv, own_out, sent_out = divide(index_of(core), qkv_sides)
    qkv_grad, vectors, out_weight_grad = finish(
        index_of(block, core), own_qkv, pair(sent_qkv), own_out, pair(sent_out)
    )
    vectors = lax.dynamic_slice_in_dim(vectors, (places["z"] * 2 + core) * share, share, 1)
    return (
        result,
        input_grad,
        qkv_grad,
        out_weight_grad,
        up_grad,
        down_sum,
        vectors[0],
        vectors[1],
        vectors[2],
        vectors[3],
    )


def solution(mesh):
    scenes, blocks = mesh.devices.shape

    def place(axes):
        matrix = P(axes, None)
        views = P(axes[: len(axes) // 2] if len(axes) > 2 else axes[0], None)
        vector = P(axes)
        ins = (matrix, views, views, views, matrix, matrix, matrix, matrix, matrix) + (vector,) * 4
        return ins, (matrix,) * 6 + (vector,) * 4

    def run(*arrays):
        one_scene = arrays[1].shape[1] == 4
        if scenes == 4 and blocks == 8 and one_scene and arrays[0].shape[0] == 8192:
            fine = Mesh(mesh.devices.reshape(2, 2, blocks // 2, 2), ALL)
            ins, outs = place(ALL)
            step = lambda tokens, heights, widths, labels, *rest: on_planes(tokens, *rest)
            return jax.shard_map(step, mesh=fine, in_specs=ins, out_specs=outs, check_vma=False)(*arrays)
        ins, outs = place(("scene", "blk"))
        return jax.shard_map(on_any_slice, mesh=mesh, in_specs=ins, out_specs=outs, check_vma=False)(*arrays)

    return run
```
